128 devices in a mesh: rep: 4 (over z), tile: 32 (over y, x, core).
Axes of the slice: x: 4, y: 4, z: 4, core: 2. Of those that a mesh axis runs over, the one named last changes fastest.
Arguments:
- features: bfloat16 [512, 32, 32, 256], P(('rep', 'tile')), may hold values from -6 to 6
- cotangent: bfloat16 [512, 32, 2048], P(('rep', 'tile')), may hold values from -0.29882812 to 0.29882812
- neighbors: int32 [512, 8], P(('rep', 'tile')), may hold values from -1 to 3, as said below
- live_count: int32 [128], P(('rep', 'tile')), may hold values from 1 to 4, as said below
- kernel_mid: bfloat16 [3, 3, 256, 128], replicated, may hold values from -0.125 to 0.125
- bias_mid: float32 [128], replicated, may hold values from -0.5 to 0.5
- kernel_top: bfloat16 [3, 3, 128, 64], replicated, may hold values from -0.1875 to 0.1875
- bias_top: float32 [64], replicated, may hold values from -0.5 to 0.5
Outputs:
- backend_out: bfloat16 [512, 32, 2048], P(('rep', 'tile'))
- gradient_mid: float32 [3, 3, 256, 128], replicated
- gradbias_mid: float32 [128], replicated
- gradient_top: float32 [3, 3, 128, 64], replicated
- gradbias_top: float32 [64], replicated
The draws below stay inside these ranges and needn't reach their ends.
Inputs may be any that keep to these rules, and one draw needn't show every extreme that they name: Slots 0 to live_count - 1 of a column hold populated tiles; some column holds 4 in every draw. `neighbors`: entry k names a live slot of the column offset by that direction's dc within the same scene, whose tile sits at the adjacent scene position; -1 where no populated tile is there, for every direction of an empty slot, and past either end of a scene's 32 columns. Two live slots of one column never sit at the same position.
All inputs are finite; a program needn't handle non-finite values.
Results may differ from the reference program's by a relative error of at most 0.009.
Values may be sent and summed in bfloat16 or wider, within the bound.
A program may use at most 128 MiB of HBM per device.

```python
import jax
import jax.numpy as jnp
from jax import lax

CIN = 256
CMID = 128
COUT = 64
TILE = 32
SLOTS = 4
SCENE_COLS = 32
COLUMNS = 128
TILES = 512
N_TILE = 32


DIRECTIONS = ((-1, -1), (-1, 0), (-1, 1), (0, -1), (0, 1), (1, -1), (1, 0), (1, 1))


def scene_layout(key):
    key_count, key_force, key_start, key_turn, key_flip = jax.random.split(key, 5)
    counts = jax.random.randint(key_count, (COLUMNS,), 1, 3)
    forced = jax.random.randint(key_force, (), 0, COLUMNS)
    column_ids = jnp.arange(COLUMNS, dtype=jnp.int32)
    counts = jnp.where(column_ids == forced, SLOTS, counts).astype(jnp.int32)
    starts = jax.random.randint(key_start, (COLUMNS,), 0, 3 + SLOTS - counts)
    turns = jax.random.randint(key_turn, (COLUMNS,), 0, SLOTS) % counts
    flips = jax.random.randint(key_flip, (COLUMNS,), 0, 2)
    slot_ids = jnp.arange(SLOTS, dtype=jnp.int32)[None, :]
    offsets = (slot_ids + turns[:, None]) % counts[:, None]
    offsets = jnp.where(flips[:, None] == 1, counts[:, None] - 1 - offsets, offsets)
    rows = jnp.where(slot_ids < counts[:, None], starts[:, None] + offsets, -1)
    position = column_ids % SCENE_COLS
    found_all = []
    for step_row, step_col in DIRECTIONS:
        others = jnp.roll(rows, -step_col, axis=0)
        inside = (position + step_col >= 0) & (position + step_col < SCENE_COLS)
        wanted = rows + step_row
        match = (others[:, None, :] == wanted[:, :, None]) & (others[:, None, :] >= 0)
        match = match & (rows[:, :, None] >= 0) & inside[:, None, None]
        found = jnp.max(match.astype(jnp.int32) * (slot_ids[:, None, :] + 1), axis=2) - 1
        found_all.append(found)
    links = jnp.stack(found_all, axis=2).reshape(COLUMNS * SLOTS, 8).astype(jnp.int32)
    return (counts, links)


def draw_live_count(key, part):
    counts, links = scene_layout(key)
    return counts


def draw_neighbors(key, part):
    counts, links = scene_layout(key)
    return links


def steps_of(stream_key, extent, cuts, low, largest):
    level = 1.0
    for axis_at, shards_of in cuts:
        draws = jax.random.uniform(jax.random.fold_in(jax.random.fold_in(stream_key, 6), axis_at), (shards_of,), jnp.float32, low / len(cuts), largest / len(cuts))
        level = level * jnp.repeat(jnp.exp(draws), extent[axis_at] // shards_of).reshape((-1,) + (1,) * (len(extent) - 1 - axis_at))
    return level


def bell_draw(key, dims, scale, limit, shards=(), kind=jnp.bfloat16):
    result = scale * jax.random.normal(key, dims, jnp.float32)
    if shards:
        result = result * steps_of(key, dims, shards, -0.22, 0.18)
    return jnp.clip(result, -limit, limit).astype(kind)


def setup_inputs(seed: int = 0) -> dict:
    splits = jax.random.split(jax.random.key(seed), 9)
    return {
        "features": bell_draw(splits[0], (TILES, TILE, TILE, CIN), 1.0, 6.0, ((0, 128),)),
        "cotangent": bell_draw(splits[1], (TILES, TILE, TILE * COUT), 0.05, 0.29882812, ((0, 128),)),
        "neighbors": draw_neighbors(jax.random.fold_in(splits[8], 71), 0),
        "live_count": draw_live_count(jax.random.fold_in(splits[8], 71), 0),
        "kernel_mid": bell_draw(splits[4], (3, 3, CIN, CMID), (9 * CIN) ** -0.5, 0.125),
        "bias_mid": jnp.clip(jax.random.uniform(splits[5], (CMID,), jnp.float32, -0.5, 0.5), -0.5, 0.5),
        "kernel_top": bell_draw(splits[6], (3, 3, CMID, COUT), (9 * CMID) ** -0.5, 0.1875),
        "bias_top": jnp.clip(jax.random.uniform(splits[7], (COUT,), jnp.float32, -0.5, 0.5), -0.5, 0.5),
    }


def select_slots(indices, source):
    slot_count = source.shape[0]
    onehot = indices[:, None] == jnp.arange(slot_count, dtype=jnp.int32)[None, :]
    onehot = onehot.reshape(onehot.shape + (1,) * (source.ndim - 1))
    picked = jnp.where(onehot, source[None], jnp.zeros((), source.dtype))
    return jnp.sum(picked, axis=1).astype(source.dtype)


def assemble(values, links, from_left, from_right):
    tile_side = values.shape[1]
    north_band = select_slots(links[:, 1], values[:, tile_side - 2:])
    south_band = select_slots(links[:, 6], values[:, :2])
    west_side = select_slots(links[:, 3], from_left)
    east_side = select_slots(links[:, 4], from_right)
    corner_nw = select_slots(links[:, 0], from_left[:, tile_side - 2:])
    corner_ne = select_slots(links[:, 2], from_right[:, tile_side - 2:])
    corner_sw = select_slots(links[:, 5], from_left[:, :2])
    corner_se = select_slots(links[:, 7], from_right[:, :2])
    upper_band = jnp.concatenate([corner_nw, north_band, corner_ne], axis=2)
    middle = jnp.concatenate([west_side, values, east_side], axis=2)
    lower_band = jnp.concatenate([corner_sw, south_band, corner_se], axis=2)
    return jnp.concatenate([upper_band, middle, lower_band], axis=1)


def dilated_conv(padded, kernel):
    slot_count, tile_side = padded.shape[0], padded.shape[1] - 4
    channels = padded.shape[3]
    accumulated = jnp.zeros((slot_count * tile_side * tile_side, kernel.shape[3]), jnp.float32)
    for row_tap in range(3):
        for col_tap in range(3):
            window = padded[:, 2 * row_tap:2 * row_tap + tile_side, 2 * col_tap:2 * col_tap + tile_side, :]
            accumulated = accumulated + jnp.dot(window.reshape(-1, channels), kernel[row_tap, col_tap], preferred_element_type=jnp.float32)
    return accumulated.reshape(slot_count, tile_side, tile_side, kernel.shape[3])


def kernel_gradient(padded, upstream):
    tile_side = padded.shape[1] - 4
    channels = padded.shape[3]
    out_chans = upstream.shape[3]
    flat_up = upstream.reshape(-1, out_chans)
    tap_grads = []
    for row_tap in range(3):
        for col_tap in range(3):
            window = padded[:, 2 * row_tap:2 * row_tap + tile_side, 2 * col_tap:2 * col_tap + tile_side, :]
            tap_grads.append(lax.dot_general(window.reshape(-1, channels), flat_up, (((0,), (0,)), ((), ())), preferred_element_type=jnp.float32))
    return jnp.stack(tap_grads).reshape(3, 3, channels, out_chans)


def flipped(kernel):
    return jnp.transpose(kernel[::-1, ::-1], (0, 1, 3, 2))


def silu_slope(pre):
    sigma = jax.nn.sigmoid(pre)
    return sigma * (1.0 + pre * (1.0 - sigma))


def edge_strips(values, keep_left, keep_right):
    right_edges = values[:, :, :, -2:]
    left_edges = values[:, :, :, :2]
    blank = jnp.zeros_like(right_edges[:1])
    zero_value = jnp.zeros((), values.dtype)
    from_left = jnp.where(keep_left[:, None, None, None, None], jnp.concatenate([blank, right_edges[:-1]], axis=0), zero_value)
    from_right = jnp.where(keep_right[:, None, None, None, None], jnp.concatenate([left_edges[1:], blank], axis=0), zero_value)
    return from_left, from_right


def reference(features, cotangent, neighbors, live_count, kernel_mid, bias_mid, kernel_top, bias_top):
    columns = features.reshape(COLUMNS, SLOTS, TILE, TILE, CIN)
    links = neighbors.reshape(COLUMNS, SLOTS, 8)
    live_slots = jnp.arange(SLOTS, dtype=jnp.int32)[None, :] < live_count[:, None]
    position = jnp.arange(COLUMNS, dtype=jnp.int32) % N_TILE
    keep_left = position != 0
    keep_right = position != N_TILE - 1

    feat_left, feat_right = edge_strips(columns, keep_left, keep_right)

    def layer_mid(packed):
        values, link_rows, left_in, right_in, alive = packed
        padded = assemble(values, link_rows, left_in, right_in)
        pre = dilated_conv(padded, kernel_mid) + bias_mid
        activ = jnp.where(alive[:, None, None, None], jax.nn.silu(pre), 0.0).astype(jnp.bfloat16)
        slope = jnp.where(alive[:, None, None, None], silu_slope(pre), 0.0)
        return activ, slope

    hidden, slope_mid = lax.map(layer_mid, (columns, links, feat_left, feat_right, live_slots))
    hid_left, hid_right = edge_strips(hidden, keep_left, keep_right)

    def layer_top(packed):
        values, link_rows, left_in, right_in, alive, cot = packed
        padded = assemble(values, link_rows, left_in, right_in)
        pre = dilated_conv(padded, kernel_top) + bias_top
        activ = jnp.where(alive[:, None, None, None], jax.nn.silu(pre), 0.0).astype(jnp.bfloat16)
        ups = jnp.where(alive[:, None, None, None], cot.astype(jnp.float32) * silu_slope(pre), 0.0).astype(jnp.bfloat16)
        return activ, ups

    output, upstream = lax.map(layer_top, (hidden, links, hid_left, hid_right, live_slots, cotangent.reshape(COLUMNS, SLOTS, TILE, TILE, COUT)))
    up_left, up_right = edge_strips(upstream, keep_left, keep_right)
    kernel_back = flipped(kernel_top)

    def backward(carry, packed):
        values, hid, slope, ups, link_rows, fl, fr, hl, hr, ul, ur = packed
        input_pad = assemble(values, link_rows, fl, fr)
        hidden_pad = assemble(hid, link_rows, hl, hr)
        upstream_pad = assemble(ups, link_rows, ul, ur)
        back_hidden = dilated_conv(upstream_pad, kernel_back)
        hidden_slope = (back_hidden * slope).astype(jnp.bfloat16)
        grad_mid, bias_mid_sum, grad_top, bias_top_sum = carry
        grad_mid = grad_mid + kernel_gradient(input_pad, hidden_slope)
        bias_mid_sum = bias_mid_sum + jnp.sum(hidden_slope.astype(jnp.float32), axis=(0, 1, 2))
        grad_top = grad_top + kernel_gradient(hidden_pad, ups)
        bias_top_sum = bias_top_sum + jnp.sum(ups.astype(jnp.float32), axis=(0, 1, 2))
        return (grad_mid, bias_mid_sum, grad_top, bias_top_sum), None

    start = (jnp.zeros((3, 3, CIN, CMID), jnp.float32), jnp.zeros((CMID,), jnp.float32),
             jnp.zeros((3, 3, CMID, COUT), jnp.float32), jnp.zeros((COUT,), jnp.float32))
    sums, _ = lax.scan(backward, start, (columns, hidden, slope_mid, upstream, links, feat_left, feat_right, hid_left, hid_right, up_left, up_right))
    gradient_mid, gradbias_mid, gradient_top, gradbias_top = sums
    return output.reshape(TILES, TILE, TILE * COUT), gradient_mid, gradbias_mid, gradient_top, gradbias_top
```

```python
import functools

import jax
import jax.numpy as jnp
from jax import lax
from jax.experimental import pallas as pl
from jax.experimental.pallas import tpu as pltpu
from jax.sharding import PartitionSpec as P

F32 = jnp.float32
BF16 = jnp.bfloat16
MESH = pl.DeviceIdType.MESH

SLOTS = 4
SIDE = 32
CELLS = SIDE * SIDE
PADDED = CELLS + 128
WIDE = 40
FULL = 48


def sigmoid(v):
    return 0.5 * jnp.tanh(0.5 * v) + 0.5


def low_lanes(shape):
    return lax.broadcasted_iota(jnp.int32, shape, len(shape) - 1) < 64


def present(index):
    return jnp.where(index >= 0, 1.0, 0.0).astype(F32)


def fill_bands(padded, nbr):
    for t in range(SLOTS):
        north, south = nbr[t, 1], nbr[t, 6]
        band = padded[jnp.maximum(north, 0), CELLS : CELLS + 64, :].astype(F32)
        padded[t, 0:64, :] = (band * present(north)).astype(BF16)
        band = padded[jnp.maximum(south, 0), 64:128, :].astype(F32)
        padded[t, CELLS + 64 : PADDED, :] = (band * present(south)).astype(BF16)


def strip_block(received, index, col, lanes):
    return received[jnp.maximum(index, 0) * 2 + col, :, lanes].astype(F32) * present(index)


def margin_strips(received, nbr, corner_up, side, corner_down, work, shifted, channels):
    for lane_tile in range(channels // 128):
        lanes = slice(lane_tile * 128, lane_tile * 128 + 128)
        for t in range(SLOTS):
            for col in range(2):
                base = (t * 2 + col) * FULL
                up = strip_block(received, nbr[t, corner_up], col, lanes)
                mid = strip_block(received, nbr[t, side], col, lanes)
                down = strip_block(received, nbr[t, corner_down], col, lanes)
                work[base : base + 8, :] = up[24:32]
                work[base + 8 : base + 40, :] = mid
                work[base + 40 : base + 48, :] = down[0:8]
        for block in range(SLOTS * 2):
            for a in range(3):
                rows = work[block * FULL + 6 + 2 * a : block * FULL + 38 + 2 * a, :]
                at = a * channels + lane_tile * 128
                shifted[block * 32 : block * 32 + 32, at : at + 128] = rows.astype(BF16)


def kernel(
    feat, cot, nbr, live, kmid, bmid, ktop, btop,
    out, grad,
    fp, hp, wmid, wtop, wback, y0, y1, y2, ya, yb, work, sa_w, sa_e, sh_w, sh_e, su_w, su_e,
    strip_a, strip_b, fsend, frecv, hsend, hrecv, usend, urecv,
    slope, cots, outs, uf, uplo, uphi, uu, ucol_w, ucol_e, scol_w, scol_e, sf, ss,
    acc_mid, acc_top, cotv,
    local_sem, send_sem, recv_sem,
):
    n = lax.axis_size("tile")
    me = lax.axis_index("tile")
    right, left = lax.rem(me + 1, n), lax.rem(me + n - 1, n)

    loads = []
    for t in range(SLOTS):
        loads.append(pltpu.make_async_copy(
            feat.at[t], fp.at[t, pl.ds(64, CELLS)], local_sem.at[t]))
    for a in range(3):
        for b in range(3):
            loads.append(pltpu.make_async_copy(
                kmid.at[a, b],
                wmid.at[pl.ds(a * 256, 256), pl.ds(b * 128, 128)],
                local_sem.at[4 + a * 3 + b]))
    loads.append(pltpu.make_async_copy(cot, cotv, local_sem.at[13]))
    for copy in loads:
        copy.start()

    barrier = pltpu.get_barrier_semaphore()
    for neighbour in (left, right):
        pl.semaphore_signal(barrier, inc=1, device_id={"tile": neighbour}, device_id_type=MESH)

    zero8 = jnp.zeros((8, 128), F32)

    def clear(r, _):
        base = pl.multiple_of(r * FULL, 8)
        uf[pl.ds(base, 8), :] = zero8
        uf[pl.ds(base + 40, 8), :] = zero8
        sf[pl.ds(base, 8), :] = zero8
        sf[pl.ds(base + 40, 8), :] = zero8
        return 0

    lax.fori_loop(0, SLOTS * SIDE, clear, 0)

    for a in range(3):
        k0, k1, k2 = (ktop[a, b] for b in range(3))
        wtop[a * 128 : a * 128 + 128, 0:128] = jnp.concatenate([k0, k2], axis=1)
        wtop[a * 128 : a * 128 + 128, 128:256] = jnp.concatenate([k1, k1], axis=1)
    zero_kernel = jnp.zeros((128, 64), F32)
    for b in range(3):
        first = jnp.concatenate([ktop[2, 2 - b], ktop[1, 2 - b]], axis=1).astype(F32)
        last = jnp.concatenate([ktop[0, 2 - b].astype(F32), zero_kernel], axis=1)
        wback[0:128, b * 128 : b * 128 + 128] = first.T.astype(BF16)
        wback[128:256, b * 128 : b * 128 + 128] = last.T.astype(BF16)

    for copy in loads[:SLOTS]:
        copy.wait()

    for side, (cells, picks) in enumerate(((0, (0, 1)), (16, (6, 7)))):
        def gather(r, _):
            t, i = r // SIDE, r % SIDE
            rows = fp[t, pl.ds(pl.multiple_of(64 + i * SIDE + cells, 16), 16), :].astype(F32)
            rows = rows[0:8] if cells == 0 else rows[8:16]
            at = pl.multiple_of(r * 8, 8)
            strip_a[pl.ds(at, 8), :] = rows[:, 0:128]
            strip_b[pl.ds(at, 8), :] = rows[:, 128:256]
            return 0

        lax.fori_loop(0, SLOTS * SIDE, gather, 0, unroll=4)
        for t in range(SLOTS):
            for col, pick in enumerate(picks):
                at = pl.ds(t * 256 + pick, 32, stride=8)
                fsend[side, t * 2 + col, :, 0:128] = strip_a[at, :].astype(BF16)
                fsend[side, t * 2 + col, :, 128:256] = strip_b[at, :].astype(BF16)

    pl.semaphore_wait(barrier, 2)

    def exchange(send, recv, at):
        copies = []
        for side, target in ((0, left), (1, right)):
            copies.append(pltpu.make_async_remote_copy(
                src_ref=send.at[side], dst_ref=recv.at[1 - side],
                send_sem=send_sem.at[at + side], recv_sem=recv_sem.at[at + 1 - side],
                device_id={"tile": target}, device_id_type=MESH))
        for copy in copies:
            copy.start()
        return copies

    feature_copies = exchange(fsend, frecv, 0)

    fill_bands(fp, nbr)
    for copy in loads[SLOTS:]:
        copy.wait()

    def conv_mid(t, _):
        lhs = jnp.concatenate([fp[t, 64 * a : 64 * a + CELLS, :] for a in range(3)], axis=1)
        y = jnp.dot(lhs, wmid[...], preferred_element_type=F32)
        for i in range(SIDE):
            r = t * SIDE + i
            rows = slice(i * SIDE, i * SIDE + SIDE)
            y0[pl.ds(pl.multiple_of(r * WIDE + 8, 8), SIDE), :] = y[rows, 0:128]
            y1[pl.ds(pl.multiple_of(r * SIDE, 8), SIDE), :] = y[rows, 128:256]
            y2[pl.ds(pl.multiple_of(r * WIDE, 8), SIDE), :] = y[rows, 256:384]
        return 0

    lax.fori_loop(0, SLOTS, conv_mid, 0)

    low = low_lanes((SIDE, 128))
    for t in range(SLOTS):
        for pair in range(SIDE // 2):
            x = cotv[t, :, pair * 128 : pair * 128 + 128].astype(F32)
            turned = pltpu.roll(x, 64, 1)
            cots[pl.ds(t * CELLS + 2 * pair, SIDE, stride=SIDE), :] = jnp.where(low, x, turned)
            cots[pl.ds(t * CELLS + 2 * pair + 1, SIDE, stride=SIDE), :] = jnp.where(low, turned, x)

    for copy in feature_copies:
        copy.wait()
    margin_strips(frecv.at[0], nbr, 0, 3, 5, work, sa_w, 256)
    margin_strips(frecv.at[1], nbr, 2, 4, 7, work, sa_e, 256)

    def add_margins(west, east):
        for t in range(SLOTS):
            for col in range(2):
                rows = slice((t * 2 + col) * 32, (t * 2 + col) * 32 + 32)
                y0[pl.ds(t * SIDE * WIDE + 6 + col, SIDE, stride=WIDE), :] = west[rows]
                y2[pl.ds(t * SIDE * WIDE + 32 + col, SIDE, stride=WIDE), :] = east[rows]

    add_margins(
        jnp.dot(sa_w[...], wmid[:, 0:128], preferred_element_type=F32),
        jnp.dot(sa_e[...], wmid[:, 256:384], preferred_element_type=F32))

    alive = [jnp.where(t < live[0], 1.0, 0.0).astype(F32) for t in range(SLOTS)]
    columns = ((0, 0, 0), (0, 1, 1), (1, 0, 30), (1, 1, 31))

    def mid_at(t, cell):
        first = y0[pl.ds(t * SIDE * WIDE + 6 + cell, SIDE, stride=WIDE), :]
        second = y1[pl.ds(t * CELLS + cell, SIDE, stride=SIDE), :]
        third = y2[pl.ds(t * SIDE * WIDE + 2 + cell, SIDE, stride=WIDE), :]
        return first + second + third

    for t in range(SLOTS):
        for side, col, cell in columns:
            pre = mid_at(t, cell) + bmid[...]
            hsend[side, t * 2 + col, :, :] = (pre * sigmoid(pre) * alive[t]).astype(BF16)
    hidden_copies = exchange(hsend, hrecv, 2)

    def mid_rows(r):
        first = y0[pl.ds(r * WIDE + 6, SIDE), :]
        second = y1[pl.ds(pl.multiple_of(r * SIDE, 8), SIDE), :]
        third = y2[pl.ds(r * WIDE + 2, SIDE), :]
        return first + second + third

    def activate(r, _):
        t, i = r // SIDE, r % SIDE
        mask = jnp.where(t < live[0], 1.0, 0.0).astype(F32)
        pre = mid_rows(r) + bmid[...]
        gate = sigmoid(pre)
        hidden = pre * gate
        hp[t, pl.ds(pl.multiple_of(64 + i * SIDE, 16), SIDE), :] = (hidden * mask).astype(BF16)
        slope[pl.ds(pl.multiple_of(r * SIDE, 8), SIDE), :] = (gate + hidden * (1.0 - gate)) * mask
        return 0

    lax.fori_loop(0, SLOTS * SIDE, activate, 0, unroll=4)
    fill_bands(hp, nbr)

    def conv_top(t, _):
        lhs = jnp.concatenate([hp[t, 64 * a : 64 * a + CELLS, :] for a in range(3)], axis=1)
        y = jnp.dot(lhs, wtop[...], preferred_element_type=F32)
        for i in range(SIDE):
            r = t * SIDE + i
            rows = slice(i * SIDE, i * SIDE + SIDE)
            ya[pl.ds(pl.multiple_of(r * FULL + 8, 8), SIDE), :] = y[rows, 0:128]
            yb[pl.ds(pl.multiple_of(r * SIDE, 8), SIDE), :] = y[rows, 128:256]
        return 0

    lax.fori_loop(0, SLOTS, conv_top, 0)

    for copy in hidden_copies:
        copy.wait()
    margin_strips(hrecv.at[0], nbr, 0, 3, 5, work, sh_w, 128)
    margin_strips(hrecv.at[1], nbr, 2, 4, 7, work, sh_e, 128)
    west = jnp.dot(sh_w[...], wtop[:, 0:128], preferred_element_type=F32)
    east = jnp.dot(sh_e[...], wtop[:, 0:128], preferred_element_type=F32)
    for t in range(SLOTS):
        for col in range(2):
            rows = slice((t * 2 + col) * 32, (t * 2 + col) * 32 + 32)
            ya[pl.ds(t * SIDE * FULL + 6 + col, SIDE, stride=FULL), :] = west[rows]
            ya[pl.ds(t * SIDE * FULL + 40 + col, SIDE, stride=FULL), :] = east[rows]

    def up_of(before, after, centre, cotangent):
        pair = jnp.where(low, before, after)
        pre = pair + pltpu.roll(pair, 64, 1) + centre + btop[...]
        gate = sigmoid(pre)
        value = pre * gate
        return value, cotangent * (gate + value * (1.0 - gate))

    zero_rows = jnp.zeros((SIDE, 128), F32)
    for t in range(SLOTS):
        for side in range(2):
            ups = []
            for col in range(2):
                cell = 30 * side + col
                _, up = up_of(
                    ya[pl.ds(t * SIDE * FULL + 6 + cell, SIDE, stride=FULL), :],
                    ya[pl.ds(t * SIDE * FULL + 10 + cell, SIDE, stride=FULL), :],
                    yb[pl.ds(t * CELLS + cell, SIDE, stride=SIDE), :],
                    cots[pl.ds(t * CELLS + cell, SIDE, stride=SIDE), :])
                up = up * alive[t]
                ups.append(up)
                edge = ucol_w if side == 0 else ucol_e
                at = (t * 2 + col) * 32
                edge[at : at + 32, :] = jnp.where(low, up, zero_rows).astype(BF16)
            usend[side, t] = jnp.where(low, ups[0], ups[1]).astype(BF16)
    upstream_copies = exchange(usend, urecv, 4)

    def top_rows(r, total):
        t, i = r // SIDE, r % SIDE
        mask = jnp.where(t < live[0], 1.0, 0.0).astype(F32)
        value, up = up_of(
            ya[pl.ds(r * FULL + 6, SIDE), :],
            ya[pl.ds(r * FULL + 10, SIDE), :],
            yb[pl.ds(pl.multiple_of(r * SIDE, 8), SIDE), :],
            cots[pl.ds(pl.multiple_of(r * SIDE, 8), SIDE), :])
        outs[pl.ds(pl.multiple_of(r * SIDE, 8), SIDE), :] = value * mask
        up = (up * mask).astype(BF16).astype(F32)
        uf[pl.ds(pl.multiple_of(r * FULL + 8, 8), SIDE), :] = up
        at = pl.ds(pl.multiple_of(64 + i * SIDE, 16), SIDE)
        uplo[t, at, :] = jnp.where(low, up, zero_rows).astype(BF16)
        uphi[t, at, :] = jnp.where(low, zero_rows, up).astype(BF16)
        return total + jnp.sum(up.reshape(4, 8, 128), axis=0)

    bias_top = lax.fori_loop(0, SLOTS * SIDE, top_rows, jnp.zeros((8, 128), F32), unroll=4)
    fill_bands(uplo, nbr)
    fill_bands(uphi, nbr)

    def shift_up(r, _):
        before = uf[pl.ds(r * FULL + 6, SIDE), :]
        same = uf[pl.ds(pl.multiple_of(r * FULL + 8, 8), SIDE), :]
        after = uf[pl.ds(r * FULL + 10, SIDE), :]
        at = pl.ds(pl.multiple_of(r * SIDE, 16), SIDE)
        uu[at, 0:128] = jnp.where(low, after, same).astype(BF16)
        uu[at, 128:256] = before.astype(BF16)
        return 0

    lax.fori_loop(0, SLOTS * SIDE, shift_up, 0, unroll=4)

    for t in range(SLOTS):
        for pair in range(SIDE // 2):
            x0 = outs[pl.ds(t * CELLS + 2 * pair, SIDE, stride=SIDE), :]
            x1 = outs[pl.ds(t * CELLS + 2 * pair + 1, SIDE, stride=SIDE), :]
            out[t, :, pair * 128 : pair * 128 + 128] = jnp.where(low, x0, x1).astype(BF16)

    zero_cols = jnp.zeros((256, 128), BF16)
    edges_l = jnp.concatenate([
        jnp.concatenate([ucol_w[...], zero_cols], axis=1),
        jnp.concatenate([zero_cols, ucol_e[...]], axis=1)], axis=0)
    edges_r = jnp.concatenate([sh_w[...], sh_e[...]], axis=0)
    across = (((0,), (0,)), ((), ()))
    acc_top[...] = lax.dot_general(edges_l, edges_r, across, preferred_element_type=F32)

    def grad_top(t, _):
        rhs = jnp.concatenate([hp[t, 64 * a : 64 * a + CELLS, :] for a in range(3)], axis=1)
        lhs = uu[pl.ds(pl.multiple_of(t * CELLS, 16), CELLS), :]
        acc_top[...] += lax.dot_general(lhs, rhs, across, preferred_element_type=F32)
        return 0

    lax.fori_loop(0, SLOTS, grad_top, 0)

    def conv_back(t, _):
        first = uplo[t, 0:CELLS, :] + uphi[t, 64 : 64 + CELLS, :]
        lhs = jnp.concatenate([first, uplo[t, 128 : 128 + CELLS, :]], axis=1)
        y = jnp.dot(lhs, wback[...], preferred_element_type=F32)
        for i in range(SIDE):
            r = t * SIDE + i
            rows = slice(i * SIDE, i * SIDE + SIDE)
            y0[pl.ds(pl.multiple_of(r * WIDE + 8, 8), SIDE), :] = y[rows, 0:128]
            y1[pl.ds(pl.multiple_of(r * SIDE, 8), SIDE), :] = y[rows, 128:256]
            y2[pl.ds(pl.multiple_of(r * WIDE, 8), SIDE), :] = y[rows, 256:384]
        return 0

    lax.fori_loop(0, SLOTS, conv_back, 0)

    for copy in upstream_copies:
        copy.wait()
    for received, up, side, down, dest in (
        (urecv.at[0], 0, 3, 5, su_w), (urecv.at[1], 2, 4, 7, su_e)):
        def strip_of(index):
            return received[jnp.maximum(index, 0)].astype(F32) * present(index)

        for t in range(SLOTS):
            base = t * FULL
            work[base : base + 8, :] = strip_of(nbr[t, up])[24:32]
            work[base + 8 : base + 40, :] = strip_of(nbr[t, side])
            work[base + 40 : base + 48, :] = strip_of(nbr[t, down])[0:8]
        for t in range(SLOTS):
            v = [work[t * FULL + 6 + 2 * a : t * FULL + 38 + 2 * a, :] for a in range(3)]
            w = [pltpu.roll(x, 64, 1) for x in v]
            at = t * 64
            dest[at : at + 32, 0:128] = jnp.where(low, v[0], w[1]).astype(BF16)
            dest[at : at + 32, 128:256] = jnp.where(low, v[2], zero_rows).astype(BF16)
            dest[at + 32 : at + 64, 0:128] = jnp.where(low, w[0], v[1]).astype(BF16)
            dest[at + 32 : at + 64, 128:256] = jnp.where(low, w[2], zero_rows).astype(BF16)
    add_margins(
        jnp.dot(su_w[...], wback[:, 0:128], preferred_element_type=F32),
        jnp.dot(su_e[...], wback[:, 256:384], preferred_element_type=F32))

    def slopes(r, total):
        back = mid_rows(r) * slope[pl.ds(pl.multiple_of(r * SIDE, 8), SIDE), :]
        back = back.astype(BF16).astype(F32)
        sf[pl.ds(pl.multiple_of(r * FULL + 8, 8), SIDE), :] = back
        return total + jnp.sum(back.reshape(4, 8, 128), axis=0)

    bias_mid = lax.fori_loop(0, SLOTS * SIDE, slopes, jnp.zeros((8, 128), F32), unroll=4)

    def shift_slope(r, _):
        at = pl.ds(pl.multiple_of(r * SIDE, 16), SIDE)
        ss[at, 0:128] = sf[pl.ds(r * FULL + 10, SIDE), :].astype(BF16)
        ss[at, 128:256] = sf[pl.ds(pl.multiple_of(r * FULL + 8, 8), SIDE), :].astype(BF16)
        ss[at, 256:384] = sf[pl.ds(r * FULL + 6, SIDE), :].astype(BF16)
        return 0

    lax.fori_loop(0, SLOTS * SIDE, shift_slope, 0, unroll=4)
    for t in range(SLOTS):
        for side, col, cell in columns:
            edge = scol_w if side == 0 else scol_e
            at = (t * 2 + col) * 32
            edge[at : at + 32, :] = sf[
                pl.ds(t * SIDE * FULL + 8 + cell, SIDE, stride=FULL), :].astype(BF16)

    acc_mid[0:128, :] = lax.dot_general(scol_w[...], sa_w[...], across, preferred_element_type=F32)
    acc_mid[128:256, :] = jnp.zeros((128, 768), F32)
    acc_mid[256:384, :] = lax.dot_general(scol_e[...], sa_e[...], across, preferred_element_type=F32)

    def grad_mid(t, _):
        rhs = jnp.concatenate([fp[t, 64 * a : 64 * a + CELLS, :] for a in range(3)], axis=1)
        lhs = ss[pl.ds(pl.multiple_of(t * CELLS, 16), CELLS), :]
        acc_mid[...] += lax.dot_general(lhs, rhs, across, preferred_element_type=F32)
        return 0

    lax.fori_loop(0, SLOTS, grad_mid, 0)

    for a in range(3):
        for b in range(3):
            at = (a * 3 + b) * 256
            grad[at : at + 256, :] = acc_mid[b * 128 : b * 128 + 128, a * 256 : a * 256 + 256].T
        for half in range(2):
            at = 2304 + half * 384 + a * 128
            grad[at : at + 128, :] = acc_top[
                half * 128 : half * 128 + 128, a * 128 : a * 128 + 128].T
    grad[3072:3080, :] = bias_mid
    grad[3080:3088, :] = bias_top


def shards(features, cotangent, neighbors, live_count, kernel_mid, bias_mid, kernel_top, bias_top):
    slots, side, _, channels = features.shape
    vmem = pl.BlockSpec(memory_space=pltpu.VMEM)
    smem = pl.BlockSpec(memory_space=pltpu.SMEM)
    hbm = pl.BlockSpec(memory_space=pl.ANY)
    rows = SLOTS * SIDE
    out, grad = pl.pallas_call(
        kernel,
        out_shape=(
            jax.ShapeDtypeStruct((SLOTS, SIDE, 2048), BF16),
            jax.ShapeDtypeStruct((3088, 128), F32),
        ),
        in_specs=[hbm, hbm, smem, smem, hbm, vmem, vmem, vmem],
        out_specs=(vmem, vmem),
        scratch_shapes=[
            pltpu.VMEM((SLOTS, PADDED, 256), BF16),
            pltpu.VMEM((SLOTS, PADDED, 128), BF16),
            pltpu.VMEM((768, 384), BF16),
            pltpu.VMEM((384, 256), BF16),
            pltpu.VMEM((256, 384), BF16),
            pltpu.VMEM((rows * WIDE, 128), F32),
            pltpu.VMEM((rows * SIDE, 128), F32),
            pltpu.VMEM((rows * WIDE, 128), F32),
            pltpu.VMEM((rows * FULL, 128), F32),
            pltpu.VMEM((rows * SIDE, 128), F32),
            pltpu.VMEM((8 * FULL, 128), F32),
            pltpu.VMEM((256, 768), BF16),
            pltpu.VMEM((256, 768), BF16),
            pltpu.VMEM((256, 384), BF16),
            pltpu.VMEM((256, 384), BF16),
            pltpu.VMEM((256, 256), BF16),
            pltpu.VMEM((256, 256), BF16),
            pltpu.VMEM((rows * 8, 128), F32),
            pltpu.VMEM((rows * 8, 128), F32),
            pltpu.VMEM((2, 8, 32, 256), BF16),
            pltpu.VMEM((2, 8, 32, 256), BF16),
            pltpu.VMEM((2, 8, 32, 128), BF16),
            pltpu.VMEM((2, 8, 32, 128), BF16),
            pltpu.VMEM((2, 4, 32, 128), BF16),
            pltpu.VMEM((2, 4, 32, 128), BF16),
            pltpu.VMEM((rows * SIDE, 128), F32),
            pltpu.VMEM((rows * SIDE, 128), F32),
            pltpu.VMEM((rows * SIDE, 128), F32),
            pltpu.VMEM((rows * FULL, 128), F32),
            pltpu.VMEM((SLOTS, PADDED, 128), BF16),
            pltpu.VMEM((SLOTS, PADDED, 128), BF16),
            pltpu.VMEM((rows * SIDE, 256), BF16),
            pltpu.VMEM((256, 128), BF16),
            pltpu.VMEM((256, 128), BF16),
            pltpu.VMEM((256, 128), BF16),
            pltpu.VMEM((256, 128), BF16),
            pltpu.VMEM((rows * FULL, 128), F32),
            pltpu.VMEM((rows * SIDE, 384), BF16),
            pltpu.VMEM((384, 768), F32),
            pltpu.VMEM((256, 384), F32),
            pltpu.VMEM((SLOTS, SIDE, 2048), BF16),
            pltpu.SemaphoreType.DMA((14,)),
            pltpu.SemaphoreType.DMA((6,)),
            pltpu.SemaphoreType.DMA((6,)),
        ],
        compiler_params=pltpu.CompilerParams(
            collective_id=0, has_side_effects=True, vmem_limit_bytes=60 * 2**20),
        name="backend_layers",
    )(
        features.reshape(slots, side * side, channels), cotangent, neighbors, live_count,
        kernel_mid, bias_mid.reshape(1, 128), kernel_top,
        jnp.concatenate([bias_top, bias_top]).reshape(1, 128),
    )
    grad = lax.psum(grad, ("rep", "tile"))
    grad_mid = grad[:2304].reshape(3, 3, 256, 128)
    low = grad[2304:2688].reshape(3, 128, 2, 64).transpose(0, 2, 1, 3)
    high = grad[2688:3072, 0:64].reshape(3, 1, 128, 64)
    grad_top = jnp.concatenate([low, high], axis=1)
    bias_mid_sum = jnp.sum(grad[3072:3080], axis=0)
    bias_top_sum = jnp.sum(grad[3080:3088, 0:64], axis=0)
    return out, grad_mid, bias_mid_sum, grad_top, bias_top_sum


def solution(mesh):
    in_specs = (
        P(("rep", "tile"), None, None, None),
        P(("rep", "tile"), None, None),
        P(("rep", "tile"), None),
        P(("rep", "tile")),
        P(),
        P(),
        P(),
        P(),
    )
    out_specs = (P(("rep", "tile"), None, None), P(), P(), P(), P())
    return jax.shard_map(shards, mesh=mesh, in_specs=in_specs, out_specs=out_specs, check_vma=False)
```

```python
import functools

import jax
import jax.numpy as jnp
from jax import lax
from jax.experimental import pallas as pl
from jax.experimental.pallas import tpu as pltpu
from jax.sharding import PartitionSpec as P

F32 = jnp.float32
BF16 = jnp.bfloat16
MESH = pl.DeviceIdType.MESH

SLOTS = 4
SIDE = 32
CELLS = SIDE * SIDE
PADDED = CELLS + 128
WIDE = 40
FULL = 48


def sigmoid(v):
    return 0.5 * jnp.tanh(0.5 * v) + 0.5


def low_lanes(shape):
    return lax.broadcasted_iota(jnp.int32, shape, len(shape) - 1) < 64


def present(index):
    return jnp.where(index >= 0, 1.0, 0.0).astype(F32)


def fill_bands(padded, nbr):
    for t in range(SLOTS):
        north, south = nbr[t, 1], nbr[t, 6]
        band = padded[jnp.maximum(north, 0), CELLS : CELLS + 64, :].astype(F32)
        padded[t, 0:64, :] = (band * present(north)).astype(BF16)
        band = padded[jnp.maximum(south, 0), 64:128, :].astype(F32)
        padded[t, CELLS + 64 : PADDED, :] = (band * present(south)).astype(BF16)


def strip_block(received, index, col, lanes):
    return received[jnp.maximum(index, 0) * 2 + col, :, lanes].astype(F32) * present(index)


def margin_strips(received, nbr, corner_up, side, corner_down, work, shifted, channels):
    for lane_tile in range(channels // 128):
        lanes = slice(lane_tile * 128, lane_tile * 128 + 128)
        for t in range(SLOTS):
            for col in range(2):
                base = (t * 2 + col) * FULL
                up = strip_block(received, nbr[t, corner_up], col, lanes)
                mid = strip_block(received, nbr[t, side], col, lanes)
                down = strip_block(received, nbr[t, corner_down], col, lanes)
                work[base : base + 8, :] = up[24:32]
                work[base + 8 : base + 40, :] = mid
                work[base + 40 : base + 48, :] = down[0:8]
        for block in range(SLOTS * 2):
            for a in range(3):
                rows = work[block * FULL + 6 + 2 * a : block * FULL + 38 + 2 * a, :]
                at = a * channels + lane_tile * 128
                shifted[block * 32 : block * 32 + 32, at : at + 128] = rows.astype(BF16)


def kernel(
    feat, cot, nbr, live, kmid, bmid, ktop, btop,
    out, gmid_out, gtop_out, bmid_out, btop_out,
    fp, hp, wmid, wtop, wback, y0, y1, y2, ya, yb, work, sa_w, sa_e, sh_w, sh_e, su_w, su_e,
    strip_a, strip_b, fsend, frecv, hsend, hrecv, usend, urecv,
    slope, cots, outs, uf, uplo, uphi, uu, ucol_w, ucol_e, scol_w, scol_e, sf,
    sst, acc_top, cotv, grad, sum_core, core_in, first_out, first_in, second_out, second_in,
    third_in, second_back, first_back, total,
    local_sem, send_sem, recv_sem, sum_send, sum_recv,
):
    n = lax.axis_size("tile")
    me = lax.axis_index("tile")
    right, left = lax.rem(me + 1, n), lax.rem(me + n - 1, n)
    z, y, x, core = lax.axis_index("rep"), me // 8, lax.rem(me // 2, 4), lax.rem(me, 2)
    place = {"x": x, "y": y, "z": z}

    def on_chip(where, c):
        return {"rep": where["z"], "tile": where["y"] * 8 + where["x"] * 2 + c}

    def along(axis, distance):
        there = dict(place)
        there[axis] = lax.rem(place[axis] + distance, 4)
        return on_chip(there, core)

    loads = []
    for t in range(SLOTS):
        loads.append(pltpu.make_async_copy(
            feat.at[t], fp.at[t, pl.ds(64, CELLS)], local_sem.at[t]))
    for a in range(3):
        for b in range(3):
            loads.append(pltpu.make_async_copy(
                kmid.at[a, b],
                wmid.at[pl.ds(a * 256, 256), pl.ds(b * 128, 128)],
                local_sem.at[4 + a * 3 + b]))
    loads.append(pltpu.make_async_copy(cot, cotv, local_sem.at[13]))
    for copy in loads:
        copy.start()

    barrier = pltpu.get_barrier_semaphore()
    for neighbour in (left, right):
        pl.semaphore_signal(barrier, inc=1, device_id={"tile": neighbour}, device_id_type=MESH)
    pl.semaphore_signal(barrier, inc=1, device_id=on_chip(place, 1 - core), device_id_type=MESH)
    for axis in "xyz":
        for distance in (1, 2, 3):
            pl.semaphore_signal(
                barrier, inc=1, device_id=along(axis, distance), device_id_type=MESH)

    zero8 = jnp.zeros((8, 128), F32)

    def clear(r, _):
        base = pl.multiple_of(r * FULL, 8)
        uf[pl.ds(base, 8), :] = zero8
        uf[pl.ds(base + 40, 8), :] = zero8
        sf[pl.ds(base, 8), :] = zero8
        sf[pl.ds(base + 40, 8), :] = zero8
        return 0

    lax.fori_loop(0, SLOTS * SIDE, clear, 0)

    for a in range(3):
        outer = jnp.concatenate([ktop[a, 0], ktop[a, 2]], axis=0).astype(F32).T
        centre = jnp.concatenate([ktop[a, 1], ktop[a, 1]], axis=0).astype(F32).T
        wtop[a * 128 : a * 128 + 128, 0:128] = outer.astype(BF16)
        wtop[a * 128 : a * 128 + 128, 128:256] = centre.astype(BF16)
        for b in range(3):
            wback[a * 64 : a * 64 + 64, b * 128 : b * 128 + 128] = ktop[2 - a, 2 - b]
    wback[192:256, :] = jnp.zeros((64, 384), BF16)
    btop_twice = jnp.concatenate([btop[...], btop[...]], axis=1)

    for copy in loads[:SLOTS]:
        copy.wait()

    for side, (cells, picks) in enumerate(((0, (0, 1)), (16, (6, 7)))):
        def gather(r, _):
            t, i = r // SIDE, r % SIDE
            rows = fp[t, pl.ds(pl.multiple_of(64 + i * SIDE + cells, 16), 16), :].astype(F32)
            rows = rows[0:8] if cells == 0 else rows[8:16]
            at = pl.multiple_of(r * 8, 8)
            strip_a[pl.ds(at, 8), :] = rows[:, 0:128]
            strip_b[pl.ds(at, 8), :] = rows[:, 128:256]
            return 0

        lax.fori_loop(0, SLOTS * SIDE, gather, 0, unroll=4)
        for t in range(SLOTS):
            for col, pick in enumerate(picks):
                at = pl.ds(t * 256 + pick, 32, stride=8)
                fsend[side, t * 2 + col, :, 0:128] = strip_a[at, :].astype(BF16)
                fsend[side, t * 2 + col, :, 128:256] = strip_b[at, :].astype(BF16)

    pl.semaphore_wait(barrier, 12)

    def exchange(send, recv, at):
        copies = []
        for side, target in ((0, left), (1, right)):
            copies.append(pltpu.make_async_remote_copy(
                src_ref=send.at[side], dst_ref=recv.at[1 - side],
                send_sem=send_sem.at[at + side], recv_sem=recv_sem.at[at + 1 - side],
                device_id={"tile": target}, device_id_type=MESH))
        for copy in copies:
            copy.start()
        return copies

    feature_copies = exchange(fsend, frecv, 0)

    fill_bands(fp, nbr)
    for copy in loads[SLOTS:]:
        copy.wait()

    def conv_mid(t, _):
        lhs = jnp.concatenate([fp[t, 64 * a : 64 * a + CELLS, :] for a in range(3)], axis=1)
        y = jnp.dot(lhs, wmid[...], preferred_element_type=F32)
        for i in range(SIDE):
            r = t * SIDE + i
            rows = slice(i * SIDE, i * SIDE + SIDE)
            y0[pl.ds(pl.multiple_of(r * WIDE + 8, 8), SIDE), :] = y[rows, 0:128]
            y1[pl.ds(pl.multiple_of(r * SIDE, 8), SIDE), :] = y[rows, 128:256]
            y2[pl.ds(pl.multiple_of(r * WIDE, 8), SIDE), :] = y[rows, 256:384]
        return 0

    lax.fori_loop(0, SLOTS, conv_mid, 0)

    low = low_lanes((SIDE, 128))
    for t in range(SLOTS):
        for pair in range(SIDE // 2):
            x = cotv[t, :, pair * 128 : pair * 128 + 128].astype(F32)
            turned = pltpu.roll(x, 64, 1)
            cots[pl.ds(t * CELLS + 2 * pair, SIDE, stride=SIDE), :] = jnp.where(low, x, turned)
            cots[pl.ds(t * CELLS + 2 * pair + 1, SIDE, stride=SIDE), :] = jnp.where(low, turned, x)

    for copy in feature_copies:
        copy.wait()
    margin_strips(frecv.at[0], nbr, 0, 3, 5, work, sa_w, 256)
    margin_strips(frecv.at[1], nbr, 2, 4, 7, work, sa_e, 256)

    def add_margins(west, east):
        for t in range(SLOTS):
            for col in range(2):
                rows = slice((t * 2 + col) * 32, (t * 2 + col) * 32 + 32)
                y0[pl.ds(t * SIDE * WIDE + 6 + col, SIDE, stride=WIDE), :] = west[rows]
                y2[pl.ds(t * SIDE * WIDE + 32 + col, SIDE, stride=WIDE), :] = east[rows]

    add_margins(
        jnp.dot(sa_w[...], wmid[:, 0:128], preferred_element_type=F32),
        jnp.dot(sa_e[...], wmid[:, 256:384], preferred_element_type=F32))

    alive = [jnp.where(t < live[0], 1.0, 0.0).astype(F32) for t in range(SLOTS)]
    columns = ((0, 0, 0), (0, 1, 1), (1, 0, 30), (1, 1, 31))

    def mid_at(t, cell):
        first = y0[pl.ds(t * SIDE * WIDE + 6 + cell, SIDE, stride=WIDE), :]
        second = y1[pl.ds(t * CELLS + cell, SIDE, stride=SIDE), :]
        third = y2[pl.ds(t * SIDE * WIDE + 2 + cell, SIDE, stride=WIDE), :]
        return first + second + third

    for t in range(SLOTS):
        for side, col, cell in columns:
            pre = mid_at(t, cell) + bmid[...]
            hsend[side, t * 2 + col, :, :] = (pre * sigmoid(pre) * alive[t]).astype(BF16)
    hidden_copies = exchange(hsend, hrecv, 2)

    def mid_rows(r):
        first = y0[pl.ds(r * WIDE + 6, SIDE), :]
        second = y1[pl.ds(pl.multiple_of(r * SIDE, 8), SIDE), :]
        third = y2[pl.ds(r * WIDE + 2, SIDE), :]
        return first + second + third

    def activate(r, _):
        t, i = r // SIDE, r % SIDE
        mask = jnp.where(t < live[0], 1.0, 0.0).astype(F32)
        pre = mid_rows(r) + bmid[...]
        gate = sigmoid(pre)
        hidden = pre * gate
        hp[t, pl.ds(pl.multiple_of(64 + i * SIDE, 16), SIDE), :] = (hidden * mask).astype(BF16)
        slope[pl.ds(pl.multiple_of(r * SIDE, 8), SIDE), :] = (gate + hidden * (1.0 - gate)) * mask
        return 0

    lax.fori_loop(0, SLOTS * SIDE, activate, 0, unroll=4)
    fill_bands(hp, nbr)

    def conv_top(t, _):
        lhs = jnp.concatenate([hp[t, 64 * a : 64 * a + CELLS, :] for a in range(3)], axis=1)
        y = jnp.dot(lhs, wtop[...], preferred_element_type=F32)
        for i in range(SIDE):
            r = t * SIDE + i
            rows = slice(i * SIDE, i * SIDE + SIDE)
            ya[pl.ds(pl.multiple_of(r * FULL + 8, 8), SIDE), :] = y[rows, 0:128]
            yb[pl.ds(pl.multiple_of(r * SIDE, 8), SIDE), :] = y[rows, 128:256]
        return 0

    lax.fori_loop(0, SLOTS, conv_top, 0)

    for copy in hidden_copies:
        copy.wait()
    margin_strips(hrecv.at[0], nbr, 0, 3, 5, work, sh_w, 128)
    margin_strips(hrecv.at[1], nbr, 2, 4, 7, work, sh_e, 128)
    west = jnp.dot(sh_w[...], wtop[:, 0:128], preferred_element_type=F32)
    east = jnp.dot(sh_e[...], wtop[:, 0:128], preferred_element_type=F32)
    for t in range(SLOTS):
        for col in range(2):
            rows = slice((t * 2 + col) * 32, (t * 2 + col) * 32 + 32)
            ya[pl.ds(t * SIDE * FULL + 6 + col, SIDE, stride=FULL), :] = west[rows]
            ya[pl.ds(t * SIDE * FULL + 40 + col, SIDE, stride=FULL), :] = east[rows]

    def up_of(before, after, centre, cotangent):
        pair = jnp.where(low, before, after)
        pre = pair + pltpu.roll(pair, 64, 1) + centre + btop_twice
        gate = sigmoid(pre)
        value = pre * gate
        return value, cotangent * (gate + value * (1.0 - gate))

    zero_rows = jnp.zeros((SIDE, 128), F32)
    for t in range(SLOTS):
        for side in range(2):
            ups = []
            for col in range(2):
                cell = 30 * side + col
                _, up = up_of(
                    ya[pl.ds(t * SIDE * FULL + 6 + cell, SIDE, stride=FULL), :],
                    ya[pl.ds(t * SIDE * FULL + 10 + cell, SIDE, stride=FULL), :],
                    yb[pl.ds(t * CELLS + cell, SIDE, stride=SIDE), :],
                    cots[pl.ds(t * CELLS + cell, SIDE, stride=SIDE), :])
                up = up * alive[t]
                ups.append(up)
                edge = ucol_w if side == 0 else ucol_e
                at = (t * 2 + col) * 32
                edge[at : at + 32, :] = jnp.where(low, up, zero_rows).astype(BF16)
            usend[side, t] = jnp.where(low, ups[0], ups[1]).astype(BF16)
    upstream_copies = exchange(usend, urecv, 4)

    def top_rows(r, total):
        t, i = r // SIDE, r % SIDE
        mask = jnp.where(t < live[0], 1.0, 0.0).astype(F32)
        value, up = up_of(
            ya[pl.ds(r * FULL + 6, SIDE), :],
            ya[pl.ds(r * FULL + 10, SIDE), :],
            yb[pl.ds(pl.multiple_of(r * SIDE, 8), SIDE), :],
            cots[pl.ds(pl.multiple_of(r * SIDE, 8), SIDE), :])
        outs[pl.ds(pl.multiple_of(r * SIDE, 8), SIDE), :] = value * mask
        up = (up * mask).astype(BF16).astype(F32)
        uf[pl.ds(pl.multiple_of(r * FULL + 8, 8), SIDE), :] = up
        at = pl.ds(pl.multiple_of(64 + i * SIDE, 16), SIDE)
        uplo[t, at, :] = jnp.where(low, up, zero_rows).astype(BF16)
        uphi[t, at, :] = jnp.where(low, zero_rows, up).astype(BF16)
        return total + jnp.sum(up.reshape(4, 8, 128), axis=0)

    bias_top = lax.fori_loop(0, SLOTS * SIDE, top_rows, jnp.zeros((8, 128), F32), unroll=4)
    fill_bands(uplo, nbr)
    fill_bands(uphi, nbr)

    def shift_up(r, _):
        before = uf[pl.ds(r * FULL + 6, SIDE), :]
        same = uf[pl.ds(pl.multiple_of(r * FULL + 8, 8), SIDE), :]
        after = uf[pl.ds(r * FULL + 10, SIDE), :]
        at = pl.ds(pl.multiple_of(r * SIDE, 16), SIDE)
        uu[at, 0:128] = jnp.where(low, after, same).astype(BF16)
        uu[at, 128:256] = before.astype(BF16)
        return 0

    lax.fori_loop(0, SLOTS * SIDE, shift_up, 0, unroll=4)

    for t in range(SLOTS):
        for pair in range(SIDE // 2):
            x0 = outs[pl.ds(t * CELLS + 2 * pair, SIDE, stride=SIDE), :]
            x1 = outs[pl.ds(t * CELLS + 2 * pair + 1, SIDE, stride=SIDE), :]
            out[t, :, pair * 128 : pair * 128 + 128] = jnp.where(low, x0, x1).astype(BF16)

    zero_cols = jnp.zeros((256, 128), BF16)
    edges_l = jnp.concatenate([
        jnp.concatenate([ucol_w[...], zero_cols], axis=1),
        jnp.concatenate([zero_cols, ucol_e[...]], axis=1)], axis=0)
    edges_r = jnp.concatenate([sh_w[...], sh_e[...]], axis=0)
    across = (((0,), (0,)), ((), ()))
    acc_top[...] = lax.dot_general(edges_l, edges_r, across, preferred_element_type=F32)

    def grad_top(t, _):
        rhs = jnp.concatenate([hp[t, 64 * a : 64 * a + CELLS, :] for a in range(3)], axis=1)
        lhs = uu[pl.ds(pl.multiple_of(t * CELLS, 16), CELLS), :]
        acc_top[...] += lax.dot_general(lhs, rhs, across, preferred_element_type=F32)
        return 0

    lax.fori_loop(0, SLOTS, grad_top, 0)

    def conv_back(t, _):
        first = uplo[t, 0:CELLS, :] + uphi[t, 64 : 64 + CELLS, :]
        lhs = jnp.concatenate([first, uplo[t, 128 : 128 + CELLS, :]], axis=1)
        y = jnp.dot(lhs, wback[...], preferred_element_type=F32)
        for i in range(SIDE):
            r = t * SIDE + i
            rows = slice(i * SIDE, i * SIDE + SIDE)
            y0[pl.ds(pl.multiple_of(r * WIDE + 8, 8), SIDE), :] = y[rows, 0:128]
            y1[pl.ds(pl.multiple_of(r * SIDE, 8), SIDE), :] = y[rows, 128:256]
            y2[pl.ds(pl.multiple_of(r * WIDE, 8), SIDE), :] = y[rows, 256:384]
        return 0

    lax.fori_loop(0, SLOTS, conv_back, 0)

    for copy in upstream_copies:
        copy.wait()
    for received, up, side, down, dest in (
        (urecv.at[0], 0, 3, 5, su_w), (urecv.at[1], 2, 4, 7, su_e)):
        def strip_of(index):
            return received[jnp.maximum(index, 0)].astype(F32) * present(index)

        for t in range(SLOTS):
            base = t * FULL
            work[base : base + 8, :] = strip_of(nbr[t, up])[24:32]
            work[base + 8 : base + 40, :] = strip_of(nbr[t, side])
            work[base + 40 : base + 48, :] = strip_of(nbr[t, down])[0:8]
        for t in range(SLOTS):
            v = [work[t * FULL + 6 + 2 * a : t * FULL + 38 + 2 * a, :] for a in range(3)]
            w = [pltpu.roll(x, 64, 1) for x in v]
            at = t * 64
            dest[at : at + 32, 0:128] = jnp.where(low, v[0], w[1]).astype(BF16)
            dest[at : at + 32, 128:256] = jnp.where(low, v[2], zero_rows).astype(BF16)
            dest[at + 32 : at + 64, 0:128] = jnp.where(low, w[0], v[1]).astype(BF16)
            dest[at + 32 : at + 64, 128:256] = jnp.where(low, w[2], zero_rows).astype(BF16)
    add_margins(
        jnp.dot(su_w[...], wback[:, 0:128], preferred_element_type=F32),
        jnp.dot(su_e[...], wback[:, 256:384], preferred_element_type=F32))

    def slopes(r, total):
        back = mid_rows(r) * slope[pl.ds(pl.multiple_of(r * SIDE, 8), SIDE), :]
        back = back.astype(BF16).astype(F32)
        sf[pl.ds(pl.multiple_of(r * FULL + 8, 8), SIDE), :] = back
        return total + jnp.sum(back.reshape(4, 8, 128), axis=0)

    bias_mid = lax.fori_loop(0, SLOTS * SIDE, slopes, jnp.zeros((8, 128), F32), unroll=4)

    def shift_slope(g, _):
        at = pl.ds(pl.multiple_of(g * 128, 128), 128)
        for b, first in enumerate((10, 8, 6)):
            rows = [sf[pl.ds((g * 4 + k) * FULL + first, SIDE), :] for k in range(4)]
            block = jnp.concatenate(rows, axis=0).astype(BF16)
            sst[b * 128 : b * 128 + 128, at] = block.T
        return 0

    lax.fori_loop(0, SLOTS * SIDE // 4, shift_slope, 0)
    for t in range(SLOTS):
        for side, col, cell in columns:
            edge = scol_w if side == 0 else scol_e
            at = (t * 2 + col) * 32
            edge[at : at + 32, :] = sf[
                pl.ds(t * SIDE * FULL + 8 + cell, SIDE, stride=FULL), :].astype(BF16)

    def send(chunk, at, src, dst, device):
        copy = pltpu.make_async_remote_copy(
            src_ref=src, dst_ref=dst, send_sem=sum_send.at[chunk, at],
            recv_sem=sum_recv.at[chunk, at], device_id=device, device_id_type=MESH)
        copy.start()
        return copy

    def reducer(chunk, order):
        axes = tuple(order)
        at = [place[axis] for axis in axes]
        other = on_chip(place, 1 - core)
        pending, started = [], []

        def spread(base, axis_at, src_of, dst_of):
            pending.clear()
            for d in (1, 2, 3):
                to = lax.rem(at[axis_at] + d, 4)
                copy = send(chunk, base + d - 1, src_of(to), dst_of(d), along(axes[axis_at], d))
                pending.append(copy)
            started.extend(pending)

        def arrive():
            for copy in pending:
                copy.wait_recv()

        def rows_at(index, size):
            return pl.ds(pl.multiple_of(index * size, 8), size)

        def split_core():
            sum_core[chunk] = grad[chunk].astype(BF16)
            pending.clear()
            pending.append(send(
                chunk, 0, sum_core.at[chunk, rows_at(1 - core, 384)], core_in.at[chunk], other))
            started.extend(pending)

        def split_first():
            arrive()
            mine = grad[chunk, rows_at(core, 384), :]
            first_out[chunk] = (mine + core_in[chunk].astype(F32)).astype(BF16)
            spread(1, 0, lambda to: first_out.at[chunk, rows_at(to, 96)],
                   lambda d: first_in.at[chunk, d - 1])

        def split_second():
            arrive()
            value = first_out[chunk, rows_at(at[0], 96), :].astype(F32)
            for d in range(3):
                value = value + first_in[chunk, d].astype(F32)
            second_out[chunk] = value
            spread(4, 1, lambda to: second_out.at[chunk, rows_at(to, 24)],
                   lambda d: second_in.at[chunk, d - 1])

        def swap_third():
            arrive()
            value = second_out[chunk, rows_at(at[1], 24), :]
            for d in range(3):
                value = value + second_in[chunk, d]
            third_in[chunk, at[2]] = value
            spread(7, 2, lambda to: third_in.at[chunk, at[2]],
                   lambda d: third_in.at[chunk, at[2]])

        def back_second():
            arrive()
            value = third_in[chunk, 0] + third_in[chunk, 1]
            value = value + (third_in[chunk, 2] + third_in[chunk, 3])
            mine = rows_at(at[1], 24)
            second_back[chunk, mine, :] = value
            spread(10, 1, lambda to: second_back.at[chunk, mine],
                   lambda d: second_back.at[chunk, mine])

        def back_first():
            arrive()
            mine = rows_at(at[0], 96)
            first_back[chunk, mine, :] = second_back[chunk].astype(BF16)
            spread(13, 0, lambda to: first_back.at[chunk, mine],
                   lambda d: first_back.at[chunk, mine])

        def back_core():
            arrive()
            mine = rows_at(core, 384)
            pending.clear()
            pending.append(send(
                chunk, 16, first_back.at[chunk], total.at[chunk, mine], other))
            started.extend(pending)
            total[chunk, mine, :] = first_back[chunk]

        def finish():
            arrive()
            for copy in started:
                copy.wait_send()

        return iter((split_core, split_first, split_second, swap_third,
                     back_second, back_first, back_core, finish))

    reducers = [reducer(0, "zyx"), reducer(1, "xyz"), reducer(2, "yzx"), reducer(3, "zxy")]

    def advance(*chunks):
        for chunk in chunks:
            step = next(reducers[chunk], None)
            if step is not None:
                step()

    for a in range(3):
        for b in range(3):
            at = (a * 3 + b) * 64
            grad[0, at : at + 64, :] = acc_top[b * 64 : b * 64 + 64, a * 128 : a * 128 + 128]
    grad[0, 576:584, :] = bias_mid
    grad[0, 584:592, :] = bias_top
    grad[0, 592:768, :] = jnp.zeros((176, 128), F32)
    advance(0)

    for a in range(3):
        parts = []
        for t in range(SLOTS):
            parts.append(jnp.dot(
                sst[:, t * CELLS : t * CELLS + CELLS], fp[t, 64 * a : 64 * a + CELLS, :],
                preferred_element_type=F32))
        acc = (parts[0] + parts[1]) + (parts[2] + parts[3])
        q = slice(a * 256, a * 256 + 256)
        west = lax.dot_general(scol_w[...], sa_w[:, q], across, preferred_element_type=F32)
        east = lax.dot_general(scol_e[...], sa_e[:, q], across, preferred_element_type=F32)
        grad[1 + a, 0:256, :] = (acc[0:128] + west).T
        grad[1 + a, 256:512, :] = acc[128:256].T
        grad[1 + a, 512:768, :] = (acc[256:384] + east).T
        advance(*range(a + 1, -1, -1))
    for _ in range(7):
        advance(0, 1, 2, 3)

    for a in range(3):
        gmid_out[a * 768 : a * 768 + 768, :] = total[1 + a]
    gtop_out[...] = total[0, 0:576, :]
    sums = total[0, 576:592, :].astype(F32)
    bmid_out[...] = jnp.sum(sums[0:8], axis=0, keepdims=True)
    btop_out[...] = jnp.sum(sums[8:16], axis=0, keepdims=True)[:, 0:64]


def shards(features, cotangent, neighbors, live_count, kernel_mid, bias_mid, kernel_top, bias_top):
    slots, side, _, channels = features.shape
    vmem = pl.BlockSpec(memory_space=pltpu.VMEM)
    smem = pl.BlockSpec(memory_space=pltpu.SMEM)
    hbm = pl.BlockSpec(memory_space=pl.ANY)
    rows = SLOTS * SIDE
    out, grad_mid, grad_top, bias_mid_sum, bias_top_sum = pl.pallas_call(
        kernel,
        out_shape=(
            jax.ShapeDtypeStruct((SLOTS, SIDE, 2048), BF16),
            jax.ShapeDtypeStruct((2304, 128), BF16),
            jax.ShapeDtypeStruct((576, 128), BF16),
            jax.ShapeDtypeStruct((1, 128), F32),
            jax.ShapeDtypeStruct((1, 64), F32),
        ),
        in_specs=[hbm, hbm, smem, smem, hbm, vmem, vmem, vmem],
        out_specs=(vmem,) * 5,
        scratch_shapes=[
            pltpu.VMEM((SLOTS, PADDED, 256), BF16),
            pltpu.VMEM((SLOTS, PADDED, 128), BF16),
            pltpu.VMEM((768, 384), BF16),
            pltpu.VMEM((384, 256), BF16),
            pltpu.VMEM((256, 384), BF16),
            pltpu.VMEM((rows * WIDE, 128), F32),
            pltpu.VMEM((rows * SIDE, 128), F32),
            pltpu.VMEM((rows * WIDE, 128), F32),
            pltpu.VMEM((rows * FULL, 128), F32),
            pltpu.VMEM((rows * SIDE, 128), F32),
            pltpu.VMEM((8 * FULL, 128), F32),
            pltpu.VMEM((256, 768), BF16),
            pltpu.VMEM((256, 768), BF16),
            pltpu.VMEM((256, 384), BF16),
            pltpu.VMEM((256, 384), BF16),
            pltpu.VMEM((256, 256), BF16),
            pltpu.VMEM((256, 256), BF16),
            pltpu.VMEM((rows * 8, 128), F32),
            pltpu.VMEM((rows * 8, 128), F32),
            pltpu.VMEM((2, 8, 32, 256), BF16),
            pltpu.VMEM((2, 8, 32, 256), BF16),
            pltpu.VMEM((2, 8, 32, 128), BF16),
            pltpu.VMEM((2, 8, 32, 128), BF16),
            pltpu.VMEM((2, 4, 32, 128), BF16),
            pltpu.VMEM((2, 4, 32, 128), BF16),
            pltpu.VMEM((rows * SIDE, 128), F32),
            pltpu.VMEM((rows * SIDE, 128), F32),
            pltpu.VMEM((rows * SIDE, 128), F32),
            pltpu.VMEM((rows * FULL, 128), F32),
            pltpu.VMEM((SLOTS, PADDED, 128), BF16),
            pltpu.VMEM((SLOTS, PADDED, 128), BF16),
            pltpu.VMEM((rows * SIDE, 256), BF16),
            pltpu.VMEM((256, 128), BF16),
            pltpu.VMEM((256, 128), BF16),
            pltpu.VMEM((256, 128), BF16),
            pltpu.VMEM((256, 128), BF16),
            pltpu.VMEM((rows * FULL, 128), F32),
            pltpu.VMEM((384, rows * SIDE), BF16),
            pltpu.VMEM((256, 384), F32),
            pltpu.VMEM((SLOTS, SIDE, 2048), BF16),
            pltpu.VMEM((4, 768, 128), F32),
            pltpu.VMEM((4, 768, 128), BF16),
            pltpu.VMEM((4, 384, 128), BF16),
            pltpu.VMEM((4, 384, 128), BF16),
            pltpu.VMEM((4, 3, 96, 128), BF16),
            pltpu.VMEM((4, 96, 128), F32),
            pltpu.VMEM((4, 3, 24, 128), F32),
            pltpu.VMEM((4, 4, 24, 128), F32),
            pltpu.VMEM((4, 96, 128), F32),
            pltpu.VMEM((4, 384, 128), BF16),
            pltpu.VMEM((4, 768, 128), BF16),
            pltpu.SemaphoreType.DMA((14,)),
            pltpu.SemaphoreType.DMA((6,)),
            pltpu.SemaphoreType.DMA((6,)),
            pltpu.SemaphoreType.DMA((4, 17)),
            pltpu.SemaphoreType.DMA((4, 17)),
        ],
        compiler_params=pltpu.CompilerParams(
            collective_id=0, has_side_effects=True, vmem_limit_bytes=60 * 2**20),
        name="backend_layers",
    )(
        features.reshape(slots, side * side, channels), cotangent, neighbors, live_count,
        kernel_mid, bias_mid.reshape(1, 128), jnp.swapaxes(kernel_top, 2, 3),
        bias_top.reshape(1, 64),
    )
    grad_mid = grad_mid.reshape(3, 3, 256, 128).astype(F32)
    grad_top = jnp.swapaxes(grad_top.reshape(3, 3, 64, 128), 2, 3).astype(F32)
    return out, grad_mid, bias_mid_sum.reshape(128), grad_top, bias_top_sum.reshape(64)


def solution(mesh):
    in_specs = (
        P(("rep", "tile"), None, None, None),
        P(("rep", "tile"), None, None),
        P(("rep", "tile"), None),
        P(("rep", "tile")),
        P(),
        P(),
        P(),
        P(),
    )
    out_specs = (P(("rep", "tile"), None, None), P(), P(), P(), P())
    return jax.shard_map(shards, mesh=mesh, in_specs=in_specs, out_specs=out_specs, check_vma=False)
```

```python
import functools

import jax
import jax.numpy as jnp
from jax import lax
from jax.experimental import pallas as pl
from jax.experimental.pallas import tpu as pltpu
from jax.sharding import PartitionSpec as P

F32 = jnp.float32
BF16 = jnp.bfloat16
MESH = pl.DeviceIdType.MESH

SLOTS = 4
SIDE = 32
CELLS = SIDE * SIDE
PADDED = CELLS + 128
WIDE = 40
FULL = 48


def sigmoid(v):
    return 0.5 * jnp.tanh(0.5 * v) + 0.5


def low_lanes(shape):
    return lax.broadcasted_iota(jnp.int32, shape, len(shape) - 1) < 64


def present(index):
    return jnp.where(index >= 0, 1.0, 0.0).astype(F32)


def fill_bands(padded, nbr):
    for t in range(SLOTS):
        north, south = nbr[t, 1], nbr[t, 6]
        band = padded[jnp.maximum(north, 0), CELLS : CELLS + 64, :].astype(F32)
        padded[t, 0:64, :] = (band * present(north)).astype(BF16)
        band = padded[jnp.maximum(south, 0), 64:128, :].astype(F32)
        padded[t, CELLS + 64 : PADDED, :] = (band * present(south)).astype(BF16)


def strip_block(received, index, col, lanes):
    return received[jnp.maximum(index, 0) * 2 + col, :, lanes].astype(F32) * present(index)


def margin_strips(received, nbr, corner_up, side, corner_down, work, shifted, channels):
    for lane_tile in range(channels // 128):
        lanes = slice(lane_tile * 128, lane_tile * 128 + 128)
        for t in range(SLOTS):
            for col in range(2):
                base = (t * 2 + col) * FULL
                up = strip_block(received, nbr[t, corner_up], col, lanes)
                mid = strip_block(received, nbr[t, side], col, lanes)
                down = strip_block(received, nbr[t, corner_down], col, lanes)
                work[base : base + 8, :] = up[24:32]
                work[base + 8 : base + 40, :] = mid
                work[base + 40 : base + 48, :] = down[0:8]
        for block in range(SLOTS * 2):
            for a in range(3):
                rows = work[block * FULL + 6 + 2 * a : block * FULL + 38 + 2 * a, :]
                at = a * channels + lane_tile * 128
                shifted[block * 32 : block * 32 + 32, at : at + 128] = rows.astype(BF16)


def kernel(
    feat, cot, nbr, live, kmid, bmid, ktop, btop,
    out, sums,
    fp, hp, wmid, wtop, wback, y0, y1, y2, ya, yb, work, sa_w, sa_e, sh_w, sh_e, su_w, su_e,
    strip_a, strip_b, fsend, frecv, hsend, hrecv, usend, urecv,
    slope, uf, uplo, uphi, uut, ucol_w, ucol_e, scol_w, scol_e, sf,
    sst, acc_mid, acc_top, cotv, grad, sum_core, core_in, plane_out, plane_in, line_in, total,
    local_sem, send_sem, recv_sem, sum_send, sum_recv,
):
    n = lax.axis_size("tile")
    me = lax.axis_index("tile")
    right, left = lax.rem(me + 1, n), lax.rem(me + n - 1, n)
    z, y, x, core = lax.axis_index("rep"), me // 8, lax.rem(me // 2, 4), lax.rem(me, 2)
    place = {"x": x, "y": y, "z": z}

    def on_chip(where, c):
        return {"rep": where["z"], "tile": where["y"] * 8 + where["x"] * 2 + c}

    def moved(steps):
        there = dict(place)
        for axis, distance in steps:
            there[axis] = lax.rem(place[axis] + distance, 4)
        return there

    corners = [(d, e) for d in range(4) for e in range(4) if d or e]
    orders = ("xyz", "yzx", "zxy")

    loads = []
    for t in range(SLOTS):
        loads.append(pltpu.make_async_copy(
            feat.at[t], fp.at[t, pl.ds(64, CELLS)], local_sem.at[t]))
    for a in range(3):
        for b in range(3):
            loads.append(pltpu.make_async_copy(
                kmid.at[a, b],
                wmid.at[pl.ds(a * 256, 256), pl.ds(b * 128, 128)],
                local_sem.at[4 + a * 3 + b]))
    loads.append(pltpu.make_async_copy(cot, cotv, local_sem.at[13]))
    for copy in loads:
        copy.start()

    barrier = pltpu.get_barrier_semaphore()
    for neighbour in (left, right):
        pl.semaphore_signal(barrier, inc=1, device_id={"tile": neighbour}, device_id_type=MESH)
    pl.semaphore_signal(barrier, inc=1, device_id=on_chip(place, 1 - core), device_id_type=MESH)
    for first, second, _ in orders:
        for d, e in corners:
            if d:
                pl.semaphore_signal(
                    barrier, inc=1, device_id=on_chip(moved(((first, d), (second, e))), core),
                    device_id_type=MESH)

    for copy in loads[:SLOTS]:
        copy.wait()

    for side, (cells, picks) in enumerate(((0, (0, 1)), (16, (6, 7)))):
        def gather(r, _):
            t, i = r // SIDE, r % SIDE
            rows = fp[t, pl.ds(pl.multiple_of(64 + i * SIDE + cells, 16), 16), :].astype(F32)
            rows = rows[0:8] if cells == 0 else rows[8:16]
            at = pl.multiple_of(r * 8, 8)
            strip_a[pl.ds(at, 8), :] = rows[:, 0:128]
            strip_b[pl.ds(at, 8), :] = rows[:, 128:256]
            return 0

        lax.fori_loop(0, SLOTS * SIDE, gather, 0, unroll=16)
        for t in range(SLOTS):
            for col, pick in enumerate(picks):
                at = pl.ds(t * 256 + pick, 32, stride=8)
                fsend[side, t * 2 + col, :, 0:128] = strip_a[at, :].astype(BF16)
                fsend[side, t * 2 + col, :, 128:256] = strip_b[at, :].astype(BF16)

    pl.semaphore_wait(barrier, 39)

    def exchange(send, recv, at):
        copies = []
        for side, target in ((0, left), (1, right)):
            copies.append(pltpu.make_async_remote_copy(
                src_ref=send.at[side], dst_ref=recv.at[1 - side],
                send_sem=send_sem.at[at + side], recv_sem=recv_sem.at[at + 1 - side],
                device_id={"tile": target}, device_id_type=MESH))
        for copy in copies:
            copy.start()
        return copies

    feature_copies = exchange(fsend, frecv, 0)

    zero8 = jnp.zeros((8, 128), F32)

    def clear(r, _):
        base = pl.multiple_of(r * FULL, 8)
        uf[pl.ds(base, 8), :] = zero8
        uf[pl.ds(base + 40, 8), :] = zero8
        sf[pl.ds(base, 8), :] = zero8
        sf[pl.ds(base + 40, 8), :] = zero8
        return 0

    lax.fori_loop(0, SLOTS * SIDE, clear, 0, unroll=8)

    for a in range(3):
        outer = jnp.concatenate([ktop[a, 0], ktop[a, 2]], axis=0).astype(F32).T
        centre = jnp.concatenate([ktop[a, 1], ktop[a, 1]], axis=0).astype(F32).T
        wtop[a * 128 : a * 128 + 128, 0:128] = outer.astype(BF16)
        wtop[a * 128 : a * 128 + 128, 128:256] = centre.astype(BF16)
        for b in range(3):
            wback[a * 64 : a * 64 + 64, b * 128 : b * 128 + 128] = ktop[2 - a, 2 - b]
    wback[192:256, :] = jnp.zeros((64, 384), BF16)
    btop_twice = jnp.concatenate([btop[...], btop[...]], axis=1)

    fill_bands(fp, nbr)
    for copy in loads[SLOTS:]:
        copy.wait()

    def conv_mid(t, _):
        lhs = jnp.concatenate([fp[t, 64 * a : 64 * a + CELLS, :] for a in range(3)], axis=1)
        y = jnp.dot(lhs, wmid[...], preferred_element_type=F32)
        for i in range(SIDE):
            r = t * SIDE + i
            rows = slice(i * SIDE, i * SIDE + SIDE)
            y0[pl.ds(pl.multiple_of(r * WIDE + 8, 8), SIDE), :] = y[rows, 0:128]
            y1[pl.ds(pl.multiple_of(r * SIDE, 8), SIDE), :] = y[rows, 128:256]
            y2[pl.ds(pl.multiple_of(r * WIDE, 8), SIDE), :] = y[rows, 256:384]
        return 0

    lax.fori_loop(0, SLOTS, conv_mid, 0)

    low = low_lanes((SIDE, 128))
    for copy in feature_copies:
        copy.wait()
    margin_strips(frecv.at[0], nbr, 0, 3, 5, work, sa_w, 256)
    margin_strips(frecv.at[1], nbr, 2, 4, 7, work, sa_e, 256)

    def add_margins(west, east):
        for t in range(SLOTS):
            for col in range(2):
                rows = slice((t * 2 + col) * 32, (t * 2 + col) * 32 + 32)
                y0[pl.ds(t * SIDE * WIDE + 6 + col, SIDE, stride=WIDE), :] = west[rows]
                y2[pl.ds(t * SIDE * WIDE + 32 + col, SIDE, stride=WIDE), :] = east[rows]

    add_margins(
        jnp.dot(sa_w[...], wmid[:, 0:128], preferred_element_type=F32),
        jnp.dot(sa_e[...], wmid[:, 256:384], preferred_element_type=F32))

    alive = [jnp.where(t < live[0], 1.0, 0.0).astype(F32) for t in range(SLOTS)]
    columns = ((0, 0, 0), (0, 1, 1), (1, 0, 30), (1, 1, 31))

    def mid_at(t, cell):
        first = y0[pl.ds(t * SIDE * WIDE + 6 + cell, SIDE, stride=WIDE), :]
        second = y1[pl.ds(t * CELLS + cell, SIDE, stride=SIDE), :]
        third = y2[pl.ds(t * SIDE * WIDE + 2 + cell, SIDE, stride=WIDE), :]
        return first + second + third

    for t in range(SLOTS):
        for side, col, cell in columns:
            pre = mid_at(t, cell) + bmid[...]
            hsend[side, t * 2 + col, :, :] = (pre * sigmoid(pre) * alive[t]).astype(BF16)
    hidden_copies = exchange(hsend, hrecv, 2)

    def mid_rows(r):
        first = y0[pl.ds(r * WIDE + 6, SIDE), :]
        second = y1[pl.ds(pl.multiple_of(r * SIDE, 8), SIDE), :]
        third = y2[pl.ds(r * WIDE + 2, SIDE), :]
        return first + second + third

    def activate(r, _):
        t, i = r // SIDE, r % SIDE
        mask = jnp.where(t < live[0], 1.0, 0.0).astype(F32)
        pre = mid_rows(r) + bmid[...]
        gate = sigmoid(pre)
        hidden = pre * gate
        hp[t, pl.ds(pl.multiple_of(64 + i * SIDE, 16), SIDE), :] = (hidden * mask).astype(BF16)
        slope[pl.ds(pl.multiple_of(r * SIDE, 8), SIDE), :] = (gate + hidden * (1.0 - gate)) * mask
        return 0

    lax.fori_loop(0, SLOTS * SIDE, activate, 0, unroll=4)
    fill_bands(hp, nbr)

    def conv_top(t, _):
        lhs = jnp.concatenate([hp[t, 64 * a : 64 * a + CELLS, :] for a in range(3)], axis=1)
        y = jnp.dot(lhs, wtop[...], preferred_element_type=F32)
        for i in range(SIDE):
            r = t * SIDE + i
            rows = slice(i * SIDE, i * SIDE + SIDE)
            ya[pl.ds(pl.multiple_of(r * FULL + 8, 8), SIDE), :] = y[rows, 0:128]
            yb[pl.ds(pl.multiple_of(r * SIDE, 8), SIDE), :] = y[rows, 128:256]
        return 0

    lax.fori_loop(0, SLOTS, conv_top, 0)

    for copy in hidden_copies:
        copy.wait()
    margin_strips(hrecv.at[0], nbr, 0, 3, 5, work, sh_w, 128)
    margin_strips(hrecv.at[1], nbr, 2, 4, 7, work, sh_e, 128)
    west = jnp.dot(sh_w[...], wtop[:, 0:128], preferred_element_type=F32)
    east = jnp.dot(sh_e[...], wtop[:, 0:128], preferred_element_type=F32)
    for t in range(SLOTS):
        for col in range(2):
            rows = slice((t * 2 + col) * 32, (t * 2 + col) * 32 + 32)
            ya[pl.ds(t * SIDE * FULL + 6 + col, SIDE, stride=FULL), :] = west[rows]
            ya[pl.ds(t * SIDE * FULL + 40 + col, SIDE, stride=FULL), :] = east[rows]

    zero_rows = jnp.zeros((SIDE, 128), F32)

    def up_pair(t, pair, mask):
        cell = 2 * pair
        base = t * SIDE * FULL
        before = [ya[pl.ds(base + 6 + cell + k, SIDE, stride=FULL), :] for k in range(2)]
        after = [ya[pl.ds(base + 10 + cell + k, SIDE, stride=FULL), :] for k in range(2)]
        centre = [yb[pl.ds(t * CELLS + cell + k, SIDE, stride=SIDE), :] for k in range(2)]
        pre = jnp.where(low, before[0], after[1])
        pre = pre + pltpu.roll(jnp.where(low, before[1], after[0]), 64, 1)
        pre = pre + jnp.where(low, centre[0], centre[1]) + btop_twice
        gate = sigmoid(pre)
        value = pre * gate
        lanes = pl.ds(pair * 128, 128)
        if not isinstance(pair, int):
            lanes = pl.ds(pl.multiple_of(pair * 128, 128), 128)
        out[t, :, lanes] = (value * mask).astype(BF16)
        up = cotv[t, :, lanes].astype(F32) * (gate + value * (1.0 - gate)) * mask
        up = up.astype(BF16).astype(F32)
        turned = pltpu.roll(up, 64, 1)
        uf[pl.ds(base + 8 + cell, SIDE, stride=FULL), :] = jnp.where(low, up, turned)
        uf[pl.ds(base + 9 + cell, SIDE, stride=FULL), :] = jnp.where(low, turned, up)
        return up, turned

    def tile_sum(up):
        return jnp.sum(up.reshape(4, 8, 128), axis=0)

    bias_top = jnp.zeros((8, 128), F32)
    for t in range(SLOTS):
        for side, edge in enumerate((ucol_w, ucol_e)):
            up, turned = up_pair(t, 15 * side, alive[t])
            usend[side, t] = up.astype(BF16)
            for col, rows in enumerate((up, turned)):
                at = (t * 2 + col) * 32
                edge[at : at + 32, :] = jnp.where(low, rows, zero_rows).astype(BF16)
            bias_top = bias_top + tile_sum(up)
    upstream_copies = exchange(usend, urecv, 4)

    def top_pairs(r, total):
        t, pair = r // 14, lax.rem(r, 14) + 1
        mask = jnp.where(t < live[0], 1.0, 0.0).astype(F32)
        up, _ = up_pair(t, pair, mask)
        return total + tile_sum(up)

    bias_top = lax.fori_loop(0, SLOTS * 14, top_pairs, bias_top, unroll=7)

    def shift_up(g, _):
        at = pl.ds(pl.multiple_of(g * 128, 128), 128)
        t, quarter = g // 8, lax.rem(g, 8)

        def cells(first):
            return jnp.concatenate(
                [uf[pl.ds((g * 4 + k) * FULL + first, SIDE), :] for k in range(4)], axis=0)

        left_half = low_lanes((128, 128))
        zero = jnp.zeros((128, 128), F32)
        same = cells(8)
        rows = pl.ds(pl.multiple_of(64 + quarter * 128, 16), 128)
        uplo[t, rows, :] = jnp.where(left_half, same, zero).astype(BF16)
        uphi[t, rows, :] = jnp.where(left_half, zero, same).astype(BF16)
        uut[0:128, at] = jnp.where(left_half, cells(10), same).astype(BF16).T
        uut[128:192, at] = cells(6).astype(BF16).T[0:64]
        return 0

    lax.fori_loop(0, SLOTS * SIDE // 4, shift_up, 0, unroll=4)
    fill_bands(uplo, nbr)
    fill_bands(uphi, nbr)

    zero_cols = jnp.zeros((256, 128), BF16)
    edges_l = jnp.concatenate([
        jnp.concatenate([ucol_w[...], zero_cols], axis=1),
        jnp.concatenate([zero_cols, ucol_e[...]], axis=1)], axis=0)
    edges_r = jnp.concatenate([sh_w[...], sh_e[...]], axis=0)
    across = (((0,), (0,)), ((), ()))
    edges = lax.dot_general(edges_l, edges_r, across, preferred_element_type=F32)
    acc_top[...] = edges[0:192]

    def grad_top(t, _):
        rhs = jnp.concatenate([hp[t, 64 * a : 64 * a + CELLS, :] for a in range(3)], axis=1)
        lhs = uut[:, pl.ds(pl.multiple_of(t * CELLS, 128), CELLS)]
        acc_top[...] += jnp.dot(lhs, rhs, preferred_element_type=F32)
        return 0

    lax.fori_loop(0, SLOTS, grad_top, 0)

    def conv_back(t, _):
        first = uplo[t, 0:CELLS, :] + uphi[t, 64 : 64 + CELLS, :]
        lhs = jnp.concatenate([first, uplo[t, 128 : 128 + CELLS, :]], axis=1)
        y = jnp.dot(lhs, wback[...], preferred_element_type=F32)
        for i in range(SIDE):
            r = t * SIDE + i
            rows = slice(i * SIDE, i * SIDE + SIDE)
            y0[pl.ds(pl.multiple_of(r * WIDE + 8, 8), SIDE), :] = y[rows, 0:128]
            y1[pl.ds(pl.multiple_of(r * SIDE, 8), SIDE), :] = y[rows, 128:256]
            y2[pl.ds(pl.multiple_of(r * WIDE, 8), SIDE), :] = y[rows, 256:384]
        return 0

    lax.fori_loop(0, SLOTS, conv_back, 0)

    for copy in upstream_copies:
        copy.wait()
    for received, up, side, down, dest in (
        (urecv.at[0], 0, 3, 5, su_w), (urecv.at[1], 2, 4, 7, su_e)):
        def strip_of(index):
            return received[jnp.maximum(index, 0)].astype(F32) * present(index)

        for t in range(SLOTS):
            base = t * FULL
            work[base : base + 8, :] = strip_of(nbr[t, up])[24:32]
            work[base + 8 : base + 40, :] = strip_of(nbr[t, side])
            work[base + 40 : base + 48, :] = strip_of(nbr[t, down])[0:8]
        for t in range(SLOTS):
            v = [work[t * FULL + 6 + 2 * a : t * FULL + 38 + 2 * a, :] for a in range(3)]
            w = [pltpu.roll(x, 64, 1) for x in v]
            at = t * 64
            dest[at : at + 32, 0:128] = jnp.where(low, v[0], w[1]).astype(BF16)
            dest[at : at + 32, 128:256] = jnp.where(low, v[2], zero_rows).astype(BF16)
            dest[at + 32 : at + 64, 0:128] = jnp.where(low, w[0], v[1]).astype(BF16)
            dest[at + 32 : at + 64, 128:256] = jnp.where(low, w[2], zero_rows).astype(BF16)
    add_margins(
        jnp.dot(su_w[...], wback[:, 0:128], preferred_element_type=F32),
        jnp.dot(su_e[...], wback[:, 256:384], preferred_element_type=F32))

    def slopes(r, total):
        back = mid_rows(r) * slope[pl.ds(pl.multiple_of(r * SIDE, 8), SIDE), :]
        back = back.astype(BF16).astype(F32)
        sf[pl.ds(pl.multiple_of(r * FULL + 8, 8), SIDE), :] = back
        return total + jnp.sum(back.reshape(4, 8, 128), axis=0)

    bias_mid = lax.fori_loop(0, SLOTS * SIDE, slopes, jnp.zeros((8, 128), F32), unroll=4)

    def shift_slope(g, _):
        at = pl.ds(pl.multiple_of(g * 128, 128), 128)
        for b, first in enumerate((10, 8, 6)):
            rows = [sf[pl.ds((g * 4 + k) * FULL + first, SIDE), :] for k in range(4)]
            block = jnp.concatenate(rows, axis=0).astype(BF16)
            sst[b * 128 : b * 128 + 128, at] = block.T
        return 0

    lax.fori_loop(0, SLOTS * SIDE // 4, shift_slope, 0, unroll=4)
    for t in range(SLOTS):
        for side, col, cell in columns:
            edge = scol_w if side == 0 else scol_e
            at = (t * 2 + col) * 32
            edge[at : at + 32, :] = sf[
                pl.ds(t * SIDE * FULL + 8 + cell, SIDE, stride=FULL), :].astype(BF16)

    def reducer(chunk, order):
        base = chunk * 1024
        first, second, third = order
        shard = place[first] * 4 + place[second]
        other = on_chip(place, 1 - core)
        pending, started = [], []

        def send(at, src, dst, device):
            copy = pltpu.make_async_remote_copy(
                src_ref=src, dst_ref=dst, send_sem=sum_send.at[chunk, at],
                recv_sem=sum_recv.at[chunk, at], device_id=device, device_id_type=MESH)
            copy.start()
            pending.append(copy)
            started.append(copy)

        def arrive():
            for copy in pending:
                copy.wait_recv()
            pending.clear()

        def rows_at(index, size, offset=0):
            return pl.ds(pl.multiple_of(offset + index * size, 16), size)

        def split_core():
            sum_core[chunk] = grad[base : base + 1024, :].astype(BF16)
            send(0, sum_core.at[chunk, rows_at(1 - core, 512)], core_in.at[chunk], other)

        def split_plane():
            arrive()
            mine = grad[rows_at(core, 512, base), :]
            plane_out[chunk] = (mine + core_in[chunk].astype(F32)).astype(BF16)
            for k, (d, e) in enumerate(corners):
                there = moved(((first, d), (second, e)))
                to = there[first] * 4 + there[second]
                send(1 + k, plane_out.at[chunk, rows_at(to, 32)], plane_in.at[chunk, k],
                     on_chip(there, core))

        def swap_line():
            arrive()
            value = plane_out[chunk, rows_at(shard, 32), :].astype(F32)
            for k in range(15):
                value = value + plane_in[chunk, k].astype(F32)
            mine = place[third]
            line_in[chunk, mine] = value
            for d in (1, 2, 3):
                send(15 + d, line_in.at[chunk, mine], line_in.at[chunk, mine],
                     on_chip(moved(((third, d),)), core))

        def back_plane():
            arrive()
            value = line_in[chunk, 0] + line_in[chunk, 1]
            value = value + (line_in[chunk, 2] + line_in[chunk, 3])
            mine = rows_at(core * 16 + shard, 32, base)
            total[mine, :] = value.astype(BF16)
            for k, (d, e) in enumerate(corners):
                send(19 + k, total.at[mine], total.at[mine],
                     on_chip(moved(((first, d), (second, e))), core))

        def back_core():
            arrive()
            half = rows_at(core, 512, base)
            send(34, total.at[half], total.at[half], other)

        def finish():
            arrive()
            for copy in started:
                copy.wait_send()

        return iter((split_core, split_plane, swap_line, back_plane, back_core, finish))

    reducers = [reducer(chunk, order) for chunk, order in enumerate(orders)]

    def advance(*chunks):
        for chunk in chunks:
            step = next(reducers[chunk], None)
            if step is not None:
                step()

    for a in range(3):
        for b in range(3):
            at = (a * 3 + b) * 64
            grad[at : at + 64, :] = acc_top[b * 64 : b * 64 + 64, a * 128 : a * 128 + 128]
    grad[576:584, :] = bias_mid
    grad[584:592, :] = bias_top
    grad[592:768, :] = jnp.zeros((176, 128), F32)

    for a in range(3):
        q = slice(a * 256, a * 256 + 256)
        acc_mid[0:128, :] = lax.dot_general(
            scol_w[...], sa_w[:, q], across, preferred_element_type=F32)
        acc_mid[128:256, :] = jnp.zeros((128, 256), F32)
        acc_mid[256:384, :] = lax.dot_general(
            scol_e[...], sa_e[:, q], across, preferred_element_type=F32)

        def grad_mid(t, _):
            acc_mid[...] += jnp.dot(
                sst[:, pl.ds(pl.multiple_of(t * CELLS, 128), CELLS)],
                fp[t, 64 * a : 64 * a + CELLS, :], preferred_element_type=F32)
            return 0

        lax.fori_loop(0, SLOTS, grad_mid, 0)
        for b in range(3):
            at = 768 + (a * 3 + b) * 256
            grad[at : at + 256, :] = acc_mid[b * 128 : b * 128 + 128, :].T
        advance(*((0,), (1, 0), (2, 1, 2))[a])
    for _ in range(4):
        advance(0, 1, 2)

    sums[...] = total[...]


def finish_kernel(sums, out_in, gmid, gtop, bmid, btop, out, mid_half, mid_full, top_half, out_held, sem):
    whole = pltpu.make_async_copy(out_in, out_held, sem.at[0])
    top = pltpu.make_async_copy(sums.at[pl.ds(0, 592)], top_half, sem.at[1])
    mid = pltpu.make_async_copy(sums.at[pl.ds(768, 2304)], mid_half, sem.at[2])
    mid.start()
    whole.start()
    top.start()
    mid.wait()
    mid_full[...] = mid_half[...].astype(F32)
    mid_back = pltpu.make_async_copy(mid_full, gmid, sem.at[3])
    mid_back.start()
    whole.wait()
    whole_back = pltpu.make_async_copy(out_held, out, sem.at[4])
    whole_back.start()
    top.wait()
    gtop[...] = top_half[0:576, :].astype(F32)
    tail = top_half[576:592, :].astype(F32)
    bmid[...] = jnp.sum(tail[0:8], axis=0, keepdims=True)
    twice = jnp.sum(tail[8:16], axis=0, keepdims=True)
    btop[...] = twice[:, 0:64] + twice[:, 64:128]
    mid_back.wait()
    whole_back.wait()


def shards(features, cotangent, neighbors, live_count, kernel_mid, bias_mid, kernel_top, bias_top):
    slots, side, _, channels = features.shape
    vmem = pl.BlockSpec(memory_space=pltpu.VMEM)
    smem = pl.BlockSpec(memory_space=pltpu.SMEM)
    hbm = pl.BlockSpec(memory_space=pl.ANY)
    rows = SLOTS * SIDE
    out, sums = pl.pallas_call(
        kernel,
        out_shape=(
            jax.ShapeDtypeStruct((SLOTS, SIDE, 2048), BF16),
            jax.ShapeDtypeStruct((3072, 128), BF16),
        ),
        in_specs=[hbm, hbm, smem, smem, hbm, vmem, vmem, vmem],
        out_specs=(vmem, vmem),
        scratch_shapes=[
            pltpu.VMEM((SLOTS, PADDED, 256), BF16),
            pltpu.VMEM((SLOTS, PADDED, 128), BF16),
            pltpu.VMEM((768, 384), BF16),
            pltpu.VMEM((384, 256), BF16),
            pltpu.VMEM((256, 384), BF16),
            pltpu.VMEM((rows * WIDE, 128), F32),
            pltpu.VMEM((rows * SIDE, 128), F32),
            pltpu.VMEM((rows * WIDE, 128), F32),
            pltpu.VMEM((rows * FULL, 128), F32),
            pltpu.VMEM((rows * SIDE, 128), F32),
            pltpu.VMEM((8 * FULL, 128), F32),
            pltpu.VMEM((256, 768), BF16),
            pltpu.VMEM((256, 768), BF16),
            pltpu.VMEM((256, 384), BF16),
            pltpu.VMEM((256, 384), BF16),
            pltpu.VMEM((256, 256), BF16),
            pltpu.VMEM((256, 256), BF16),
            pltpu.VMEM((rows * 8, 128), F32),
            pltpu.VMEM((rows * 8, 128), F32),
            pltpu.VMEM((2, 8, 32, 256), BF16),
            pltpu.VMEM((2, 8, 32, 256), BF16),
            pltpu.VMEM((2, 8, 32, 128), BF16),
            pltpu.VMEM((2, 8, 32, 128), BF16),
            pltpu.VMEM((2, 4, 32, 128), BF16),
            pltpu.VMEM((2, 4, 32, 128), BF16),
            pltpu.VMEM((rows * SIDE, 128), F32),
            pltpu.VMEM((rows * FULL, 128), F32),
            pltpu.VMEM((SLOTS, PADDED, 128), BF16),
            pltpu.VMEM((SLOTS, PADDED, 128), BF16),
            pltpu.VMEM((192, rows * SIDE), BF16),
            pltpu.VMEM((256, 128), BF16),
            pltpu.VMEM((256, 128), BF16),
            pltpu.VMEM((256, 128), BF16),
            pltpu.VMEM((256, 128), BF16),
            pltpu.VMEM((rows * FULL, 128), F32),
            pltpu.VMEM((384, rows * SIDE), BF16),
            pltpu.VMEM((384, 256), F32),
            pltpu.VMEM((192, 384), F32),
            pltpu.VMEM((SLOTS, SIDE, 2048), BF16),
            pltpu.VMEM((3072, 128), F32),
            pltpu.VMEM((3, 1024, 128), BF16),
            pltpu.VMEM((3, 512, 128), BF16),
            pltpu.VMEM((3, 512, 128), BF16),
            pltpu.VMEM((3, 15, 32, 128), BF16),
            pltpu.VMEM((3, 4, 32, 128), F32),
            pltpu.VMEM((3072, 128), BF16),
            pltpu.SemaphoreType.DMA((14,)),
            pltpu.SemaphoreType.DMA((6,)),
            pltpu.SemaphoreType.DMA((6,)),
            pltpu.SemaphoreType.DMA((3, 35)),
            pltpu.SemaphoreType.DMA((3, 35)),
        ],
        compiler_params=pltpu.CompilerParams(
            collective_id=0, has_side_effects=True, vmem_limit_bytes=60 * 2**20),
        name="backend_layers",
    )(
        features.reshape(slots, side * side, channels), cotangent, neighbors, live_count,
        kernel_mid, bias_mid.reshape(1, 128), jnp.swapaxes(kernel_top, 2, 3),
        bias_top.reshape(1, 64),
    )
    grad_mid, grad_top, bias_mid_sum, bias_top_sum, out = pl.pallas_call(
        finish_kernel,
        out_shape=(
            jax.ShapeDtypeStruct((2304, 128), F32),
            jax.ShapeDtypeStruct((576, 128), F32),
            jax.ShapeDtypeStruct((1, 128), F32),
            jax.ShapeDtypeStruct((1, 64), F32),
            jax.ShapeDtypeStruct((SLOTS, SIDE, 2048), BF16),
        ),
        in_specs=[hbm, hbm],
        out_specs=(hbm, vmem, vmem, vmem, hbm),
        scratch_shapes=[
            pltpu.VMEM((2304, 128), BF16),
            pltpu.VMEM((2304, 128), F32),
            pltpu.VMEM((592, 128), BF16),
            pltpu.VMEM((SLOTS, SIDE, 2048), BF16),
            pltpu.SemaphoreType.DMA((5,)),
        ],
        compiler_params=pltpu.CompilerParams(vmem_limit_bytes=60 * 2**20),
        name="finish",
    )(sums, out)
    grad_mid = grad_mid.reshape(3, 3, 256, 128)
    grad_top = jnp.swapaxes(grad_top.reshape(3, 3, 64, 128), 2, 3)
    return out, grad_mid, bias_mid_sum.reshape(128), grad_top, bias_top_sum.reshape(64)


def solution(mesh):
    in_specs = (
        P(("rep", "tile"), None, None, None),
        P(("rep", "tile"), None, None),
        P(("rep", "tile"), None),
        P(("rep", "tile")),
        P(),
        P(),
        P(),
        P(),
    )
    out_specs = (P(("rep", "tile"), None, None), P(), P(), P(), P())
    return jax.shard_map(shards, mesh=mesh, in_specs=in_specs, out_specs=out_specs, check_vma=False)
```

```python
import functools

import jax
import jax.numpy as jnp
from jax import lax
from jax.experimental import pallas as pl
from jax.experimental.pallas import tpu as pltpu
from jax.sharding import PartitionSpec as P

F32 = jnp.float32
BF16 = jnp.bfloat16
MESH = pl.DeviceIdType.MESH

SLOTS = 4
SIDE = 32
CELLS = SIDE * SIDE
PADDED = CELLS + 128
FULL = 48
ODD_FULL = 49
ODD_WIDE = 41
ODD_SIDE = 33


def sigmoid(v):
    return 0.5 * jnp.tanh(0.5 * v) + 0.5


def low_lanes(shape):
    return lax.broadcasted_iota(jnp.int32, shape, len(shape) - 1) < 64


def present(index):
    return jnp.where(index >= 0, 1.0, 0.0).astype(F32)


def fill_bands(padded, nbr):
    for t in range(SLOTS):
        north, south = nbr[t, 1], nbr[t, 6]
        band = padded[jnp.maximum(north, 0), CELLS : CELLS + 64, :].astype(F32)
        padded[t, 0:64, :] = (band * present(north)).astype(BF16)
        band = padded[jnp.maximum(south, 0), 64:128, :].astype(F32)
        padded[t, CELLS + 64 : PADDED, :] = (band * present(south)).astype(BF16)


def strip_block(received, index, col, lanes):
    return received[jnp.maximum(index, 0) * 2 + col, :, lanes].astype(F32) * present(index)


def margin_strips(received, nbr, corner_up, side, corner_down, work, shifted, channels):
    for lane_tile in range(channels // 128):
        lanes = slice(lane_tile * 128, lane_tile * 128 + 128)
        for t in range(SLOTS):
            for col in range(2):
                base = (t * 2 + col) * FULL
                up = strip_block(received, nbr[t, corner_up], col, lanes)
                mid = strip_block(received, nbr[t, side], col, lanes)
                down = strip_block(received, nbr[t, corner_down], col, lanes)
                work[base : base + 8, :] = up[24:32]
                work[base + 8 : base + 40, :] = mid
                work[base + 40 : base + 48, :] = down[0:8]
        for block in range(SLOTS * 2):
            for a in range(3):
                rows = work[block * FULL + 6 + 2 * a : block * FULL + 38 + 2 * a, :]
                at = a * channels + lane_tile * 128
                shifted[block * 32 : block * 32 + 32, at : at + 128] = rows.astype(BF16)


def kernel(
    feat, cot, nbr, live, kmid, bmid, ktop, btop,
    out, sums,
    fp, hp, wmid, wtop, wback, y0, y1, y2, ya, yb, work, sa_w, sa_e, sh_w, sh_e, su_w, su_e,
    strip_a, strip_b, fsend, frecv, hsend, hrecv, usend, urecv,
    slope, uf, uplo, uphi, uut, ucol_w, ucol_e, scol_w, scol_e, sf,
    sst, acc_top, cotv, outv, grad, core_in, plane_out, plane_in, line_in, total,
    local_sem, send_sem, recv_sem, sum_send, sum_recv,
):
    n = lax.axis_size("tile")
    me = lax.axis_index("tile")
    right, left = lax.rem(me + 1, n), lax.rem(me + n - 1, n)
    z, y, x, core = lax.axis_index("rep"), me // 8, lax.rem(me // 2, 4), lax.rem(me, 2)
    place = {"x": x, "y": y, "z": z}

    def on_chip(where, c):
        return {"rep": where["z"], "tile": where["y"] * 8 + where["x"] * 2 + c}

    def moved(steps):
        there = dict(place)
        for axis, distance in steps:
            there[axis] = lax.rem(place[axis] + distance, 4)
        return there

    corners = [(d, e) for d in range(4) for e in range(4) if d or e]
    orders = ("xyz", "yzx", "zxy")

    loads = []
    for t in range(SLOTS):
        loads.append(pltpu.make_async_copy(
            feat.at[t], fp.at[t, pl.ds(64, CELLS)], local_sem.at[t]))
    for a in range(3):
        for b in range(3):
            loads.append(pltpu.make_async_copy(
                kmid.at[a, b],
                wmid.at[pl.ds(a * 256, 256), pl.ds(b * 128, 128)],
                local_sem.at[4 + a * 3 + b]))
    loads.append(pltpu.make_async_copy(cot, cotv, local_sem.at[13]))
    for copy in loads:
        copy.start()

    barrier = pltpu.get_barrier_semaphore()
    for neighbour in (left, right):
        pl.semaphore_signal(barrier, inc=1, device_id={"tile": neighbour}, device_id_type=MESH)
    pl.semaphore_signal(barrier, inc=1, device_id=on_chip(place, 1 - core), device_id_type=MESH)
    for first, second, _ in orders:
        for d, e in corners:
            if d:
                pl.semaphore_signal(
                    barrier, inc=1, device_id=on_chip(moved(((first, d), (second, e))), core),
                    device_id_type=MESH)

    for copy in loads[:SLOTS]:
        copy.wait()

    for side, (cells, picks) in enumerate(((0, (0, 1)), (16, (6, 7)))):
        def gather(r, _):
            t, i = r // SIDE, r % SIDE
            rows = fp[t, pl.ds(pl.multiple_of(64 + i * SIDE + cells, 16), 16), :].astype(F32)
            rows = rows[0:8] if cells == 0 else rows[8:16]
            at = r * 9
            strip_a[pl.ds(at, 8), :] = rows[:, 0:128]
            strip_b[pl.ds(at, 8), :] = rows[:, 128:256]
            return 0

        lax.fori_loop(0, SLOTS * SIDE, gather, 0, unroll=16)
        for t in range(SLOTS):
            for col, pick in enumerate(picks):
                at = pl.ds(t * 288 + pick, 32, stride=9)
                fsend[side, t * 2 + col, :, 0:128] = strip_a[at, :].astype(BF16)
                fsend[side, t * 2 + col, :, 128:256] = strip_b[at, :].astype(BF16)

    pl.semaphore_wait(barrier, 39)

    def exchange(send, recv, at):
        copies = []
        for side, target in ((0, left), (1, right)):
            copies.append(pltpu.make_async_remote_copy(
                src_ref=send.at[side], dst_ref=recv.at[1 - side],
                send_sem=send_sem.at[at + side], recv_sem=recv_sem.at[at + 1 - side],
                device_id={"tile": target}, device_id_type=MESH))
        for copy in copies:
            copy.start()
        return copies

    feature_copies = exchange(fsend, frecv, 0)

    zero8 = jnp.zeros((8, 128), F32)

    def clear(r, _):
        uf[pl.ds(r * ODD_FULL, 8), :] = zero8
        uf[pl.ds(r * ODD_FULL + 40, 8), :] = zero8
        sf[pl.ds(r * ODD_FULL, 8), :] = zero8
        sf[pl.ds(r * ODD_FULL + 40, 8), :] = zero8
        return 0

    lax.fori_loop(0, SLOTS * SIDE, clear, 0, unroll=8)

    for a in range(3):
        outer = jnp.concatenate([ktop[a, 0], ktop[a, 2]], axis=0).astype(F32).T
        centre = jnp.concatenate([ktop[a, 1], ktop[a, 1]], axis=0).astype(F32).T
        wtop[a * 128 : a * 128 + 128, 0:128] = outer.astype(BF16)
        wtop[a * 128 : a * 128 + 128, 128:256] = centre.astype(BF16)
        for b in range(3):
            wback[a * 64 : a * 64 + 64, b * 128 : b * 128 + 128] = ktop[2 - a, 2 - b]
    wback[192:256, :] = jnp.zeros((64, 384), BF16)
    btop_twice = jnp.concatenate([btop[...], btop[...]], axis=1)

    fill_bands(fp, nbr)
    for copy in loads[SLOTS:]:
        copy.wait()

    def conv_mid(t, _):
        lhs = jnp.concatenate([fp[t, 64 * a : 64 * a + CELLS, :] for a in range(3)], axis=1)
        y = jnp.dot(lhs, wmid[...], preferred_element_type=F32)
        for i in range(SIDE):
            r = t * SIDE + i
            rows = slice(i * SIDE, i * SIDE + SIDE)
            y0[pl.ds(r * ODD_WIDE + 8, SIDE), :] = y[rows, 0:128]
            y1[pl.ds(r * ODD_SIDE, SIDE), :] = y[rows, 128:256]
            y2[pl.ds(r * ODD_WIDE, SIDE), :] = y[rows, 256:384]
        return 0

    lax.fori_loop(0, SLOTS, conv_mid, 0)

    low = low_lanes((SIDE, 128))
    for copy in feature_copies:
        copy.wait()
    margin_strips(frecv.at[0], nbr, 0, 3, 5, work, sa_w, 256)
    margin_strips(frecv.at[1], nbr, 2, 4, 7, work, sa_e, 256)

    def add_margins(west, east):
        for t in range(SLOTS):
            for col in range(2):
                rows = slice((t * 2 + col) * 32, (t * 2 + col) * 32 + 32)
                y0[pl.ds(t * SIDE * ODD_WIDE + 6 + col, SIDE, stride=ODD_WIDE), :] = west[rows]
                y2[pl.ds(t * SIDE * ODD_WIDE + 32 + col, SIDE, stride=ODD_WIDE), :] = east[rows]

    add_margins(
        jnp.dot(sa_w[...], wmid[:, 0:128], preferred_element_type=F32),
        jnp.dot(sa_e[...], wmid[:, 256:384], preferred_element_type=F32))

    alive = [jnp.where(t < live[0], 1.0, 0.0).astype(F32) for t in range(SLOTS)]
    columns = ((0, 0, 0), (0, 1, 1), (1, 0, 30), (1, 1, 31))

    def mid_at(t, cell):
        first = y0[pl.ds(t * SIDE * ODD_WIDE + 6 + cell, SIDE, stride=ODD_WIDE), :]
        second = y1[pl.ds(t * SIDE * ODD_SIDE + cell, SIDE, stride=ODD_SIDE), :]
        third = y2[pl.ds(t * SIDE * ODD_WIDE + 2 + cell, SIDE, stride=ODD_WIDE), :]
        return first + second + third

    for t in range(SLOTS):
        for side, col, cell in columns:
            pre = mid_at(t, cell) + bmid[...]
            hsend[side, t * 2 + col, :, :] = (pre * sigmoid(pre) * alive[t]).astype(BF16)
    hidden_copies = exchange(hsend, hrecv, 2)

    def mid_rows(r):
        first = y0[pl.ds(r * ODD_WIDE + 6, SIDE), :]
        second = y1[pl.ds(r * ODD_SIDE, SIDE), :]
        third = y2[pl.ds(r * ODD_WIDE + 2, SIDE), :]
        return first + second + third

    def activate(r, _):
        t, i = r // SIDE, r % SIDE
        mask = jnp.where(t < live[0], 1.0, 0.0).astype(F32)
        pre = mid_rows(r) + bmid[...]
        gate = sigmoid(pre)
        hidden = pre * gate
        hp[t, pl.ds(pl.multiple_of(64 + i * SIDE, 16), SIDE), :] = (hidden * mask).astype(BF16)
        slope[pl.ds(pl.multiple_of(r * SIDE, 8), SIDE), :] = (gate + hidden * (1.0 - gate)) * mask
        return 0

    lax.fori_loop(0, SLOTS * SIDE, activate, 0, unroll=4)
    fill_bands(hp, nbr)

    def conv_top(t, _):
        lhs = jnp.concatenate([hp[t, 64 * a : 64 * a + CELLS, :] for a in range(3)], axis=1)
        y = jnp.dot(lhs, wtop[...], preferred_element_type=F32)
        for i in range(SIDE):
            r = t * SIDE + i
            rows = slice(i * SIDE, i * SIDE + SIDE)
            ya[pl.ds(r * ODD_FULL + 8, SIDE), :] = y[rows, 0:128]
            yb[pl.ds(r * ODD_SIDE, SIDE), :] = y[rows, 128:256]
        return 0

    lax.fori_loop(0, SLOTS, conv_top, 0)

    for copy in hidden_copies:
        copy.wait()
    margin_strips(hrecv.at[0], nbr, 0, 3, 5, work, sh_w, 128)
    margin_strips(hrecv.at[1], nbr, 2, 4, 7, work, sh_e, 128)
    west = jnp.dot(sh_w[...], wtop[:, 0:128], preferred_element_type=F32)
    east = jnp.dot(sh_e[...], wtop[:, 0:128], preferred_element_type=F32)
    for t in range(SLOTS):
        for col in range(2):
            rows = slice((t * 2 + col) * 32, (t * 2 + col) * 32 + 32)
            ya[pl.ds(t * SIDE * ODD_FULL + 6 + col, SIDE, stride=ODD_FULL), :] = west[rows]
            ya[pl.ds(t * SIDE * ODD_FULL + 40 + col, SIDE, stride=ODD_FULL), :] = east[rows]

    zero_rows = jnp.zeros((SIDE, 128), F32)

    def up_pair(t, pair, mask):
        cell = 2 * pair
        base = t * SIDE * ODD_FULL
        before = [ya[pl.ds(base + 6 + cell + k, SIDE, stride=ODD_FULL), :] for k in range(2)]
        after = [ya[pl.ds(base + 10 + cell + k, SIDE, stride=ODD_FULL), :] for k in range(2)]
        centre = [yb[pl.ds(t * SIDE * ODD_SIDE + cell + k, SIDE, stride=ODD_SIDE), :] for k in range(2)]
        pre = jnp.where(low, before[0], after[1])
        pre = pre + pltpu.roll(jnp.where(low, before[1], after[0]), 64, 1)
        pre = pre + jnp.where(low, centre[0], centre[1]) + btop_twice
        gate = sigmoid(pre)
        value = pre * gate
        lanes = pl.ds(pair * 128, 128)
        if not isinstance(pair, int):
            lanes = pl.ds(pl.multiple_of(pair * 128, 128), 128)
        outv[t, :, lanes] = (value * mask).astype(BF16)
        up = cotv[t, :, lanes].astype(F32) * (gate + value * (1.0 - gate)) * mask
        up = up.astype(BF16).astype(F32)
        turned = pltpu.roll(up, 64, 1)
        uf[pl.ds(base + 8 + cell, SIDE, stride=ODD_FULL), :] = jnp.where(low, up, turned)
        uf[pl.ds(base + 9 + cell, SIDE, stride=ODD_FULL), :] = jnp.where(low, turned, up)
        return up, turned

    def tile_sum(up):
        return jnp.sum(up.reshape(4, 8, 128), axis=0)

    bias_top = jnp.zeros((8, 128), F32)
    for t in range(SLOTS):
        for side, edge in enumerate((ucol_w, ucol_e)):
            up, turned = up_pair(t, 15 * side, alive[t])
            usend[side, t] = up.astype(BF16)
            for col, rows in enumerate((up, turned)):
                at = (t * 2 + col) * 32
                edge[at : at + 32, :] = jnp.where(low, rows, zero_rows).astype(BF16)
            bias_top = bias_top + tile_sum(up)
    upstream_copies = exchange(usend, urecv, 4)

    def top_pairs(r, total):
        t, pair = r // 14, lax.rem(r, 14) + 1
        mask = jnp.where(t < live[0], 1.0, 0.0).astype(F32)
        up, _ = up_pair(t, pair, mask)
        return total + tile_sum(up)

    bias_top = lax.fori_loop(0, SLOTS * 14, top_pairs, bias_top, unroll=7)
    out_copy = pltpu.make_async_copy(outv, out, local_sem.at[14])
    out_copy.start()

    def shift_up(g, _):
        at = pl.ds(pl.multiple_of(g * 128, 128), 128)
        t, quarter = g // 8, lax.rem(g, 8)

        def cells(first):
            return jnp.concatenate(
                [uf[pl.ds((g * 4 + k) * ODD_FULL + first, SIDE), :] for k in range(4)], axis=0)

        left_half = low_lanes((128, 128))
        zero = jnp.zeros((128, 128), F32)
        same = cells(8)
        rows = pl.ds(pl.multiple_of(64 + quarter * 128, 16), 128)
        uplo[t, rows, :] = jnp.where(left_half, same, zero).astype(BF16)
        uphi[t, rows, :] = jnp.where(left_half, zero, same).astype(BF16)
        uut[0:128, at] = jnp.where(left_half, cells(10), same).astype(BF16).T
        uut[128:192, at] = cells(6).astype(BF16).T[0:64]
        return 0

    lax.fori_loop(0, SLOTS * SIDE // 4, shift_up, 0, unroll=4)
    fill_bands(uplo, nbr)
    fill_bands(uphi, nbr)

    zero_cols = jnp.zeros((256, 128), BF16)
    edges_l = jnp.concatenate([
        jnp.concatenate([ucol_w[...], zero_cols], axis=1),
        jnp.concatenate([zero_cols, ucol_e[...]], axis=1)], axis=0)
    edges_r = jnp.concatenate([sh_w[...], sh_e[...]], axis=0)
    across = (((0,), (0,)), ((), ()))
    edges = lax.dot_general(edges_l, edges_r, across, preferred_element_type=F32)
    acc_top[...] = edges[0:192]

    def grad_top(t):
        rhs = jnp.concatenate([hp[t, 64 * a : 64 * a + CELLS, :] for a in range(3)], axis=1)
        lhs = uut[:, pl.ds(pl.multiple_of(t * CELLS, 128), CELLS)]
        acc_top[...] += jnp.dot(lhs, rhs, preferred_element_type=F32)

    def conv_back(t, _):
        first = uplo[t, 0:CELLS, :] + uphi[t, 64 : 64 + CELLS, :]
        lhs = jnp.concatenate([first, uplo[t, 128 : 128 + CELLS, :]], axis=1)
        y = jnp.dot(lhs, wback[...], preferred_element_type=F32)
        for i in range(SIDE):
            r = t * SIDE + i
            rows = slice(i * SIDE, i * SIDE + SIDE)
            y0[pl.ds(r * ODD_WIDE + 8, SIDE), :] = y[rows, 0:128]
            y1[pl.ds(r * ODD_SIDE, SIDE), :] = y[rows, 128:256]
            y2[pl.ds(r * ODD_WIDE, SIDE), :] = y[rows, 256:384]
        return 0

    lax.fori_loop(0, SLOTS, conv_back, 0)

    for copy in upstream_copies:
        copy.wait()
    for received, up, side, down, dest in (
        (urecv.at[0], 0, 3, 5, su_w), (urecv.at[1], 2, 4, 7, su_e)):
        def strip_of(index):
            return received[jnp.maximum(index, 0)].astype(F32) * present(index)

        for t in range(SLOTS):
            base = t * FULL
            work[base : base + 8, :] = strip_of(nbr[t, up])[24:32]
            work[base + 8 : base + 40, :] = strip_of(nbr[t, side])
            work[base + 40 : base + 48, :] = strip_of(nbr[t, down])[0:8]
        for t in range(SLOTS):
            v = [work[t * FULL + 6 + 2 * a : t * FULL + 38 + 2 * a, :] for a in range(3)]
            w = [pltpu.roll(x, 64, 1) for x in v]
            at = t * 64
            dest[at : at + 32, 0:128] = jnp.where(low, v[0], w[1]).astype(BF16)
            dest[at : at + 32, 128:256] = jnp.where(low, v[2], zero_rows).astype(BF16)
            dest[at + 32 : at + 64, 0:128] = jnp.where(low, w[0], v[1]).astype(BF16)
            dest[at + 32 : at + 64, 128:256] = jnp.where(low, w[2], zero_rows).astype(BF16)
    add_margins(
        jnp.dot(su_w[...], wback[:, 0:128], preferred_element_type=F32),
        jnp.dot(su_e[...], wback[:, 256:384], preferred_element_type=F32))

    def slopes(t, total):
        for i in range(SIDE):
            r = t * SIDE + i
            back = mid_rows(r) * slope[pl.ds(pl.multiple_of(r * SIDE, 8), SIDE), :]
            back = back.astype(BF16).astype(F32)
            sf[pl.ds(r * ODD_FULL + 8, SIDE), :] = back
            total = total + tile_sum(back)
        return total

    def turn_slopes(t):
        for quarter in range(8):
            g = t * 8 + quarter
            at = pl.ds(pl.multiple_of(g * 128, 128), 128)
            for b, first in enumerate((10, 8, 6)):
                rows = [sf[pl.ds((g * 4 + k) * ODD_FULL + first, SIDE), :] for k in range(4)]
                block = jnp.concatenate(rows, axis=0).astype(BF16)
                sst[b * 128 : b * 128 + 128, at] = block.T

    bias_mid = slopes(0, jnp.zeros((8, 128), F32))
    grad_top(0)

    def slopes_and_turn(t, total):
        turn_slopes(t - 1)
        grad_top(t)
        return slopes(t, total)

    bias_mid = lax.fori_loop(1, SLOTS, slopes_and_turn, bias_mid)
    turn_slopes(SLOTS - 1)
    for t in range(SLOTS):
        for side, col, cell in columns:
            edge = scol_w if side == 0 else scol_e
            at = (t * 2 + col) * 32
            edge[at : at + 32, :] = sf[
                pl.ds(t * SIDE * ODD_FULL + 8 + cell, SIDE, stride=ODD_FULL), :].astype(BF16)

    def in_halves(value):
        rounded = value.astype(BF16).astype(F32)
        return jnp.concatenate([rounded, value - rounded], axis=0)

    def split_again(rows, here):
        split = in_halves(rows[0:16] + rows[16:32])
        chosen = jnp.where(here, 1.0, 0.0).astype(F32)
        return split * chosen + rows * (1.0 - chosen)

    def reducer(chunk, order):
        base = chunk * 1024
        first, second, third = order
        shard = place[first] * 4 + place[second]
        other = on_chip(place, 1 - core)
        pending, started = [], []

        def send(at, src, dst, device):
            copy = pltpu.make_async_remote_copy(
                src_ref=src, dst_ref=dst, send_sem=sum_send.at[chunk, at],
                recv_sem=sum_recv.at[chunk, at], device_id=device, device_id_type=MESH)
            copy.start()
            pending.append(copy)
            started.append(copy)

        def arrive():
            for copy in pending:
                copy.wait_recv()
            pending.clear()

        def rows_at(index, size, offset=0):
            return pl.ds(pl.multiple_of(offset + index * size, 16), size)

        def split_core():
            send(0, grad.at[rows_at(1 - core, 512, base)], core_in.at[chunk], other)

        def split_plane():
            arrive()
            mine = grad[rows_at(core, 512, base), :].astype(F32)
            value = mine + core_in[chunk].astype(F32)
            plane_out[chunk] = value.astype(BF16)
            if chunk == 0:
                plane_out[chunk, 64:96] = split_again(value[64:96], core == 1).astype(BF16)
            for k, (d, e) in enumerate(corners):
                there = moved(((first, d), (second, e)))
                to = there[first] * 4 + there[second]
                send(1 + k, plane_out.at[chunk, rows_at(to, 32)], plane_in.at[chunk, k],
                     on_chip(there, core))

        def swap_line():
            arrive()
            value = plane_out[chunk, rows_at(shard, 32), :].astype(F32)
            for k in range(15):
                value = value + plane_in[chunk, k].astype(F32)
            mine = place[third]
            line_in[chunk, mine] = value
            for d in (1, 2, 3):
                send(15 + d, line_in.at[chunk, mine], line_in.at[chunk, mine],
                     on_chip(moved(((third, d),)), core))

        def back_plane():
            arrive()
            value = line_in[chunk, 0] + line_in[chunk, 1]
            value = value + (line_in[chunk, 2] + line_in[chunk, 3])
            if chunk == 0:
                value = split_again(value, core * 16 + shard == 18)
            mine = rows_at(core * 16 + shard, 32, base)
            total[mine, :] = value.astype(BF16)
            for k, (d, e) in enumerate(corners):
                send(19 + k, total.at[mine], total.at[mine],
                     on_chip(moved(((first, d), (second, e))), core))

        def back_core():
            arrive()
            half = rows_at(core, 512, base)
            send(34, total.at[half], total.at[half], other)

        def finish():
            arrive()
            whole = pltpu.make_async_copy(
                total.at[pl.ds(base, 1024)], sums.at[pl.ds(base, 1024)], local_sem.at[15 + chunk])
            whole.start()
            for copy in started:
                copy.wait_send()
            whole.wait()

        return iter((split_core, split_plane, swap_line, back_plane, back_core, finish))

    reducers = [reducer(chunk, order) for chunk, order in enumerate(orders)]

    def advance(*chunks):
        for chunk in chunks:
            step = next(reducers[chunk], None)
            if step is not None:
                step()

    for a in range(3):
        for b in range(3):
            at = (a * 3 + b) * 64
            block = acc_top[b * 64 : b * 64 + 64, a * 128 : a * 128 + 128]
            grad[at : at + 64, :] = block.astype(BF16)
    grad[576:608, :] = in_halves(jnp.concatenate([bias_mid, bias_top], axis=0)).astype(BF16)
    grad[608:768, :] = jnp.zeros((160, 128), BF16)

    for a in range(3):
        q = slice(a * 256, a * 256 + 256)
        rhs = jnp.concatenate(
            [fp[t, 64 * a : 64 * a + CELLS, :] for t in range(SLOTS)], axis=0)
        acc = jnp.dot(sst[...], rhs, preferred_element_type=F32)
        west = lax.dot_general(scol_w[...], sa_w[:, q], across, preferred_element_type=F32)
        east = lax.dot_general(scol_e[...], sa_e[:, q], across, preferred_element_type=F32)
        for b, block in enumerate((acc[0:128] + west, acc[128:256], acc[256:384] + east)):
            at = 768 + (a * 3 + b) * 256
            grad[at : at + 256, :] = block.astype(BF16).T
        advance(*((0,), (1, 0), (2, 1, 2))[a])
    for _ in range(4):
        advance(0, 1, 2)

    out_copy.wait()


def finish_kernel(
    sums, out_in, gmid, gtop, bmid, btop, out,
    mid_half, mid_full, top_half, top_full, bmid_full, btop_full, out_held, sem,
):
    mids, backs = [], []
    for k in range(3):
        rows = pl.ds(k * 768, 768)
        mids.append(pltpu.make_async_copy(
            sums.at[pl.ds(768 + k * 768, 768)], mid_half.at[rows], sem.at[k]))
        backs.append(pltpu.make_async_copy(mid_full.at[rows], gmid.at[rows], sem.at[3 + k]))
    top = pltpu.make_async_copy(sums.at[pl.ds(0, 608)], top_half, sem.at[6])
    held = pltpu.make_async_copy(out_in, out_held, sem.at[7])
    top_back = pltpu.make_async_copy(top_full, gtop, sem.at[8])
    held_back = pltpu.make_async_copy(out_held, out, sem.at[9])
    bmid_back = pltpu.make_async_copy(bmid_full, bmid, sem.at[10])
    btop_back = pltpu.make_async_copy(btop_full, btop, sem.at[11])
    for copy in (top, *mids, held):
        copy.start()
    top.wait()
    top_full[...] = top_half[0:576, :].astype(F32)
    top_back.start()
    tail = top_half[576:592, :].astype(F32) + top_half[592:608, :].astype(F32)
    bmid_full[...] = jnp.sum(tail[0:8], axis=0, keepdims=True)
    bmid_back.start()
    twice = jnp.sum(tail[8:16], axis=0, keepdims=True)
    btop_full[...] = twice[:, 0:64] + twice[:, 64:128]
    btop_back.start()
    for k in range(3):
        mids[k].wait()
        rows = slice(k * 768, k * 768 + 768)
        mid_full[rows, :] = mid_half[rows, :].astype(F32)
        backs[k].start()
    held.wait()
    held_back.start()
    for copy in (top_back, bmid_back, btop_back, *backs, held_back):
        copy.wait()


def shards(features, cotangent, neighbors, live_count, kernel_mid, bias_mid, kernel_top, bias_top):
    slots, side, _, channels = features.shape
    vmem = pl.BlockSpec(memory_space=pltpu.VMEM)
    smem = pl.BlockSpec(memory_space=pltpu.SMEM)
    hbm = pl.BlockSpec(memory_space=pl.ANY)
    rows = SLOTS * SIDE
    out, sums = pl.pallas_call(
        kernel,
        out_shape=(
            jax.ShapeDtypeStruct((SLOTS, SIDE, 2048), BF16),
            jax.ShapeDtypeStruct((3072, 128), BF16),
        ),
        in_specs=[hbm, hbm, smem, smem, hbm, vmem, vmem, vmem],
        out_specs=(hbm, hbm),
        scratch_shapes=[
            pltpu.VMEM((SLOTS, PADDED, 256), BF16),
            pltpu.VMEM((SLOTS, PADDED, 128), BF16),
            pltpu.VMEM((768, 384), BF16),
            pltpu.VMEM((384, 256), BF16),
            pltpu.VMEM((256, 384), BF16),
            pltpu.VMEM((rows * ODD_WIDE, 128), F32),
            pltpu.VMEM((rows * ODD_SIDE, 128), F32),
            pltpu.VMEM((rows * ODD_WIDE, 128), F32),
            pltpu.VMEM((rows * ODD_FULL, 128), F32),
            pltpu.VMEM((rows * ODD_SIDE, 128), F32),
            pltpu.VMEM((8 * FULL, 128), F32),
            pltpu.VMEM((256, 768), BF16),
            pltpu.VMEM((256, 768), BF16),
            pltpu.VMEM((256, 384), BF16),
            pltpu.VMEM((256, 384), BF16),
            pltpu.VMEM((256, 256), BF16),
            pltpu.VMEM((256, 256), BF16),
            pltpu.VMEM((rows * 9, 128), F32),
            pltpu.VMEM((rows * 9, 128), F32),
            pltpu.VMEM((2, 8, 32, 256), BF16),
            pltpu.VMEM((2, 8, 32, 256), BF16),
            pltpu.VMEM((2, 8, 32, 128), BF16),
            pltpu.VMEM((2, 8, 32, 128), BF16),
            pltpu.VMEM((2, 4, 32, 128), BF16),
            pltpu.VMEM((2, 4, 32, 128), BF16),
            pltpu.VMEM((rows * SIDE, 128), F32),
            pltpu.VMEM((rows * ODD_FULL, 128), F32),
            pltpu.VMEM((SLOTS, PADDED, 128), BF16),
            pltpu.VMEM((SLOTS, PADDED, 128), BF16),
            pltpu.VMEM((192, rows * SIDE), BF16),
            pltpu.VMEM((256, 128), BF16),
            pltpu.VMEM((256, 128), BF16),
            pltpu.VMEM((256, 128), BF16),
            pltpu.VMEM((256, 128), BF16),
            pltpu.VMEM((rows * ODD_FULL, 128), F32),
            pltpu.VMEM((384, rows * SIDE), BF16),
            pltpu.VMEM((192, 384), F32),
            pltpu.VMEM((SLOTS, SIDE, 2048), BF16),
            pltpu.VMEM((SLOTS, SIDE, 2048), BF16),
            pltpu.VMEM((3072, 128), BF16),
            pltpu.VMEM((3, 512, 128), BF16),
            pltpu.VMEM((3, 512, 128), BF16),
            pltpu.VMEM((3, 15, 32, 128), BF16),
            pltpu.VMEM((3, 4, 32, 128), F32),
            pltpu.VMEM((3072, 128), BF16),
            pltpu.SemaphoreType.DMA((18,)),
            pltpu.SemaphoreType.DMA((6,)),
            pltpu.SemaphoreType.DMA((6,)),
            pltpu.SemaphoreType.DMA((3, 35)),
            pltpu.SemaphoreType.DMA((3, 35)),
        ],
        compiler_params=pltpu.CompilerParams(
            collective_id=0, has_side_effects=True, vmem_limit_bytes=60 * 2**20),
        name="backend_layers",
    )(
        features.reshape(slots, side * side, channels), cotangent, neighbors, live_count,
        kernel_mid, bias_mid.reshape(1, 128), jnp.swapaxes(kernel_top, 2, 3),
        bias_top.reshape(1, 64),
    )
    grad_mid, grad_top, bias_mid_sum, bias_top_sum, out = pl.pallas_call(
        finish_kernel,
        out_shape=(
            jax.ShapeDtypeStruct((2304, 128), F32),
            jax.ShapeDtypeStruct((576, 128), F32),
            jax.ShapeDtypeStruct((1, 128), F32),
            jax.ShapeDtypeStruct((1, 64), F32),
            jax.ShapeDtypeStruct((SLOTS, SIDE, 2048), BF16),
        ),
        in_specs=[hbm, hbm],
        out_specs=(hbm,) * 5,
        scratch_shapes=[
            pltpu.VMEM((2304, 128), BF16),
            pltpu.VMEM((2304, 128), F32),
            pltpu.VMEM((608, 128), BF16),
            pltpu.VMEM((576, 128), F32),
            pltpu.VMEM((1, 128), F32),
            pltpu.VMEM((1, 64), F32),
            pltpu.VMEM((SLOTS, SIDE, 2048), BF16),
            pltpu.SemaphoreType.DMA((12,)),
        ],
        compiler_params=pltpu.CompilerParams(vmem_limit_bytes=60 * 2**20),
        name="finish",
    )(sums, out)
    grad_mid = grad_mid.reshape(3, 3, 256, 128)
    grad_top = jnp.swapaxes(grad_top.reshape(3, 3, 64, 128), 2, 3)
    return out, grad_mid, bias_mid_sum.reshape(128), grad_top, bias_top_sum.reshape(64)


def solution(mesh):
    in_specs = (
        P(("rep", "tile"), None, None, None),
        P(("rep", "tile"), None, None),
        P(("rep", "tile"), None),
        P(("rep", "tile")),
        P(),
        P(),
        P(),
        P(),
    )
    out_specs = (P(("rep", "tile"), None, None), P(), P(), P(), P())
    return jax.shard_map(shards, mesh=mesh, in_specs=in_specs, out_specs=out_specs, check_vma=False)
```

```python
import functools

import jax
import jax.numpy as jnp
from jax import lax
from jax.experimental import pallas as pl
from jax.experimental.pallas import tpu as pltpu
from jax.sharding import PartitionSpec as P

F32 = jnp.float32
BF16 = jnp.bfloat16
MESH = pl.DeviceIdType.MESH

SLOTS = 4
SIDE = 32
CELLS = SIDE * SIDE
PADDED = CELLS + 128
FULL = 48
ODD_FULL = 49
ODD_WIDE = 41
ODD_SIDE = 33


def sigmoid(v):
    return 0.5 * jnp.tanh(0.5 * v) + 0.5


def low_lanes(shape):
    return lax.broadcasted_iota(jnp.int32, shape, len(shape) - 1) < 64


def present(index):
    return jnp.where(index >= 0, 1.0, 0.0).astype(F32)


def fill_bands(padded, nbr):
    for t in range(SLOTS):
        north, south = nbr[t, 1], nbr[t, 6]
        band = padded[jnp.maximum(north, 0), CELLS : CELLS + 64, :].astype(F32)
        padded[t, 0:64, :] = (band * present(north)).astype(BF16)
        band = padded[jnp.maximum(south, 0), 64:128, :].astype(F32)
        padded[t, CELLS + 64 : PADDED, :] = (band * present(south)).astype(BF16)


def strip_block(received, index, col, lanes):
    return received[jnp.maximum(index, 0) * 2 + col, :, lanes].astype(F32) * present(index)


def margin_strips(received, nbr, corner_up, side, corner_down, work, shifted, channels):
    for lane_tile in range(channels // 128):
        lanes = slice(lane_tile * 128, lane_tile * 128 + 128)
        for t in range(SLOTS):
            for col in range(2):
                base = (t * 2 + col) * FULL
                up = strip_block(received, nbr[t, corner_up], col, lanes)
                mid = strip_block(received, nbr[t, side], col, lanes)
                down = strip_block(received, nbr[t, corner_down], col, lanes)
                work[base : base + 8, :] = up[24:32]
                work[base + 8 : base + 40, :] = mid
                work[base + 40 : base + 48, :] = down[0:8]
        for block in range(SLOTS * 2):
            for a in range(3):
                rows = work[block * FULL + 6 + 2 * a : block * FULL + 38 + 2 * a, :]
                at = a * channels + lane_tile * 128
                shifted[block * 32 : block * 32 + 32, at : at + 128] = rows.astype(BF16)


def kernel(
    feat, cot, nbr, live, kmid, bmid, ktop, btop,
    out, sums,
    fp, hp, wmid, wtop, wback, y0, y1, y2, ya, yb, work, sa_w, sa_e, sh_w, sh_e, su_w, su_e,
    strip_a, strip_b, fsend, frecv, hsend, hrecv, usend, urecv,
    slope, uf, uplo, uphi, uut, ucol_w, ucol_e, scol_w, scol_e, sf,
    sst, acc_top, cotv, outv, grad, core_in, plane_out, plane_in, line_in, total,
    local_sem, send_sem, recv_sem, sum_send, sum_recv,
):
    n = lax.axis_size("tile")
    me = lax.axis_index("tile")
    right, left = lax.rem(me + 1, n), lax.rem(me + n - 1, n)
    z, y, x, core = lax.axis_index("rep"), me // 8, lax.rem(me // 2, 4), lax.rem(me, 2)
    place = {"x": x, "y": y, "z": z}

    def on_chip(where, c):
        return {"rep": where["z"], "tile": where["y"] * 8 + where["x"] * 2 + c}

    def moved(steps):
        there = dict(place)
        for axis, distance in steps:
            there[axis] = lax.rem(place[axis] + distance, 4)
        return there

    corners = [(d, e) for d in range(4) for e in range(4) if d or e]
    orders = ("xyz", "yzx", "zxy")

    loads = []
    for t in range(SLOTS):
        loads.append(pltpu.make_async_copy(
            feat.at[t], fp.at[t, pl.ds(64, CELLS)], local_sem.at[t]))
    for a in range(3):
        for b in range(3):
            loads.append(pltpu.make_async_copy(
                kmid.at[a, b],
                wmid.at[pl.ds(a * 256, 256), pl.ds(b * 128, 128)],
                local_sem.at[4 + a * 3 + b]))
    loads.append(pltpu.make_async_copy(cot, cotv, local_sem.at[13]))
    for copy in loads:
        copy.start()

    barrier = pltpu.get_barrier_semaphore()
    for neighbour in (left, right):
        pl.semaphore_signal(barrier, inc=1, device_id={"tile": neighbour}, device_id_type=MESH)
    pl.semaphore_signal(barrier, inc=1, device_id=on_chip(place, 1 - core), device_id_type=MESH)
    for first, second, _ in orders:
        for d, e in corners:
            if d:
                pl.semaphore_signal(
                    barrier, inc=1, device_id=on_chip(moved(((first, d), (second, e))), core),
                    device_id_type=MESH)

    for copy in loads[:SLOTS]:
        copy.wait()

    for side, (cells, picks) in enumerate(((0, (0, 1)), (16, (6, 7)))):
        def gather(r, _):
            t, i = r // SIDE, r % SIDE
            rows = fp[t, pl.ds(pl.multiple_of(64 + i * SIDE + cells, 16), 16), :].astype(F32)
            rows = rows[0:8] if cells == 0 else rows[8:16]
            at = r * 9
            strip_a[pl.ds(at, 8), :] = rows[:, 0:128]
            strip_b[pl.ds(at, 8), :] = rows[:, 128:256]
            return 0

        lax.fori_loop(0, SLOTS * SIDE, gather, 0, unroll=16)
        for t in range(SLOTS):
            for col, pick in enumerate(picks):
                at = pl.ds(t * 288 + pick, 32, stride=9)
                fsend[side, t * 2 + col, :, 0:128] = strip_a[at, :].astype(BF16)
                fsend[side, t * 2 + col, :, 128:256] = strip_b[at, :].astype(BF16)

    pl.semaphore_wait(barrier, 39)

    def exchange(send, recv, at):
        copies = []
        for side, target in ((0, left), (1, right)):
            copies.append(pltpu.make_async_remote_copy(
                src_ref=send.at[side], dst_ref=recv.at[1 - side],
                send_sem=send_sem.at[at + side], recv_sem=recv_sem.at[at + 1 - side],
                device_id={"tile": target}, device_id_type=MESH))
        for copy in copies:
            copy.start()
        return copies

    feature_copies = exchange(fsend, frecv, 0)

    zero8 = jnp.zeros((8, 128), F32)

    def clear(r, _):
        uf[pl.ds(r * ODD_FULL, 8), :] = zero8
        uf[pl.ds(r * ODD_FULL + 40, 8), :] = zero8
        sf[pl.ds(r * ODD_FULL, 8), :] = zero8
        sf[pl.ds(r * ODD_FULL + 40, 8), :] = zero8
        return 0

    lax.fori_loop(0, SLOTS * SIDE, clear, 0, unroll=8)

    for a in range(3):
        outer = jnp.concatenate([ktop[a, 0], ktop[a, 2]], axis=0).astype(F32).T
        centre = jnp.concatenate([ktop[a, 1], ktop[a, 1]], axis=0).astype(F32).T
        wtop[a * 128 : a * 128 + 128, 0:128] = outer.astype(BF16)
        wtop[a * 128 : a * 128 + 128, 128:256] = centre.astype(BF16)
        for b in range(3):
            wback[a * 64 : a * 64 + 64, b * 128 : b * 128 + 128] = ktop[2 - a, 2 - b]
    wback[192:256, :] = jnp.zeros((64, 384), BF16)
    btop_twice = jnp.concatenate([btop[...], btop[...]], axis=1)

    fill_bands(fp, nbr)
    for copy in loads[SLOTS:]:
        copy.wait()

    def conv_mid(t, _):
        lhs = jnp.concatenate([fp[t, 64 * a : 64 * a + CELLS, :] for a in range(3)], axis=1)
        y = jnp.dot(lhs, wmid[...], preferred_element_type=F32)
        for i in range(SIDE):
            r = t * SIDE + i
            rows = slice(i * SIDE, i * SIDE + SIDE)
            y0[pl.ds(r * ODD_WIDE + 8, SIDE), :] = y[rows, 0:128]
            y1[pl.ds(r * ODD_SIDE, SIDE), :] = y[rows, 128:256]
            y2[pl.ds(r * ODD_WIDE, SIDE), :] = y[rows, 256:384]
        return 0

    lax.fori_loop(0, SLOTS, conv_mid, 0)

    low = low_lanes((SIDE, 128))
    for copy in feature_copies:
        copy.wait()
    margin_strips(frecv.at[0], nbr, 0, 3, 5, work, sa_w, 256)
    margin_strips(frecv.at[1], nbr, 2, 4, 7, work, sa_e, 256)

    def add_margins(west, east):
        for t in range(SLOTS):
            for col in range(2):
                rows = slice((t * 2 + col) * 32, (t * 2 + col) * 32 + 32)
                y0[pl.ds(t * SIDE * ODD_WIDE + 6 + col, SIDE, stride=ODD_WIDE), :] = west[rows]
                y2[pl.ds(t * SIDE * ODD_WIDE + 32 + col, SIDE, stride=ODD_WIDE), :] = east[rows]

    add_margins(
        jnp.dot(sa_w[...], wmid[:, 0:128], preferred_element_type=F32),
        jnp.dot(sa_e[...], wmid[:, 256:384], preferred_element_type=F32))

    alive = [jnp.where(t < live[0], 1.0, 0.0).astype(F32) for t in range(SLOTS)]
    columns = ((0, 0, 0), (0, 1, 1), (1, 0, 30), (1, 1, 31))

    def mid_at(t, cell):
        first = y0[pl.ds(t * SIDE * ODD_WIDE + 6 + cell, SIDE, stride=ODD_WIDE), :]
        second = y1[pl.ds(t * SIDE * ODD_SIDE + cell, SIDE, stride=ODD_SIDE), :]
        third = y2[pl.ds(t * SIDE * ODD_WIDE + 2 + cell, SIDE, stride=ODD_WIDE), :]
        return first + second + third

    for t in range(SLOTS):
        for side, col, cell in columns:
            pre = mid_at(t, cell) + bmid[...]
            hsend[side, t * 2 + col, :, :] = (pre * sigmoid(pre) * alive[t]).astype(BF16)
    hidden_copies = exchange(hsend, hrecv, 2)

    def mid_rows(r):
        first = y0[pl.ds(r * ODD_WIDE + 6, SIDE), :]
        second = y1[pl.ds(r * ODD_SIDE, SIDE), :]
        third = y2[pl.ds(r * ODD_WIDE + 2, SIDE), :]
        return first + second + third

    def activate(r, _):
        t, i = r // SIDE, r % SIDE
        mask = jnp.where(t < live[0], 1.0, 0.0).astype(F32)
        pre = mid_rows(r) + bmid[...]
        gate = sigmoid(pre)
        hidden = pre * gate
        hp[t, pl.ds(pl.multiple_of(64 + i * SIDE, 16), SIDE), :] = (hidden * mask).astype(BF16)
        slope[pl.ds(pl.multiple_of(r * SIDE, 8), SIDE), :] = (gate + hidden * (1.0 - gate)) * mask
        return 0

    lax.fori_loop(0, SLOTS * SIDE, activate, 0, unroll=8)
    fill_bands(hp, nbr)

    def conv_top(t, _):
        lhs = jnp.concatenate([hp[t, 64 * a : 64 * a + CELLS, :] for a in range(3)], axis=1)
        y = jnp.dot(lhs, wtop[...], preferred_element_type=F32)
        for i in range(SIDE):
            r = t * SIDE + i
            rows = slice(i * SIDE, i * SIDE + SIDE)
            ya[pl.ds(r * ODD_FULL + 8, SIDE), :] = y[rows, 0:128]
            yb[pl.ds(r * ODD_SIDE, SIDE), :] = y[rows, 128:256]
        return 0

    lax.fori_loop(0, SLOTS, conv_top, 0, unroll=2)

    for copy in hidden_copies:
        copy.wait()
    margin_strips(hrecv.at[0], nbr, 0, 3, 5, work, sh_w, 128)
    margin_strips(hrecv.at[1], nbr, 2, 4, 7, work, sh_e, 128)
    west = jnp.dot(sh_w[...], wtop[:, 0:128], preferred_element_type=F32)
    east = jnp.dot(sh_e[...], wtop[:, 0:128], preferred_element_type=F32)
    for t in range(SLOTS):
        for col in range(2):
            rows = slice((t * 2 + col) * 32, (t * 2 + col) * 32 + 32)
            ya[pl.ds(t * SIDE * ODD_FULL + 6 + col, SIDE, stride=ODD_FULL), :] = west[rows]
            ya[pl.ds(t * SIDE * ODD_FULL + 40 + col, SIDE, stride=ODD_FULL), :] = east[rows]

    zero_rows = jnp.zeros((SIDE, 128), F32)

    def up_pair(t, pair, mask):
        cell = 2 * pair
        base = t * SIDE * ODD_FULL
        before = [ya[pl.ds(base + 6 + cell + k, SIDE, stride=ODD_FULL), :] for k in range(2)]
        after = [ya[pl.ds(base + 10 + cell + k, SIDE, stride=ODD_FULL), :] for k in range(2)]
        centre = [yb[pl.ds(t * SIDE * ODD_SIDE + cell + k, SIDE, stride=ODD_SIDE), :] for k in range(2)]
        pre = jnp.where(low, before[0], after[1])
        pre = pre + pltpu.roll(jnp.where(low, before[1], after[0]), 64, 1)
        pre = pre + jnp.where(low, centre[0], centre[1]) + btop_twice
        gate = sigmoid(pre)
        value = pre * gate
        lanes = pl.ds(pair * 128, 128)
        if not isinstance(pair, int):
            lanes = pl.ds(pl.multiple_of(pair * 128, 128), 128)
        outv[t, :, lanes] = (value * mask).astype(BF16)
        up = cotv[t, :, lanes].astype(F32) * (gate + value * (1.0 - gate)) * mask
        up = up.astype(BF16).astype(F32)
        turned = pltpu.roll(up, 64, 1)
        uf[pl.ds(base + 8 + cell, SIDE, stride=ODD_FULL), :] = jnp.where(low, up, turned)
        uf[pl.ds(base + 9 + cell, SIDE, stride=ODD_FULL), :] = jnp.where(low, turned, up)
        return up, turned

    def tile_sum(up):
        return jnp.sum(up.reshape(4, 8, 128), axis=0)

    bias_top = jnp.zeros((8, 128), F32)
    for t in range(SLOTS):
        for side, edge in enumerate((ucol_w, ucol_e)):
            up, turned = up_pair(t, 15 * side, alive[t])
            usend[side, t] = up.astype(BF16)
            for col, rows in enumerate((up, turned)):
                at = (t * 2 + col) * 32
                edge[at : at + 32, :] = jnp.where(low, rows, zero_rows).astype(BF16)
            bias_top = bias_top + tile_sum(up)
    upstream_copies = exchange(usend, urecv, 4)

    def top_pairs(r, total):
        t, pair = r // 14, lax.rem(r, 14) + 1
        mask = jnp.where(t < live[0], 1.0, 0.0).astype(F32)
        up, _ = up_pair(t, pair, mask)
        return total + tile_sum(up)

    bias_top = lax.fori_loop(0, SLOTS * 14, top_pairs, bias_top, unroll=14)
    out_copy = pltpu.make_async_copy(outv, out, local_sem.at[14])
    out_copy.start()

    def shift_up(g, _):
        at = pl.ds(pl.multiple_of(g * 128, 128), 128)
        t, quarter = g // 8, lax.rem(g, 8)

        def cells(first):
            return jnp.concatenate(
                [uf[pl.ds((g * 4 + k) * ODD_FULL + first, SIDE), :] for k in range(4)], axis=0)

        left_half = low_lanes((128, 128))
        zero = jnp.zeros((128, 128), F32)
        same = cells(8)
        rows = pl.ds(pl.multiple_of(64 + quarter * 128, 16), 128)
        uplo[t, rows, :] = jnp.where(left_half, same, zero).astype(BF16)
        uphi[t, rows, :] = jnp.where(left_half, zero, same).astype(BF16)
        uut[0:128, at] = jnp.where(left_half, cells(10), same).astype(BF16).T
        uut[128:192, at] = cells(6).astype(BF16).T[0:64]
        return 0

    lax.fori_loop(0, SLOTS * SIDE // 4, shift_up, 0, unroll=8)
    fill_bands(uplo, nbr)
    fill_bands(uphi, nbr)

    zero_cols = jnp.zeros((256, 128), BF16)
    edges_l = jnp.concatenate([
        jnp.concatenate([ucol_w[...], zero_cols], axis=1),
        jnp.concatenate([zero_cols, ucol_e[...]], axis=1)], axis=0)
    edges_r = jnp.concatenate([sh_w[...], sh_e[...]], axis=0)
    across = (((0,), (0,)), ((), ()))
    edges = lax.dot_general(edges_l, edges_r, across, preferred_element_type=F32)
    acc_top[...] = edges[0:192]

    def grad_top(t):
        rhs = jnp.concatenate([hp[t, 64 * a : 64 * a + CELLS, :] for a in range(3)], axis=1)
        lhs = uut[:, pl.ds(pl.multiple_of(t * CELLS, 128), CELLS)]
        acc_top[...] += jnp.dot(lhs, rhs, preferred_element_type=F32)

    def conv_back(t, _):
        first = uplo[t, 0:CELLS, :] + uphi[t, 64 : 64 + CELLS, :]
        lhs = jnp.concatenate([first, uplo[t, 128 : 128 + CELLS, :]], axis=1)
        y = jnp.dot(lhs, wback[...], preferred_element_type=F32)
        for i in range(SIDE):
            r = t * SIDE + i
            rows = slice(i * SIDE, i * SIDE + SIDE)
            y0[pl.ds(r * ODD_WIDE + 8, SIDE), :] = y[rows, 0:128]
            y1[pl.ds(r * ODD_SIDE, SIDE), :] = y[rows, 128:256]
            y2[pl.ds(r * ODD_WIDE, SIDE), :] = y[rows, 256:384]
        return 0

    lax.fori_loop(0, SLOTS, conv_back, 0, unroll=2)

    for copy in upstream_copies:
        copy.wait()
    for received, up, side, down, dest in (
        (urecv.at[0], 0, 3, 5, su_w), (urecv.at[1], 2, 4, 7, su_e)):
        def strip_of(index):
            return received[jnp.maximum(index, 0)].astype(F32) * present(index)

        for t in range(SLOTS):
            base = t * FULL
            work[base : base + 8, :] = strip_of(nbr[t, up])[24:32]
            work[base + 8 : base + 40, :] = strip_of(nbr[t, side])
            work[base + 40 : base + 48, :] = strip_of(nbr[t, down])[0:8]
        for t in range(SLOTS):
            v = [work[t * FULL + 6 + 2 * a : t * FULL + 38 + 2 * a, :] for a in range(3)]
            w = [pltpu.roll(x, 64, 1) for x in v]
            at = t * 64
            dest[at : at + 32, 0:128] = jnp.where(low, v[0], w[1]).astype(BF16)
            dest[at : at + 32, 128:256] = jnp.where(low, v[2], zero_rows).astype(BF16)
            dest[at + 32 : at + 64, 0:128] = jnp.where(low, w[0], v[1]).astype(BF16)
            dest[at + 32 : at + 64, 128:256] = jnp.where(low, w[2], zero_rows).astype(BF16)
    add_margins(
        jnp.dot(su_w[...], wback[:, 0:128], preferred_element_type=F32),
        jnp.dot(su_e[...], wback[:, 256:384], preferred_element_type=F32))

    def slopes(t, total):
        for i in range(SIDE):
            r = t * SIDE + i
            back = mid_rows(r) * slope[pl.ds(pl.multiple_of(r * SIDE, 8), SIDE), :]
            back = back.astype(BF16).astype(F32)
            sf[pl.ds(r * ODD_FULL + 8, SIDE), :] = back
            total = total + tile_sum(back)
        return total

    def turn_slopes(t):
        for quarter in range(8):
            g = t * 8 + quarter
            at = pl.ds(pl.multiple_of(g * 128, 128), 128)
            for b, first in enumerate((10, 8, 6)):
                rows = [sf[pl.ds((g * 4 + k) * ODD_FULL + first, SIDE), :] for k in range(4)]
                block = jnp.concatenate(rows, axis=0).astype(BF16)
                sst[b * 128 : b * 128 + 128, at] = block.T

    bias_mid = slopes(0, jnp.zeros((8, 128), F32))
    grad_top(0)

    def slopes_and_turn(t, total):
        turn_slopes(t - 1)
        grad_top(t)
        return slopes(t, total)

    bias_mid = lax.fori_loop(1, SLOTS, slopes_and_turn, bias_mid)
    turn_slopes(SLOTS - 1)
    for t in range(SLOTS):
        for side, col, cell in columns:
            edge = scol_w if side == 0 else scol_e
            at = (t * 2 + col) * 32
            edge[at : at + 32, :] = sf[
                pl.ds(t * SIDE * ODD_FULL + 8 + cell, SIDE, stride=ODD_FULL), :].astype(BF16)

    def in_halves(value):
        rounded = value.astype(BF16).astype(F32)
        return jnp.concatenate([rounded, value - rounded], axis=0)

    def split_again(rows, here):
        split = in_halves(rows[0:16] + rows[16:32])
        chosen = jnp.where(here, 1.0, 0.0).astype(F32)
        return split * chosen + rows * (1.0 - chosen)

    def reducer(chunk, order):
        base = chunk * 1024
        first, second, third = order
        shard = place[first] * 4 + place[second]
        other = on_chip(place, 1 - core)
        pending, started = [], []

        def send(at, src, dst, device):
            copy = pltpu.make_async_remote_copy(
                src_ref=src, dst_ref=dst, send_sem=sum_send.at[chunk, at],
                recv_sem=sum_recv.at[chunk, at], device_id=device, device_id_type=MESH)
            copy.start()
            pending.append(copy)
            started.append(copy)

        def arrive():
            for copy in pending:
                copy.wait_recv()
            pending.clear()

        def rows_at(index, size, offset=0):
            return pl.ds(pl.multiple_of(offset + index * size, 16), size)

        def split_core():
            send(0, grad.at[rows_at(1 - core, 512, base)], core_in.at[chunk], other)

        def split_plane():
            arrive()
            mine = grad[rows_at(core, 512, base), :].astype(F32)
            value = mine + core_in[chunk].astype(F32)
            plane_out[chunk] = value.astype(BF16)
            if chunk == 0:
                plane_out[chunk, 64:96] = split_again(value[64:96], core == 1).astype(BF16)
            for k, (d, e) in enumerate(corners):
                there = moved(((first, d), (second, e)))
                to = there[first] * 4 + there[second]
                send(1 + k, plane_out.at[chunk, rows_at(to, 32)], plane_in.at[chunk, k],
                     on_chip(there, core))

        def swap_line():
            arrive()
            value = plane_out[chunk, rows_at(shard, 32), :].astype(F32)
            for k in range(15):
                value = value + plane_in[chunk, k].astype(F32)
            mine = place[third]
            line_in[chunk, mine] = value
            for d in (1, 2, 3):
                send(15 + d, line_in.at[chunk, mine], line_in.at[chunk, mine],
                     on_chip(moved(((third, d),)), core))

        def back_plane():
            arrive()
            value = line_in[chunk, 0] + line_in[chunk, 1]
            value = value + (line_in[chunk, 2] + line_in[chunk, 3])
            if chunk == 0:
                value = split_again(value, core * 16 + shard == 18)
            mine = rows_at(core * 16 + shard, 32, base)
            total[mine, :] = value.astype(BF16)
            for k, (d, e) in enumerate(corners):
                send(19 + k, total.at[mine], total.at[mine],
                     on_chip(moved(((first, d), (second, e))), core))

        def back_core():
            arrive()
            half = rows_at(core, 512, base)
            send(34, total.at[half], total.at[half], other)

        def finish():
            arrive()
            whole = pltpu.make_async_copy(
                total.at[pl.ds(base, 1024)], sums.at[pl.ds(base, 1024)], local_sem.at[15 + chunk])
            whole.start()
            started.append(whole)

        def drain():
            *sent, whole = started
            for copy in sent:
                copy.wait_send()
            whole.wait()

        return iter((split_core, split_plane, swap_line, back_plane, back_core, finish, drain))

    reducers = [reducer(chunk, order) for chunk, order in enumerate(orders)]

    def advance(*chunks):
        for chunk in chunks:
            step = next(reducers[chunk], None)
            if step is not None:
                step()

    for a in range(3):
        for b in range(3):
            at = (a * 3 + b) * 64
            block = acc_top[b * 64 : b * 64 + 64, a * 128 : a * 128 + 128]
            grad[at : at + 64, :] = block.astype(BF16)
    grad[576:608, :] = in_halves(jnp.concatenate([bias_mid, bias_top], axis=0)).astype(BF16)
    grad[608:768, :] = jnp.zeros((160, 128), BF16)

    for a in range(3):
        q = slice(a * 256, a * 256 + 256)
        rhs = jnp.concatenate(
            [fp[t, 64 * a : 64 * a + CELLS, :] for t in range(SLOTS)], axis=0)
        acc = jnp.dot(sst[...], rhs, preferred_element_type=F32)
        west = lax.dot_general(scol_w[...], sa_w[:, q], across, preferred_element_type=F32)
        east = lax.dot_general(scol_e[...], sa_e[:, q], across, preferred_element_type=F32)
        for b, block in enumerate((acc[0:128] + west, acc[128:256], acc[256:384] + east)):
            at = 768 + (a * 3 + b) * 256
            grad[at : at + 256, :] = block.astype(BF16).T
        advance(*((0,), (1, 0), (2, 1, 2))[a])
    for _ in range(5):
        advance(0, 1, 2)

    out_copy.wait()


def finish_kernel(
    sums, out_in, gmid, gtop, bmid, btop, out,
    mid_half, mid_full, top_half, top_full, bmid_full, btop_full, out_held, sem,
):
    mids, backs = [], []
    for k in range(3):
        rows = pl.ds(k * 768, 768)
        mids.append(pltpu.make_async_copy(
            sums.at[pl.ds(768 + k * 768, 768)], mid_half.at[rows], sem.at[k]))
        backs.append(pltpu.make_async_copy(mid_full.at[rows], gmid.at[rows], sem.at[3 + k]))
    top = pltpu.make_async_copy(sums.at[pl.ds(0, 608)], top_half, sem.at[6])
    held = pltpu.make_async_copy(out_in, out_held, sem.at[7])
    top_back = pltpu.make_async_copy(top_full, gtop, sem.at[8])
    held_back = pltpu.make_async_copy(out_held, out, sem.at[9])
    bmid_back = pltpu.make_async_copy(bmid_full, bmid, sem.at[10])
    btop_back = pltpu.make_async_copy(btop_full, btop, sem.at[11])
    for copy in (top, *mids, held):
        copy.start()
    top.wait()
    top_full[...] = top_half[0:576, :].astype(F32)
    top_back.start()
    tail = top_half[576:592, :].astype(F32) + top_half[592:608, :].astype(F32)
    bmid_full[...] = jnp.sum(tail[0:8], axis=0, keepdims=True)
    bmid_back.start()
    twice = jnp.sum(tail[8:16], axis=0, keepdims=True)
    btop_full[...] = twice[:, 0:64] + twice[:, 64:128]
    btop_back.start()
    for k in range(3):
        mids[k].wait()
        rows = slice(k * 768, k * 768 + 768)
        mid_full[rows, :] = mid_half[rows, :].astype(F32)
        backs[k].start()
    held.wait()
    held_back.start()
    for copy in (top_back, bmid_back, btop_back, *backs, held_back):
        copy.wait()


def shards(features, cotangent, neighbors, live_count, kernel_mid, bias_mid, kernel_top, bias_top):
    slots, side, _, channels = features.shape
    vmem = pl.BlockSpec(memory_space=pltpu.VMEM)
    smem = pl.BlockSpec(memory_space=pltpu.SMEM)
    hbm = pl.BlockSpec(memory_space=pl.ANY)
    rows = SLOTS * SIDE
    out, sums = pl.pallas_call(
        kernel,
        out_shape=(
            jax.ShapeDtypeStruct((SLOTS, SIDE, 2048), BF16),
            jax.ShapeDtypeStruct((3072, 128), BF16),
        ),
        in_specs=[hbm, hbm, smem, smem, hbm, vmem, vmem, vmem],
        out_specs=(hbm, hbm),
        scratch_shapes=[
            pltpu.VMEM((SLOTS, PADDED, 256), BF16),
            pltpu.VMEM((SLOTS, PADDED, 128), BF16),
            pltpu.VMEM((768, 384), BF16),
            pltpu.VMEM((384, 256), BF16),
            pltpu.VMEM((256, 384), BF16),
            pltpu.VMEM((rows * ODD_WIDE, 128), F32),
            pltpu.VMEM((rows * ODD_SIDE, 128), F32),
            pltpu.VMEM((rows * ODD_WIDE, 128), F32),
            pltpu.VMEM((rows * ODD_FULL, 128), F32),
            pltpu.VMEM((rows * ODD_SIDE, 128), F32),
            pltpu.VMEM((8 * FULL, 128), F32),
            pltpu.VMEM((256, 768), BF16),
            pltpu.VMEM((256, 768), BF16),
            pltpu.VMEM((256, 384), BF16),
            pltpu.VMEM((256, 384), BF16),
            pltpu.VMEM((256, 256), BF16),
            pltpu.VMEM((256, 256), BF16),
            pltpu.VMEM((rows * 9, 128), F32),
            pltpu.VMEM((rows * 9, 128), F32),
            pltpu.VMEM((2, 8, 32, 256), BF16),
            pltpu.VMEM((2, 8, 32, 256), BF16),
            pltpu.VMEM((2, 8, 32, 128), BF16),
            pltpu.VMEM((2, 8, 32, 128), BF16),
            pltpu.VMEM((2, 4, 32, 128), BF16),
            pltpu.VMEM((2, 4, 32, 128), BF16),
            pltpu.VMEM((rows * SIDE, 128), F32),
            pltpu.VMEM((rows * ODD_FULL, 128), F32),
            pltpu.VMEM((SLOTS, PADDED, 128), BF16),
            pltpu.VMEM((SLOTS, PADDED, 128), BF16),
            pltpu.VMEM((192, rows * SIDE), BF16),
            pltpu.VMEM((256, 128), BF16),
            pltpu.VMEM((256, 128), BF16),
            pltpu.VMEM((256, 128), BF16),
            pltpu.VMEM((256, 128), BF16),
            pltpu.VMEM((rows * ODD_FULL, 128), F32),
            pltpu.VMEM((384, rows * SIDE), BF16),
            pltpu.VMEM((192, 384), F32),
            pltpu.VMEM((SLOTS, SIDE, 2048), BF16),
            pltpu.VMEM((SLOTS, SIDE, 2048), BF16),
            pltpu.VMEM((3072, 128), BF16),
            pltpu.VMEM((3, 512, 128), BF16),
            pltpu.VMEM((3, 512, 128), BF16),
            pltpu.VMEM((3, 15, 32, 128), BF16),
            pltpu.VMEM((3, 4, 32, 128), F32),
            pltpu.VMEM((3072, 128), BF16),
            pltpu.SemaphoreType.DMA((18,)),
            pltpu.SemaphoreType.DMA((6,)),
            pltpu.SemaphoreType.DMA((6,)),
            pltpu.SemaphoreType.DMA((3, 35)),
            pltpu.SemaphoreType.DMA((3, 35)),
        ],
        compiler_params=pltpu.CompilerParams(
            collective_id=0, has_side_effects=True, vmem_limit_bytes=60 * 2**20),
        name="backend_layers",
    )(
        features.reshape(slots, side * side, channels), cotangent, neighbors, live_count,
        kernel_mid, bias_mid.reshape(1, 128), jnp.swapaxes(kernel_top, 2, 3),
        bias_top.reshape(1, 64),
    )
    grad_mid, grad_top, bias_mid_sum, bias_top_sum, out = pl.pallas_call(
        finish_kernel,
        out_shape=(
            jax.ShapeDtypeStruct((2304, 128), F32),
            jax.ShapeDtypeStruct((576, 128), F32),
            jax.ShapeDtypeStruct((1, 128), F32),
            jax.ShapeDtypeStruct((1, 64), F32),
            jax.ShapeDtypeStruct((SLOTS, SIDE, 2048), BF16),
        ),
        in_specs=[hbm, hbm],
        out_specs=(hbm,) * 5,
        scratch_shapes=[
            pltpu.VMEM((2304, 128), BF16),
            pltpu.VMEM((2304, 128), F32),
            pltpu.VMEM((608, 128), BF16),
            pltpu.VMEM((576, 128), F32),
            pltpu.VMEM((1, 128), F32),
            pltpu.VMEM((1, 64), F32),
            pltpu.VMEM((SLOTS, SIDE, 2048), BF16),
            pltpu.SemaphoreType.DMA((12,)),
        ],
        compiler_params=pltpu.CompilerParams(vmem_limit_bytes=60 * 2**20),
        name="finish",
    )(sums, out)
    grad_mid = grad_mid.reshape(3, 3, 256, 128)
    grad_top = jnp.swapaxes(grad_top.reshape(3, 3, 64, 128), 2, 3)
    return out, grad_mid, bias_mid_sum.reshape(128), grad_top, bias_top_sum.reshape(64)


def solution(mesh):
    in_specs = (
        P(("rep", "tile"), None, None, None),
        P(("rep", "tile"), None, None),
        P(("rep", "tile"), None),
        P(("rep", "tile")),
        P(),
        P(),
        P(),
        P(),
    )
    out_specs = (P(("rep", "tile"), None, None), P(), P(), P(), P())
    return jax.shard_map(shards, mesh=mesh, in_specs=in_specs, out_specs=out_specs, check_vma=False)
```

```python
import functools

import jax
import jax.numpy as jnp
from jax import lax
from jax.experimental import pallas as pl
from jax.experimental.pallas import tpu as pltpu
from jax.sharding import PartitionSpec as P

F32 = jnp.float32
BF16 = jnp.bfloat16
MESH = pl.DeviceIdType.MESH

SLOTS = 4
SIDE = 32
CELLS = SIDE * SIDE
PADDED = CELLS + 128
FULL = 48
ODD_FULL = 49
ODD_WIDE = 41
ODD_SIDE = 33


def sigmoid(v):
    return 0.5 * jnp.tanh(0.5 * v) + 0.5


def low_lanes(shape):
    return lax.broadcasted_iota(jnp.int32, shape, len(shape) - 1) < 64


def present(index):
    return jnp.where(index >= 0, 1.0, 0.0).astype(F32)


def fill_bands(padded, nbr):
    for t in range(SLOTS):
        north, south = nbr[t, 1], nbr[t, 6]
        band = padded[jnp.maximum(north, 0), CELLS : CELLS + 64, :].astype(F32)
        padded[t, 0:64, :] = (band * present(north)).astype(BF16)
        band = padded[jnp.maximum(south, 0), 64:128, :].astype(F32)
        padded[t, CELLS + 64 : PADDED, :] = (band * present(south)).astype(BF16)


def strip_block(received, index, col, lanes):
    return received[jnp.maximum(index, 0) * 2 + col, :, lanes].astype(F32) * present(index)


def margin_strips(received, nbr, corner_up, side, corner_down, work, shifted, channels):
    for lane_tile in range(channels // 128):
        lanes = slice(lane_tile * 128, lane_tile * 128 + 128)
        for t in range(SLOTS):
            for col in range(2):
                base = (t * 2 + col) * FULL
                up = strip_block(received, nbr[t, corner_up], col, lanes)
                mid = strip_block(received, nbr[t, side], col, lanes)
                down = strip_block(received, nbr[t, corner_down], col, lanes)
                work[base : base + 8, :] = up[24:32]
                work[base + 8 : base + 40, :] = mid
                work[base + 40 : base + 48, :] = down[0:8]
        for block in range(SLOTS * 2):
            for a in range(3):
                rows = work[block * FULL + 6 + 2 * a : block * FULL + 38 + 2 * a, :]
                at = a * channels + lane_tile * 128
                shifted[block * 32 : block * 32 + 32, at : at + 128] = rows.astype(BF16)


def kernel(
    feat, cot, nbr, live, kmid, bmid, ktop, btop,
    out, sums,
    fp, hp, wmid, wtop, wback, y0, y1, y2, ya, yb, work, sa_w, sa_e, sh_w, sh_e, su_w, su_e,
    strip_a, strip_b, fsend, frecv, hsend, hrecv, usend, urecv,
    slope, uf, uplo, uphi, uut, ucol_w, ucol_e, scol_w, scol_e, sf,
    sst, acc_top, cotv, outv, grad, core_in, plane_out, plane_in, line_in, total,
    local_sem, send_sem, recv_sem, sum_send, sum_recv,
):
    n = lax.axis_size("tile")
    me = lax.axis_index("tile")
    right, left = lax.rem(me + 1, n), lax.rem(me + n - 1, n)
    z, y, x, core = lax.axis_index("rep"), me // 8, lax.rem(me // 2, 4), lax.rem(me, 2)
    place = {"x": x, "y": y, "z": z}

    def on_chip(where, c):
        return {"rep": where["z"], "tile": where["y"] * 8 + where["x"] * 2 + c}

    def moved(steps):
        there = dict(place)
        for axis, distance in steps:
            there[axis] = lax.rem(place[axis] + distance, 4)
        return there

    corners = [(d, e) for d in range(4) for e in range(4) if d or e]
    orders = ("xyz", "yzx", "zxy")

    loads = []
    for t in range(SLOTS):
        loads.append(pltpu.make_async_copy(
            feat.at[t], fp.at[t, pl.ds(64, CELLS)], local_sem.at[t]))
    for a in range(3):
        for b in range(3):
            loads.append(pltpu.make_async_copy(
                kmid.at[a, b],
                wmid.at[pl.ds(a * 256, 256), pl.ds(b * 128, 128)],
                local_sem.at[4 + a * 3 + b]))
    loads.append(pltpu.make_async_copy(cot, cotv, local_sem.at[13]))
    for copy in loads:
        copy.start()

    barrier = pltpu.get_barrier_semaphore()
    for neighbour in (left, right):
        pl.semaphore_signal(barrier, inc=1, device_id={"tile": neighbour}, device_id_type=MESH)
    pl.semaphore_signal(barrier, inc=1, device_id=on_chip(place, 1 - core), device_id_type=MESH)
    for first, second, _ in orders:
        for d, e in corners:
            if d:
                pl.semaphore_signal(
                    barrier, inc=1, device_id=on_chip(moved(((first, d), (second, e))), core),
                    device_id_type=MESH)

    for copy in loads[:SLOTS]:
        copy.wait()

    for side, (cells, picks) in enumerate(((0, (0, 1)), (16, (6, 7)))):
        def gather(r, _):
            t, i = r // SIDE, r % SIDE
            rows = fp[t, pl.ds(pl.multiple_of(64 + i * SIDE + cells, 16), 16), :].astype(F32)
            rows = rows[0:8] if cells == 0 else rows[8:16]
            at = r * 9
            strip_a[pl.ds(at, 8), :] = rows[:, 0:128]
            strip_b[pl.ds(at, 8), :] = rows[:, 128:256]
            return 0

        lax.fori_loop(0, SLOTS * SIDE, gather, 0, unroll=16)
        for t in range(SLOTS):
            for col, pick in enumerate(picks):
                at = pl.ds(t * 288 + pick, 32, stride=9)
                fsend[side, t * 2 + col, :, 0:128] = strip_a[at, :].astype(BF16)
                fsend[side, t * 2 + col, :, 128:256] = strip_b[at, :].astype(BF16)

    pl.semaphore_wait(barrier, 39)

    def exchange(send, recv, at):
        copies = []
        for side, target in ((0, left), (1, right)):
            copies.append(pltpu.make_async_remote_copy(
                src_ref=send.at[side], dst_ref=recv.at[1 - side],
                send_sem=send_sem.at[at + side], recv_sem=recv_sem.at[at + 1 - side],
                device_id={"tile": target}, device_id_type=MESH))
        for copy in copies:
            copy.start()
        return copies

    feature_copies = exchange(fsend, frecv, 0)

    zero8 = jnp.zeros((8, 128), F32)

    def clear(r, _):
        uf[pl.ds(r * ODD_FULL, 8), :] = zero8
        uf[pl.ds(r * ODD_FULL + 40, 8), :] = zero8
        sf[pl.ds(r * ODD_FULL, 8), :] = zero8
        sf[pl.ds(r * ODD_FULL + 40, 8), :] = zero8
        return 0

    lax.fori_loop(0, SLOTS * SIDE, clear, 0, unroll=8)

    for a in range(3):
        outer = jnp.concatenate([ktop[a, 0], ktop[a, 2]], axis=0).astype(F32).T
        centre = jnp.concatenate([ktop[a, 1], ktop[a, 1]], axis=0).astype(F32).T
        wtop[a * 128 : a * 128 + 128, 0:128] = outer.astype(BF16)
        wtop[a * 128 : a * 128 + 128, 128:256] = centre.astype(BF16)
        for b in range(3):
            wback[a * 64 : a * 64 + 64, b * 128 : b * 128 + 128] = ktop[2 - a, 2 - b]
    wback[192:256, :] = jnp.zeros((64, 384), BF16)
    btop_twice = jnp.concatenate([btop[...], btop[...]], axis=1)

    fill_bands(fp, nbr)
    for copy in loads[SLOTS:]:
        copy.wait()

    def conv_mid(t, _):
        lhs = jnp.concatenate([fp[t, 64 * a : 64 * a + CELLS, :] for a in range(3)], axis=1)
        y = jnp.dot(lhs, wmid[...], preferred_element_type=F32)
        for i in range(SIDE):
            r = t * SIDE + i
            rows = slice(i * SIDE, i * SIDE + SIDE)
            y0[pl.ds(r * ODD_WIDE + 8, SIDE), :] = y[rows, 0:128]
            y1[pl.ds(r * ODD_SIDE, SIDE), :] = y[rows, 128:256]
            y2[pl.ds(r * ODD_WIDE, SIDE), :] = y[rows, 256:384]
        return 0

    lax.fori_loop(0, SLOTS, conv_mid, 0)

    low = low_lanes((SIDE, 128))
    for copy in feature_copies:
        copy.wait()
    margin_strips(frecv.at[0], nbr, 0, 3, 5, work, sa_w, 256)
    margin_strips(frecv.at[1], nbr, 2, 4, 7, work, sa_e, 256)

    def add_margins(west, east):
        for t in range(SLOTS):
            for col in range(2):
                rows = slice((t * 2 + col) * 32, (t * 2 + col) * 32 + 32)
                y0[pl.ds(t * SIDE * ODD_WIDE + 6 + col, SIDE, stride=ODD_WIDE), :] = west[rows]
                y2[pl.ds(t * SIDE * ODD_WIDE + 32 + col, SIDE, stride=ODD_WIDE), :] = east[rows]

    add_margins(
        jnp.dot(sa_w[...], wmid[:, 0:128], preferred_element_type=F32),
        jnp.dot(sa_e[...], wmid[:, 256:384], preferred_element_type=F32))

    alive = [jnp.where(t < live[0], 1.0, 0.0).astype(F32) for t in range(SLOTS)]
    columns = ((0, 0, 0), (0, 1, 1), (1, 0, 30), (1, 1, 31))

    def mid_at(t, cell):
        first = y0[pl.ds(t * SIDE * ODD_WIDE + 6 + cell, SIDE, stride=ODD_WIDE), :]
        second = y1[pl.ds(t * SIDE * ODD_SIDE + cell, SIDE, stride=ODD_SIDE), :]
        third = y2[pl.ds(t * SIDE * ODD_WIDE + 2 + cell, SIDE, stride=ODD_WIDE), :]
        return first + second + third

    for t in range(SLOTS):
        for side, col, cell in columns:
            pre = mid_at(t, cell) + bmid[...]
            hsend[side, t * 2 + col, :, :] = (pre * sigmoid(pre) * alive[t]).astype(BF16)
    hidden_copies = exchange(hsend, hrecv, 2)

    def mid_rows(r):
        first = y0[pl.ds(r * ODD_WIDE + 6, SIDE), :]
        second = y1[pl.ds(r * ODD_SIDE, SIDE), :]
        third = y2[pl.ds(r * ODD_WIDE + 2, SIDE), :]
        return first + second + third

    def activate(r, _):
        t, i = r // SIDE, r % SIDE
        mask = jnp.where(t < live[0], 1.0, 0.0).astype(F32)
        pre = mid_rows(r) + bmid[...]
        gate = sigmoid(pre)
        hidden = pre * gate
        hp[t, pl.ds(pl.multiple_of(64 + i * SIDE, 16), SIDE), :] = (hidden * mask).astype(BF16)
        slope[pl.ds(pl.multiple_of(r * SIDE, 8), SIDE), :] = (gate + hidden * (1.0 - gate)) * mask
        return 0

    lax.fori_loop(0, SLOTS * SIDE, activate, 0, unroll=8)
    fill_bands(hp, nbr)

    def conv_top(t, _):
        lhs = jnp.concatenate([hp[t, 64 * a : 64 * a + CELLS, :] for a in range(3)], axis=1)
        y = jnp.dot(lhs, wtop[...], preferred_element_type=F32)
        for i in range(SIDE):
            r = t * SIDE + i
            rows = slice(i * SIDE, i * SIDE + SIDE)
            ya[pl.ds(r * ODD_FULL + 8, SIDE), :] = y[rows, 0:128]
            yb[pl.ds(r * ODD_SIDE, SIDE), :] = y[rows, 128:256]
        return 0

    lax.fori_loop(0, SLOTS, conv_top, 0, unroll=2)

    for copy in hidden_copies:
        copy.wait()
    margin_strips(hrecv.at[0], nbr, 0, 3, 5, work, sh_w, 128)
    margin_strips(hrecv.at[1], nbr, 2, 4, 7, work, sh_e, 128)
    west = jnp.dot(sh_w[...], wtop[:, 0:128], preferred_element_type=F32)
    east = jnp.dot(sh_e[...], wtop[:, 0:128], preferred_element_type=F32)
    for t in range(SLOTS):
        for col in range(2):
            rows = slice((t * 2 + col) * 32, (t * 2 + col) * 32 + 32)
            ya[pl.ds(t * SIDE * ODD_FULL + 6 + col, SIDE, stride=ODD_FULL), :] = west[rows]
            ya[pl.ds(t * SIDE * ODD_FULL + 40 + col, SIDE, stride=ODD_FULL), :] = east[rows]

    zero_rows = jnp.zeros((SIDE, 128), F32)

    def up_pair(t, pair, mask):
        cell = 2 * pair
        base = t * SIDE * ODD_FULL
        before = [ya[pl.ds(base + 6 + cell + k, SIDE, stride=ODD_FULL), :] for k in range(2)]
        after = [ya[pl.ds(base + 10 + cell + k, SIDE, stride=ODD_FULL), :] for k in range(2)]
        centre = [yb[pl.ds(t * SIDE * ODD_SIDE + cell + k, SIDE, stride=ODD_SIDE), :] for k in range(2)]
        pre = jnp.where(low, before[0], after[1])
        pre = pre + pltpu.roll(jnp.where(low, before[1], after[0]), 64, 1)
        pre = pre + jnp.where(low, centre[0], centre[1]) + btop_twice
        gate = sigmoid(pre)
        value = pre * gate
        lanes = pl.ds(pair * 128, 128)
        if not isinstance(pair, int):
            lanes = pl.ds(pl.multiple_of(pair * 128, 128), 128)
        outv[t, :, lanes] = (value * mask).astype(BF16)
        up = cotv[t, :, lanes].astype(F32) * (gate + value * (1.0 - gate)) * mask
        up = up.astype(BF16).astype(F32)
        turned = pltpu.roll(up, 64, 1)
        uf[pl.ds(base + 8 + cell, SIDE, stride=ODD_FULL), :] = jnp.where(low, up, turned)
        uf[pl.ds(base + 9 + cell, SIDE, stride=ODD_FULL), :] = jnp.where(low, turned, up)
        return up, turned

    def tile_sum(up):
        return jnp.sum(up.reshape(4, 8, 128), axis=0)

    bias_top = jnp.zeros((8, 128), F32)
    for t in range(SLOTS):
        for side, edge in enumerate((ucol_w, ucol_e)):
            up, turned = up_pair(t, 15 * side, alive[t])
            usend[side, t] = up.astype(BF16)
            for col, rows in enumerate((up, turned)):
                at = (t * 2 + col) * 32
                edge[at : at + 32, :] = jnp.where(low, rows, zero_rows).astype(BF16)
            bias_top = bias_top + tile_sum(up)
    upstream_copies = exchange(usend, urecv, 4)

    def top_pairs(r, total):
        t, pair = r // 14, lax.rem(r, 14) + 1
        mask = jnp.where(t < live[0], 1.0, 0.0).astype(F32)
        up, _ = up_pair(t, pair, mask)
        return total + tile_sum(up)

    bias_top = lax.fori_loop(0, SLOTS * 14, top_pairs, bias_top, unroll=14)
    out_copy = pltpu.make_async_copy(outv, out, local_sem.at[14])
    out_copy.start()

    def shift_up(g, _):
        at = pl.ds(pl.multiple_of(g * 128, 128), 128)
        t, quarter = g // 8, lax.rem(g, 8)

        def cells(first):
            return jnp.concatenate(
                [uf[pl.ds((g * 4 + k) * ODD_FULL + first, SIDE), :] for k in range(4)], axis=0)

        left_half = low_lanes((128, 128))
        zero = jnp.zeros((128, 128), F32)
        same = cells(8)
        rows = pl.ds(pl.multiple_of(64 + quarter * 128, 16), 128)
        uplo[t, rows, :] = jnp.where(left_half, same, zero).astype(BF16)
        uphi[t, rows, :] = jnp.where(left_half, zero, same).astype(BF16)
        uut[0:128, at] = jnp.where(left_half, cells(10), same).astype(BF16).T
        uut[128:192, at] = cells(6).astype(BF16).T[0:64]
        return 0

    lax.fori_loop(0, SLOTS * SIDE // 4, shift_up, 0, unroll=8)
    fill_bands(uplo, nbr)
    fill_bands(uphi, nbr)

    zero_cols = jnp.zeros((256, 128), BF16)
    edges_l = jnp.concatenate([
        jnp.concatenate([ucol_w[...], zero_cols], axis=1),
        jnp.concatenate([zero_cols, ucol_e[...]], axis=1)], axis=0)
    edges_r = jnp.concatenate([sh_w[...], sh_e[...]], axis=0)
    across = (((0,), (0,)), ((), ()))
    edges = lax.dot_general(edges_l, edges_r, across, preferred_element_type=F32)
    acc_top[...] = edges[0:192]

    def grad_top(t):
        rhs = jnp.concatenate([hp[t, 64 * a : 64 * a + CELLS, :] for a in range(3)], axis=1)
        lhs = uut[:, pl.ds(pl.multiple_of(t * CELLS, 128), CELLS)]
        acc_top[...] += jnp.dot(lhs, rhs, preferred_element_type=F32)

    def conv_back(t, _):
        first = uplo[t, 0:CELLS, :] + uphi[t, 64 : 64 + CELLS, :]
        lhs = jnp.concatenate([first, uplo[t, 128 : 128 + CELLS, :]], axis=1)
        y = jnp.dot(lhs, wback[...], preferred_element_type=F32)
        for i in range(SIDE):
            r = t * SIDE + i
            rows = slice(i * SIDE, i * SIDE + SIDE)
            y0[pl.ds(r * ODD_WIDE + 8, SIDE), :] = y[rows, 0:128]
            y1[pl.ds(r * ODD_SIDE, SIDE), :] = y[rows, 128:256]
            y2[pl.ds(r * ODD_WIDE, SIDE), :] = y[rows, 256:384]
        return 0

    lax.fori_loop(0, SLOTS, conv_back, 0, unroll=2)

    for copy in upstream_copies:
        copy.wait()
    for received, up, side, down, dest in (
        (urecv.at[0], 0, 3, 5, su_w), (urecv.at[1], 2, 4, 7, su_e)):
        def strip_of(index):
            return received[jnp.maximum(index, 0)].astype(F32) * present(index)

        for t in range(SLOTS):
            base = t * FULL
            work[base : base + 8, :] = strip_of(nbr[t, up])[24:32]
            work[base + 8 : base + 40, :] = strip_of(nbr[t, side])
            work[base + 40 : base + 48, :] = strip_of(nbr[t, down])[0:8]
        for t in range(SLOTS):
            v = [work[t * FULL + 6 + 2 * a : t * FULL + 38 + 2 * a, :] for a in range(3)]
            w = [pltpu.roll(x, 64, 1) for x in v]
            at = t * 64
            dest[at : at + 32, 0:128] = jnp.where(low, v[0], w[1]).astype(BF16)
            dest[at : at + 32, 128:256] = jnp.where(low, v[2], zero_rows).astype(BF16)
            dest[at + 32 : at + 64, 0:128] = jnp.where(low, w[0], v[1]).astype(BF16)
            dest[at + 32 : at + 64, 128:256] = jnp.where(low, w[2], zero_rows).astype(BF16)
    add_margins(
        jnp.dot(su_w[...], wback[:, 0:128], preferred_element_type=F32),
        jnp.dot(su_e[...], wback[:, 256:384], preferred_element_type=F32))

    def slopes(t, total):
        for i in range(SIDE):
            r = t * SIDE + i
            back = mid_rows(r) * slope[pl.ds(pl.multiple_of(r * SIDE, 8), SIDE), :]
            back = back.astype(BF16).astype(F32)
            sf[pl.ds(r * ODD_FULL + 8, SIDE), :] = back
            total = total + tile_sum(back)
        return total

    def turn_slopes(t):
        for quarter in range(8):
            g = t * 8 + quarter
            at = pl.ds(pl.multiple_of(g * 128, 128), 128)
            for b, first in enumerate((10, 8, 6)):
                rows = [sf[pl.ds((g * 4 + k) * ODD_FULL + first, SIDE), :] for k in range(4)]
                block = jnp.concatenate(rows, axis=0).astype(BF16)
                sst[b * 128 : b * 128 + 128, at] = block.T

    bias_mid = slopes(0, jnp.zeros((8, 128), F32))
    grad_top(0)

    def slopes_and_turn(t, total):
        turn_slopes(t - 1)
        grad_top(t)
        return slopes(t, total)

    bias_mid = lax.fori_loop(1, SLOTS, slopes_and_turn, bias_mid)
    turn_slopes(SLOTS - 1)
    for t in range(SLOTS):
        for side, col, cell in columns:
            edge = scol_w if side == 0 else scol_e
            at = (t * 2 + col) * 32
            edge[at : at + 32, :] = sf[
                pl.ds(t * SIDE * ODD_FULL + 8 + cell, SIDE, stride=ODD_FULL), :].astype(BF16)

    def in_halves(value):
        rounded = value.astype(BF16).astype(F32)
        return jnp.concatenate([rounded, value - rounded], axis=0)

    def split_again(rows, here):
        split = in_halves(rows[0:16] + rows[16:32])
        chosen = jnp.where(here, 1.0, 0.0).astype(F32)
        return split * chosen + rows * (1.0 - chosen)

    def reducer(chunk, order):
        base = chunk * 1024
        first, second, third = order
        shard = place[first] * 4 + place[second]
        other = on_chip(place, 1 - core)
        pending, started = [], []

        def send(at, src, dst, device):
            copy = pltpu.make_async_remote_copy(
                src_ref=src, dst_ref=dst, send_sem=sum_send.at[chunk, at],
                recv_sem=sum_recv.at[chunk, at], device_id=device, device_id_type=MESH)
            copy.start()
            pending.append(copy)
            started.append(copy)

        def arrive():
            for copy in pending:
                copy.wait_recv()
            pending.clear()

        def rows_at(index, size, offset=0):
            return pl.ds(pl.multiple_of(offset + index * size, 16), size)

        def split_core():
            send(0, grad.at[rows_at(1 - core, 512, base)], core_in.at[chunk], other)

        def split_plane():
            arrive()
            mine = grad[rows_at(core, 512, base), :].astype(F32)
            value = mine + core_in[chunk].astype(F32)
            plane_out[chunk] = value.astype(BF16)
            if chunk == 0:
                plane_out[chunk, 64:96] = split_again(value[64:96], core == 1).astype(BF16)
            for k, (d, e) in enumerate(corners):
                there = moved(((first, d), (second, e)))
                to = there[first] * 4 + there[second]
                send(1 + k, plane_out.at[chunk, rows_at(to, 32)], plane_in.at[chunk, k],
                     on_chip(there, core))

        def swap_line():
            arrive()
            value = plane_out[chunk, rows_at(shard, 32), :].astype(F32)
            for k in range(15):
                value = value + plane_in[chunk, k].astype(F32)
            mine = place[third]
            line_in[chunk, mine] = value
            for d in (1, 2, 3):
                send(15 + d, line_in.at[chunk, mine], line_in.at[chunk, mine],
                     on_chip(moved(((third, d),)), core))

        def back_plane():
            arrive()
            value = line_in[chunk, 0] + line_in[chunk, 1]
            value = value + (line_in[chunk, 2] + line_in[chunk, 3])
            if chunk == 0:
                value = split_again(value, core * 16 + shard == 18)
            mine = rows_at(core * 16 + shard, 32, base)
            total[mine, :] = value.astype(BF16)
            for k, (d, e) in enumerate(corners):
                send(19 + k, total.at[mine], total.at[mine],
                     on_chip(moved(((first, d), (second, e))), core))

        def back_core():
            arrive()
            half = rows_at(core, 512, base)
            send(34, total.at[half], total.at[half], other)

        def finish():
            arrive()
            whole = pltpu.make_async_copy(
                total.at[pl.ds(base, 1024)], sums.at[pl.ds(base, 1024)], local_sem.at[15 + chunk])
            whole.start()
            started.append(whole)

        def drain():
            *sent, whole = started
            for copy in sent:
                copy.wait_send()
            whole.wait()

        return iter((split_core, split_plane, swap_line, back_plane, back_core, finish, drain))

    reducers = [reducer(chunk, order) for chunk, order in enumerate(orders)]

    def advance(*chunks):
        for chunk in chunks:
            step = next(reducers[chunk], None)
            if step is not None:
                step()

    for a in range(3):
        for b in range(3):
            at = (a * 3 + b) * 64
            block = acc_top[b * 64 : b * 64 + 64, a * 128 : a * 128 + 128]
            grad[at : at + 64, :] = block.astype(BF16)
    grad[576:608, :] = in_halves(jnp.concatenate([bias_mid, bias_top], axis=0)).astype(BF16)
    grad[608:768, :] = jnp.zeros((160, 128), BF16)

    for a in range(3):
        q = slice(a * 256, a * 256 + 256)
        rhs = jnp.concatenate(
            [fp[t, 64 * a : 64 * a + CELLS, :] for t in range(SLOTS)], axis=0)
        acc = jnp.dot(sst[...], rhs, preferred_element_type=F32)
        west = lax.dot_general(scol_w[...], sa_w[:, q], across, preferred_element_type=F32)
        east = lax.dot_general(scol_e[...], sa_e[:, q], across, preferred_element_type=F32)
        if a:
            advance(a - 1)
        for b, block in enumerate((acc[0:128] + west, acc[128:256], acc[256:384] + east)):
            at = 768 + (a * 3 + b) * 256
            grad[at : at + 256, :] = block.astype(BF16).T
        advance(a)
    advance(2)
    for _ in range(5):
        advance(0, 1, 2)

    out_copy.wait()


def finish_kernel(
    sums, out_in, gmid, gtop, bmid, btop, out,
    mid_half, mid_full, top_half, top_full, bmid_full, btop_full, out_held, sem,
):
    mids, backs = [], []
    for k in range(3):
        rows = pl.ds(k * 768, 768)
        mids.append(pltpu.make_async_copy(
            sums.at[pl.ds(768 + k * 768, 768)], mid_half.at[rows], sem.at[k]))
        backs.append(pltpu.make_async_copy(mid_full.at[rows], gmid.at[rows], sem.at[3 + k]))
    top = pltpu.make_async_copy(sums.at[pl.ds(0, 608)], top_half, sem.at[6])
    held = pltpu.make_async_copy(out_in, out_held, sem.at[7])
    top_back = pltpu.make_async_copy(top_full, gtop, sem.at[8])
    held_back = pltpu.make_async_copy(out_held, out, sem.at[9])
    bmid_back = pltpu.make_async_copy(bmid_full, bmid, sem.at[10])
    btop_back = pltpu.make_async_copy(btop_full, btop, sem.at[11])
    for copy in (top, *mids, held):
        copy.start()
    top.wait()
    top_full[...] = top_half[0:576, :].astype(F32)
    top_back.start()
    tail = top_half[576:592, :].astype(F32) + top_half[592:608, :].astype(F32)
    bmid_full[...] = jnp.sum(tail[0:8], axis=0, keepdims=True)
    bmid_back.start()
    twice = jnp.sum(tail[8:16], axis=0, keepdims=True)
    btop_full[...] = twice[:, 0:64] + twice[:, 64:128]
    btop_back.start()
    for k in range(3):
        mids[k].wait()
        rows = slice(k * 768, k * 768 + 768)
        mid_full[rows, :] = mid_half[rows, :].astype(F32)
        backs[k].start()
    held.wait()
    held_back.start()
    for copy in (top_back, bmid_back, btop_back, *backs, held_back):
        copy.wait()


def shards(features, cotangent, neighbors, live_count, kernel_mid, bias_mid, kernel_top, bias_top):
    slots, side, _, channels = features.shape
    vmem = pl.BlockSpec(memory_space=pltpu.VMEM)
    smem = pl.BlockSpec(memory_space=pltpu.SMEM)
    hbm = pl.BlockSpec(memory_space=pl.ANY)
    rows = SLOTS * SIDE
    out, sums = pl.pallas_call(
        kernel,
        out_shape=(
            jax.ShapeDtypeStruct((SLOTS, SIDE, 2048), BF16),
            jax.ShapeDtypeStruct((3072, 128), BF16),
        ),
        in_specs=[hbm, hbm, smem, smem, hbm, vmem, vmem, vmem],
        out_specs=(hbm, hbm),
        scratch_shapes=[
            pltpu.VMEM((SLOTS, PADDED, 256), BF16),
            pltpu.VMEM((SLOTS, PADDED, 128), BF16),
            pltpu.VMEM((768, 384), BF16),
            pltpu.VMEM((384, 256), BF16),
            pltpu.VMEM((256, 384), BF16),
            pltpu.VMEM((rows * ODD_WIDE, 128), F32),
            pltpu.VMEM((rows * ODD_SIDE, 128), F32),
            pltpu.VMEM((rows * ODD_WIDE, 128), F32),
            pltpu.VMEM((rows * ODD_FULL, 128), F32),
            pltpu.VMEM((rows * ODD_SIDE, 128), F32),
            pltpu.VMEM((8 * FULL, 128), F32),
            pltpu.VMEM((256, 768), BF16),
            pltpu.VMEM((256, 768), BF16),
            pltpu.VMEM((256, 384), BF16),
            pltpu.VMEM((256, 384), BF16),
            pltpu.VMEM((256, 256), BF16),
            pltpu.VMEM((256, 256), BF16),
            pltpu.VMEM((rows * 9, 128), F32),
            pltpu.VMEM((rows * 9, 128), F32),
            pltpu.VMEM((2, 8, 32, 256), BF16),
            pltpu.VMEM((2, 8, 32, 256), BF16),
            pltpu.VMEM((2, 8, 32, 128), BF16),
            pltpu.VMEM((2, 8, 32, 128), BF16),
            pltpu.VMEM((2, 4, 32, 128), BF16),
            pltpu.VMEM((2, 4, 32, 128), BF16),
            pltpu.VMEM((rows * SIDE, 128), F32),
            pltpu.VMEM((rows * ODD_FULL, 128), F32),
            pltpu.VMEM((SLOTS, PADDED, 128), BF16),
            pltpu.VMEM((SLOTS, PADDED, 128), BF16),
            pltpu.VMEM((192, rows * SIDE), BF16),
            pltpu.VMEM((256, 128), BF16),
            pltpu.VMEM((256, 128), BF16),
            pltpu.VMEM((256, 128), BF16),
            pltpu.VMEM((256, 128), BF16),
            pltpu.VMEM((rows * ODD_FULL, 128), F32),
            pltpu.VMEM((384, rows * SIDE), BF16),
            pltpu.VMEM((192, 384), F32),
            pltpu.VMEM((SLOTS, SIDE, 2048), BF16),
            pltpu.VMEM((SLOTS, SIDE, 2048), BF16),
            pltpu.VMEM((3072, 128), BF16),
            pltpu.VMEM((3, 512, 128), BF16),
            pltpu.VMEM((3, 512, 128), BF16),
            pltpu.VMEM((3, 15, 32, 128), BF16),
            pltpu.VMEM((3, 4, 32, 128), F32),
            pltpu.VMEM((3072, 128), BF16),
            pltpu.SemaphoreType.DMA((18,)),
            pltpu.SemaphoreType.DMA((6,)),
            pltpu.SemaphoreType.DMA((6,)),
            pltpu.SemaphoreType.DMA((3, 35)),
            pltpu.SemaphoreType.DMA((3, 35)),
        ],
        compiler_params=pltpu.CompilerParams(
            collective_id=0, has_side_effects=True, vmem_limit_bytes=60 * 2**20),
        name="backend_layers",
    )(
        features.reshape(slots, side * side, channels), cotangent, neighbors, live_count,
        kernel_mid, bias_mid.reshape(1, 128), jnp.swapaxes(kernel_top, 2, 3),
        bias_top.reshape(1, 64),
    )
    grad_mid, grad_top, bias_mid_sum, bias_top_sum, out = pl.pallas_call(
        finish_kernel,
        out_shape=(
            jax.ShapeDtypeStruct((2304, 128), F32),
            jax.ShapeDtypeStruct((576, 128), F32),
            jax.ShapeDtypeStruct((1, 128), F32),
            jax.ShapeDtypeStruct((1, 64), F32),
            jax.ShapeDtypeStruct((SLOTS, SIDE, 2048), BF16),
        ),
        in_specs=[hbm, hbm],
        out_specs=(hbm,) * 5,
        scratch_shapes=[
            pltpu.VMEM((2304, 128), BF16),
            pltpu.VMEM((2304, 128), F32),
            pltpu.VMEM((608, 128), BF16),
            pltpu.VMEM((576, 128), F32),
            pltpu.VMEM((1, 128), F32),
            pltpu.VMEM((1, 64), F32),
            pltpu.VMEM((SLOTS, SIDE, 2048), BF16),
            pltpu.SemaphoreType.DMA((12,)),
        ],
        compiler_params=pltpu.CompilerParams(vmem_limit_bytes=60 * 2**20),
        name="finish",
    )(sums, out)
    grad_mid = grad_mid.reshape(3, 3, 256, 128)
    grad_top = jnp.swapaxes(grad_top.reshape(3, 3, 64, 128), 2, 3)
    return out, grad_mid, bias_mid_sum.reshape(128), grad_top, bias_top_sum.reshape(64)


def solution(mesh):
    in_specs = (
        P(("rep", "tile"), None, None, None),
        P(("rep", "tile"), None, None),
        P(("rep", "tile"), None),
        P(("rep", "tile")),
        P(),
        P(),
        P(),
        P(),
    )
    out_specs = (P(("rep", "tile"), None, None), P(), P(), P(), P())
    return jax.shard_map(shards, mesh=mesh, in_specs=in_specs, out_specs=out_specs, check_vma=False)
```
